32 devices in a mesh: seq: 16 (over z, y, core), tp: 2 (over x).
Axes of the slice: x: 2, y: 2, z: 4, core: 2. Of those that a mesh axis runs over, the one named last changes fastest.
Arguments:
- q_proj: bfloat16 [2048, 8192], P('seq', 'tp'), may hold values from -6 to 6
- k_proj: bfloat16 [2048, 8192], P('seq', 'tp'), may hold values from -6 to 6
- v_proj: bfloat16 [2048, 8192], P('seq', 'tp'), may hold values from -6 to 6
- grad_out: bfloat16 [2048, 8192], P('seq', 'tp'), may hold values from -6 to 6
- w_first: float32 [32, 64], replicated, may hold values from -2 to 2
- w_second: float32 [64, 8192], P(None, 'tp'), may hold values from -0.75 to 0.75
- decay_rate: float32 [8192], P('tp'), may hold values from 0.02 to 64
- skip_gain: float32 [8192], P('tp'), may hold values from 0.5 to 1.5
Outputs:
- grad_q: bfloat16 [2048, 8192], P('seq', 'tp')
- grad_k: bfloat16 [2048, 8192], P('seq', 'tp')
- grad_v: bfloat16 [2048, 8192], P('seq', 'tp')
- grad_first: float32 [32, 64], replicated
- grad_second: float32 [64, 8192], P(None, 'tp')
- grad_decay: float32 [8192], P('tp')
- grad_skip: float32 [8192], P('tp')
The draws below stay inside these ranges and needn't reach their ends.
All inputs are finite; a program needn't handle non-finite values.
Results may differ from the reference program's by a relative error of at most 0.0058.
Values may be sent and summed in bfloat16 or wider, within the bound.
No kernel may reach another device: no remote copies, remote signals or barrier semaphores. Data moves between devices by JAX's collectives and lax.ppermute only.
A program may use at most 128 MiB of HBM per device.

```python
import math
import jax
import jax.numpy as jnp
from jax import lax

D = 8192
F = 64
E = 32
SEQ = 2048


def block_levels(own_key, shape, split, smallest, largest):
    def one(axis_at, parts):
        heights = jax.random.uniform(jax.random.fold_in(jax.random.fold_in(own_key, 6), axis_at), (parts,), jnp.float32, smallest / len(split), largest / len(split))
        return jnp.repeat(jnp.exp(heights), shape[axis_at] // parts).reshape((-1,) + (1,) * (len(shape) - axis_at - 1))

    level = one(*split[0])
    for cut in split[1:]:
        level = level * one(*cut)
    return level


def noise(rng, dims, scale, most, pieces=(), held_as=jnp.bfloat16):
    level = block_levels(rng, dims, pieces, -0.22, 0.18) if pieces else 1.0
    values = jax.random.normal(rng, dims, jnp.float32) * scale * level
    return jnp.minimum(jnp.maximum(values, -most), most).astype(held_as)


def setup_inputs(seed: int = 0) -> dict:
    streams_of = jax.random.split(jax.random.key(seed), 9)
    q_proj = noise(streams_of[0], (SEQ, D), 1.0, 6.0, ((0, 16), (1, 2)))
    k_proj = noise(streams_of[1], (SEQ, D), 1.0, 6.0, ((0, 16), (1, 2)))
    v_proj = noise(streams_of[2], (SEQ, D), 1.0, 6.0, ((0, 16), (1, 2)))
    grad_out = noise(streams_of[3], (SEQ, D), 1.0, 6.0, ((0, 16), (1, 2)))
    w_first = noise(streams_of[4], (E, F), (E // 4) ** -0.5, 2.0, (), jnp.float32)
    w_second = noise(streams_of[5], (F, D), F ** -0.5, 0.75, ((1, 2),), jnp.float32)
    decay_rate = jnp.clip(jnp.exp(math.log(64.0) - 8.070906 * jax.random.uniform(streams_of[6], (D,), jnp.float32) ** block_levels(streams_of[6], (D,), ((0, 2),), -0.2, 0.2)), 0.02, 64.0)
    skip_gain = jnp.clip(0.5 + 1.0 * jax.random.uniform(streams_of[7], (D,), jnp.float32) ** block_levels(streams_of[7], (D,), ((0, 2),), -0.2, 0.2), 0.5, 1.5)
    return {"q_proj": q_proj, "k_proj": k_proj, "v_proj": v_proj, "grad_out": grad_out, "w_first": w_first, "w_second": w_second, "decay_rate": decay_rate, "skip_gain": skip_gain}


HIGH = lax.Precision.HIGHEST


def positional_table(length, band_count):
    positions = jnp.arange(length, dtype=jnp.int32)
    band_index = jnp.arange(band_count, dtype=jnp.int32)
    frequency = 3 * (band_index + 1) * (band_index + 1) + band_index
    phase_index = (positions[:, None] * frequency[None, :]) % length
    angles = phase_index.astype(jnp.float32) * (2.0 * math.pi / length)
    return jnp.concatenate([jnp.sin(angles), jnp.cos(angles)], axis=1)


def reference(q_proj, k_proj, v_proj, grad_out, w_first, w_second, decay_rate, skip_gain):
    length = SEQ
    scale_seq = length ** -0.5
    padded_len = 2 * length
    positional = positional_table(length, E // 2)
    sine_input = jnp.dot(positional, w_first, precision=HIGH, preferred_element_type=jnp.float32)
    hidden = jnp.sin(sine_input)
    gated_in = (k_proj.astype(jnp.float32) * v_proj.astype(jnp.float32)).astype(jnp.bfloat16)
    gated_grad = (grad_out.astype(jnp.float32) * q_proj.astype(jnp.float32)).astype(jnp.bfloat16)
    block_width = math.gcd(D, 512)
    block_count = D // block_width
    fraction = jnp.arange(length).astype(jnp.float32) / length

    def one_block(grad_hidden, block_index):
        block_start = (block_index * block_width).astype(jnp.int32)
        gated_full = lax.dynamic_slice_in_dim(gated_in, block_start, block_width, 1).astype(jnp.float32)
        grad_full = lax.dynamic_slice_in_dim(gated_grad, block_start, block_width, 1).astype(jnp.float32)
        w_block = lax.dynamic_slice_in_dim(w_second, block_start, block_width, 1)
        decay_block = lax.dynamic_slice_in_dim(decay_rate, block_start, block_width, 0)
        skip_block = lax.dynamic_slice_in_dim(skip_gain, block_start, block_width, 0)
        raw_filter = jnp.dot(hidden, w_block, precision=HIGH, preferred_element_type=jnp.float32)
        envelope = jnp.exp(-decay_block[None, :] * fraction[:, None])
        long_filter = raw_filter * envelope * scale_seq
        spectrum_filter = jnp.fft.rfft(long_filter, n=padded_len, axis=0)
        spectrum_in = jnp.fft.rfft(gated_full, n=padded_len, axis=0)
        spectrum_grad = jnp.fft.rfft(grad_full, n=padded_len, axis=0)
        convolved = jnp.fft.irfft(spectrum_filter * spectrum_in, n=padded_len, axis=0)[:length]
        convolved = convolved + skip_block[None, :] * gated_full
        grad_gated = jnp.fft.irfft(jnp.conj(spectrum_filter) * spectrum_grad, n=padded_len, axis=0)[:length]
        grad_gated = grad_gated + skip_block[None, :] * grad_full
        grad_filter = jnp.fft.irfft(jnp.conj(spectrum_in) * spectrum_grad, n=padded_len, axis=0)[:length]
        grad_raw = grad_filter * envelope * scale_seq
        grad_skip = jnp.sum(grad_full * gated_full, axis=0) * scale_seq
        grad_decay = -jnp.sum(grad_raw * raw_filter * fraction[:, None], axis=0) * scale_seq
        grad_second = jnp.dot(hidden.T, grad_raw, precision=HIGH, preferred_element_type=jnp.float32) * scale_seq
        grad_hidden = grad_hidden + jnp.dot(grad_raw, w_block.T, precision=HIGH, preferred_element_type=jnp.float32)
        return grad_hidden, (convolved.astype(jnp.bfloat16), grad_gated.astype(jnp.bfloat16), grad_skip, grad_decay, grad_second)

    grad_hidden, stacked = lax.scan(one_block, jnp.zeros((length, F), jnp.float32), jnp.arange(block_count))
    convolved, grad_gated, grad_skip, grad_decay, grad_second = stacked
    convolved = jnp.transpose(convolved, (1, 0, 2)).reshape(length, D)
    grad_gated = jnp.transpose(grad_gated, (1, 0, 2)).reshape(length, D).astype(jnp.float32)
    grad_second = jnp.transpose(grad_second, (1, 0, 2)).reshape(F, D)
    grad_skip = grad_skip.reshape(D)
    grad_decay = grad_decay.reshape(D)
    grad_q = (grad_out.astype(jnp.float32) * convolved.astype(jnp.float32)).astype(jnp.bfloat16)
    grad_k = (grad_gated * v_proj.astype(jnp.float32)).astype(jnp.bfloat16)
    grad_v = (grad_gated * k_proj.astype(jnp.float32)).astype(jnp.bfloat16)
    grad_first = jnp.dot(positional.T, grad_hidden * jnp.cos(sine_input), precision=HIGH, preferred_element_type=jnp.float32) * scale_seq
    return (grad_q, grad_k, grad_v, grad_first, grad_second, grad_decay, grad_skip)
```

```python
import functools
import math

import jax
import jax.numpy as jnp
import ml_dtypes
import numpy as np
from jax import lax
from jax.experimental import pallas as pl
from jax.experimental.pallas import tpu as pltpu
from jax.sharding import PartitionSpec as P

HIGH = lax.Precision.HIGHEST
HEIGHT = 128
VMEM_BYTES = 56 * 1024 * 1024


def positional_table(length, band_count):
    positions = jnp.arange(length, dtype=jnp.int32)
    band_index = jnp.arange(band_count, dtype=jnp.int32)
    frequency = 3 * (band_index + 1) * (band_index + 1) + band_index
    phase_index = positions[:, None] * frequency[None, :] % length
    angles = phase_index.astype(jnp.float32) * (2.0 * math.pi / length)
    return jnp.concatenate([jnp.sin(angles), jnp.cos(angles)], axis=1)


@functools.lru_cache(maxsize=None)
def transform_tables(length, height):
    j = np.arange(height)
    angles = (j[:, None] * j[None, :] % height) * (2.0 * np.pi / height)
    cosine, sine = np.cos(angles), np.sin(angles)
    forward = np.concatenate(
        [np.concatenate([cosine, sine], axis=1), np.concatenate([-sine, cosine], axis=1)], axis=0
    )
    return np.stack([forward, forward.T / length]).astype(np.float32)


@functools.lru_cache(maxsize=None)
def twiddle_table(length, height, lane):
    parts = length // height
    r = np.arange(parts)[:, None]
    j = np.arange(height)[None, :]
    angles = (j * (4 * r + 1) % (4 * length)) * (2.0 * np.pi / (4 * length))
    both = np.concatenate([np.cos(angles), -np.sin(angles)], axis=1).astype(np.float32)
    return np.repeat(both[:, :, None], lane, axis=2)


def turn(value, cosine, sine):
    real, imag = value
    return (real * cosine - imag * sine, real * sine + imag * cosine)


def small_fft(values, sign):
    count = len(values)
    if count == 1:
        return values
    even = small_fft(values[0::2], sign)
    odd = small_fft(values[1::2], sign)
    first, second = [], []
    for k in range(count // 2):
        real, imag = odd[k]
        if k == 0:
            pass
        elif 4 * k == count:
            real, imag = (-imag, real) if sign > 0 else (imag, -real)
        elif 8 * k == count:
            half = math.sqrt(0.5)
            if sign > 0:
                real, imag = (real - imag) * half, (real + imag) * half
            else:
                real, imag = (real + imag) * half, (imag - real) * half
        elif 8 * k == 3 * count:
            half = math.sqrt(0.5)
            if sign > 0:
                real, imag = (real + imag) * -half, (real - imag) * half
            else:
                real, imag = (imag - real) * half, (real + imag) * -half
        else:
            angle = sign * 2.0 * math.pi * k / count
            real, imag = turn((real, imag), math.cos(angle), math.sin(angle))
        base_real, base_imag = even[k]
        first.append((base_real + real, base_imag + imag))
        second.append((base_real - real, base_imag - imag))
    return first + second


def parts_forward(values):
    count = len(values)
    turned = []
    for p, value in enumerate(values):
        angle = 2.0 * math.pi * p / (4 * count)
        turned.append((value * math.cos(angle), value * -math.sin(angle)))
    return small_fft(turned, -1)


def parts_inverse(values):
    count = len(values)
    result = []
    for p, (real, imag) in enumerate(small_fft(values, 1)):
        angle = 2.0 * math.pi * p / (4 * count)
        result.append(real * math.cos(angle) - imag * math.sin(angle))
    return result


def split_table(table_ref, split_ref):
    table = table_ref[...]
    high = table.astype(jnp.bfloat16)
    split_ref[0] = high
    split_ref[1] = (table - high.astype(jnp.float32)).astype(jnp.bfloat16)


def dot_three(split_ref, direction, value):
    high, low = split_ref[0, direction], split_ref[1, direction]
    value_high = value.astype(jnp.bfloat16)
    value_low = (value - value_high.astype(jnp.float32)).astype(jnp.bfloat16)
    dot = functools.partial(jnp.dot, preferred_element_type=jnp.float32)
    return dot(high, value_high) + (dot(high, value_low) + dot(low, value_high))


def spectrum_product(left, right, height, conjugate):
    left_real, left_imag = left[:height], left[height:]
    right_real, right_imag = right[:height], right[height:]
    if conjugate:
        return jnp.concatenate(
            [
                left_real * right_real + left_imag * right_imag,
                left_real * right_imag - left_imag * right_real,
            ],
            axis=0,
        )
    return jnp.concatenate(
        [
            left_real * right_real - left_imag * right_imag,
            left_real * right_imag + left_imag * right_real,
        ],
        axis=0,
    )


def each_chunk(height, width, body):
    lane = min(width, 128)

    def one(index, carry):
        row = pl.multiple_of(index * 16, 16)
        for at in range(0, width, lane):
            body(row, slice(at, at + lane))
        return carry

    lax.fori_loop(0, height // 16, one, 0)


def first_stage(load, work, twiddle_ref, parts, height, width):
    def body(row, lanes):
        values = [load(p, row, lanes) for p in range(parts)]
        for half in (0, 8):
            upper = pl.ds(row + half, 8)
            lower = pl.ds(height + row + half, 8)
            turned = parts_forward([value[half : half + 8] for value in values])
            for r, value in enumerate(turned):
                real, imag = turn(value, twiddle_ref[r, upper, :], twiddle_ref[r, lower, :])
                work[r, upper, lanes] = real
                work[r, lower, lanes] = imag

    each_chunk(height, width, body)


def last_stage(store, work, twiddle_ref, parts, height, width):
    def body(row, lanes):
        halves = []
        for half in (0, 8):
            upper = pl.ds(row + half, 8)
            lower = pl.ds(height + row + half, 8)
            values = [
                turn(
                    (work[r, upper, lanes], work[r, lower, lanes]),
                    twiddle_ref[r, upper, :],
                    -twiddle_ref[r, lower, :],
                )
                for r in range(parts)
            ]
            halves.append(parts_inverse(values))
        for p in range(parts):
            store(p, row, lanes, jnp.concatenate([halves[0][p], halves[1][p]], axis=0))

    each_chunk(height, width, body)


def envelope_at(decay, row, length, shape):
    position = (row + lax.broadcasted_iota(jnp.int32, shape, 0)).astype(jnp.float32)
    fraction = position * (1.0 / length)
    return jnp.exp(-decay * fraction), fraction


def filter_kernel(
    group, hidden_ref, w_ref, decay_ref, table_ref, twiddle_ref, filter_ref, spectrum_ref, work, split
):
    parts, height = work.shape[0], work.shape[1] // 2
    length, width = filter_ref.shape
    scale = length**-0.5
    step = pl.program_id(0)

    @pl.when(step == 0)
    def _():
        split_table(table_ref, split)
        filter_ref[...] = jnp.dot(
            hidden_ref[...], w_ref[...], precision=HIGH, preferred_element_type=jnp.float32
        )

        def load(p, row, lanes):
            rows = pl.ds(pl.multiple_of(p * height + row, 16), 16)
            raw = filter_ref[rows, lanes]
            envelope, _ = envelope_at(decay_ref[:, lanes], p * height + row, length, raw.shape)
            value = raw * envelope * scale
            filter_ref[rows, lanes] = value
            return value

        first_stage(load, work, twiddle_ref, parts, height, width)

    for b in range(group):
        spectrum_ref[b] = dot_three(split, 0, work[step * group + b])


def conv_kernel(
    group, x_ref, h_ref, table_ref, twiddle_ref, skip_ref, y_ref, spectrum_ref, work, split
):
    parts, height = work.shape[0], work.shape[1] // 2
    width = x_ref.shape[1]
    step = pl.program_id(0)

    def load(p, row, lanes):
        rows = pl.ds(pl.multiple_of(p * height + row, 16), 16)
        return x_ref[rows, lanes].astype(jnp.float32)

    @pl.when(step == 0)
    def _():
        split_table(table_ref, split)
        first_stage(load, work, twiddle_ref, parts, height, width)

    for b in range(group):
        at = step * group + b
        spectrum = dot_three(split, 0, work[at])
        spectrum_ref[b] = spectrum
        product = spectrum_product(h_ref[b], spectrum, height, False)
        work[at] = dot_three(split, 1, product)

    @pl.when(step == pl.num_programs(0) - 1)
    def _():
        def store(p, row, lanes, value):
            rows = pl.ds(pl.multiple_of(p * height + row, 16), 16)
            value = value + skip_ref[:, lanes] * load(p, row, lanes)
            y_ref[rows, lanes] = value.astype(jnp.bfloat16)

        last_stage(store, work, twiddle_ref, parts, height, width)


def grad_kernel(
    group,
    x_ref,
    g_ref,
    h_ref,
    xs_ref,
    table_ref,
    twiddle_ref,
    skip_ref,
    decay_ref,
    filter_ref,
    hidden_t_ref,
    w_t_ref,
    cosine_ref,
    positional_t_ref,
    z_ref,
    small_ref,
    first_ref,
    work,
    other,
    raw,
    sums,
    split,
):
    parts, height = work.shape[0], work.shape[1] // 2
    length, width = g_ref.shape
    hidden_count = hidden_t_ref.shape[0]
    scale = length**-0.5
    step = pl.program_id(0)

    def rows_of(p, row):
        return pl.ds(pl.multiple_of(p * height + row, 16), 16)

    @pl.when(step == 0)
    def _():
        split_table(table_ref, split)
        sums[...] = jnp.zeros_like(sums)

        def load(p, row, lanes):
            value = g_ref[rows_of(p, row), lanes].astype(jnp.float32)
            both = value * x_ref[rows_of(p, row), lanes].astype(jnp.float32)
            sums[0, :, lanes] += both[:8] + both[8:]
            return value

        first_stage(load, work, twiddle_ref, parts, height, width)

    for b in range(group):
        at = step * group + b
        spectrum = dot_three(split, 0, work[at])
        product = spectrum_product(h_ref[b], spectrum, height, True)
        work[at] = dot_three(split, 1, product)
        product = spectrum_product(xs_ref[b], spectrum, height, True)
        other[at] = dot_three(split, 1, product)

    @pl.when(step == pl.num_programs(0) - 1)
    def _():
        def store(p, row, lanes, value):
            grad = g_ref[rows_of(p, row), lanes].astype(jnp.float32)
            value = value + skip_ref[:, lanes] * grad
            z_ref[rows_of(p, row), lanes] = value.astype(jnp.bfloat16)

        last_stage(store, work, twiddle_ref, parts, height, width)

        def store_raw(p, row, lanes, value):
            rows = rows_of(p, row)
            envelope, fraction = envelope_at(
                decay_ref[:, lanes], p * height + row, length, value.shape
            )
            both = value * filter_ref[rows, lanes] * fraction
            sums[1, :, lanes] += both[:8] + both[8:]
            raw[rows, lanes] = value * envelope * scale

        last_stage(store_raw, other, twiddle_ref, parts, height, width)

        dot = functools.partial(jnp.dot, precision=HIGH, preferred_element_type=jnp.float32)
        second = jnp.zeros((hidden_count, width), jnp.float32)
        first = jnp.zeros(first_ref.shape, jnp.float32)
        chunk = min(length, 512)
        for at in range(0, length, chunk):
            rows = slice(at, at + chunk)
            grad_raw = raw[rows, :]
            second += dot(hidden_t_ref[:, rows], grad_raw)
            hidden_part = dot(grad_raw, w_t_ref[...])
            first += dot(positional_t_ref[:, rows], hidden_part * cosine_ref[rows, :])
        small_ref[:hidden_count, :] = second * scale
        first_ref[...] = first * scale
        tail = small_ref.shape[0] - hidden_count
        place = lax.broadcasted_iota(jnp.int32, (tail, width), 0)
        skip_sum = jnp.sum(sums[0], axis=0, keepdims=True) * scale
        decay_sum = jnp.sum(sums[1], axis=0, keepdims=True) * -scale
        small_ref[hidden_count:, :] = jnp.where(
            place == 0, decay_sum, jnp.where(place == 1, skip_sum, 0.0)
        )


def whole(*shape):
    return pl.BlockSpec(
        shape, lambda i: (0,) * len(shape), pipeline_mode=pl.Buffered(buffer_count=1)
    )


def params():
    return pltpu.CompilerParams(vmem_limit_bytes=VMEM_BYTES)


def estimate(flops, nbytes):
    return pl.CostEstimate(flops=flops, bytes_accessed=nbytes, transcendentals=0)


def gate_kernel(left_ref, right_ref, out_ref):
    width = out_ref.shape[2]
    for at in range(out_ref.shape[0]):
        lanes = slice(at * width, (at + 1) * width)
        left = left_ref[:, lanes].astype(jnp.float32)
        right = right_ref[:, lanes].astype(jnp.float32)
        out_ref[at] = (left * right).astype(jnp.bfloat16)


def gate(left, right, count):
    rows, columns = left.shape
    width = columns // count
    if width % 128 != 0:
        product = (left.astype(jnp.float32) * right.astype(jnp.float32)).astype(jnp.bfloat16)
        return product.reshape(rows, count, width).transpose(1, 0, 2).reshape(count * rows, width)
    group = math.gcd(count, 4)
    wide = pl.BlockSpec((rows, group * width), lambda i: (0, i))
    out = pl.pallas_call(
        gate_kernel,
        grid=(count // group,),
        in_specs=[wide, wide],
        out_specs=pl.BlockSpec((group, rows, width), lambda i: (i, 0, 0)),
        out_shape=jax.ShapeDtypeStruct((count, rows, width), jnp.bfloat16),
        compiler_params=params(),
        cost_estimate=estimate(rows * columns, rows * columns * 6),
    )(left, right)
    return out.reshape(count * rows, width)


def ungate_kernel(back_ref, *refs):
    count = len(refs) // 2
    width = back_ref.shape[2]
    for at in range(back_ref.shape[0]):
        lanes = slice(at * width, (at + 1) * width)
        back = back_ref[at].astype(jnp.float32)
        for factor_ref, out_ref in zip(refs[:count], refs[count:]):
            out_ref[:, lanes] = (back * factor_ref[:, lanes].astype(jnp.float32)).astype(
                jnp.bfloat16
            )


def ungate(back, factors, count):
    rows, columns = factors[0].shape
    width = columns // count
    back = back.reshape(count, rows, width)
    if width % 128 != 0:
        back = back.transpose(1, 0, 2).reshape(rows, columns).astype(jnp.float32)
        return [(back * factor.astype(jnp.float32)).astype(jnp.bfloat16) for factor in factors]
    group = math.gcd(count, 4)
    wide = pl.BlockSpec((rows, group * width), lambda i: (0, i))
    return pl.pallas_call(
        ungate_kernel,
        grid=(count // group,),
        in_specs=[pl.BlockSpec((group, rows, width), lambda i: (i, 0, 0))]
        + [wide] * len(factors),
        out_specs=[wide] * len(factors),
        out_shape=[jax.ShapeDtypeStruct((rows, columns), jnp.bfloat16)] * len(factors),
        compiler_params=params(),
        cost_estimate=estimate(rows * columns, rows * columns * (2 + 4 * len(factors))),
    )(back, *factors)


def per_device(q_proj, k_proj, v_proj, grad_out, w_first, w_second, decay_rate, skip_gain):
    tok_rows, chan_tp = q_proj.shape
    seq_count = lax.axis_size("seq")
    length = tok_rows * seq_count
    width = chan_tp // seq_count
    height = HEIGHT
    parts = length // height
    group = math.gcd(parts, max(1, 64 // parts))
    hidden_count = w_first.shape[1]
    band_total = w_first.shape[0]
    scale = length ** (-0.5)
    seq_index = lax.axis_index("seq")

    def exchange(values):
        return lax.all_to_all(values, "seq", split_axis=0, concat_axis=0, tiled=True)

    gated_in = exchange(gate(k_proj, v_proj, seq_count))
    gated_grad = exchange(gate(grad_out, q_proj, seq_count))

    tables = jnp.asarray(transform_tables(length, height))
    twiddle = jnp.asarray(twiddle_table(length, height, min(width, 128)))
    positional = positional_table(length, band_total // 2)
    sine_input = jnp.dot(positional, w_first, precision=HIGH, preferred_element_type=jnp.float32)
    hidden = jnp.sin(sine_input)
    cosine = jnp.cos(sine_input)
    offset = seq_index * width
    w_mine = lax.dynamic_slice_in_dim(w_second, offset, width, 1)
    decay_mine = lax.dynamic_slice_in_dim(decay_rate, offset, width, 0)[None, :]
    skip_mine = lax.dynamic_slice_in_dim(skip_gain, offset, width, 0)[None, :]

    table_specs = [whole(*tables.shape), whole(*twiddle.shape)]
    spectrum = pl.BlockSpec((group, 2 * height, width), lambda i: (i, 0, 0))
    spectrum_shape = jax.ShapeDtypeStruct((parts, 2 * height, width), jnp.float32)
    work = pltpu.VMEM((parts, 2 * height, width), jnp.float32)
    split = pltpu.VMEM((2,) + tables.shape, jnp.bfloat16)
    grid = (parts // group,)
    product_flops = 2 * 3 * parts * 4 * height * height * width

    long_filter, filter_spectrum = pl.pallas_call(
        functools.partial(filter_kernel, group),
        grid=grid,
        in_specs=[
            whole(length, hidden_count),
            whole(hidden_count, width),
            whole(1, width),
            *table_specs,
        ],
        out_specs=[whole(length, width), spectrum],
        out_shape=[jax.ShapeDtypeStruct((length, width), jnp.float32), spectrum_shape],
        scratch_shapes=[work, split],
        compiler_params=params(),
        cost_estimate=estimate(product_flops, length * width * 12),
    )(hidden, w_mine, decay_mine, tables, twiddle)

    convolved, in_spectrum = pl.pallas_call(
        functools.partial(conv_kernel, group),
        grid=grid,
        in_specs=[
            whole(length, width),
            spectrum,
            *table_specs,
            whole(1, width),
        ],
        out_specs=[whole(length, width), spectrum],
        out_shape=[jax.ShapeDtypeStruct((length, width), jnp.bfloat16), spectrum_shape],
        scratch_shapes=[work, split],
        compiler_params=params(),
        cost_estimate=estimate(2 * product_flops, length * width * 20),
    )(gated_in, filter_spectrum, tables, twiddle, skip_mine)
    conv_back = exchange(convolved)

    small_rows = hidden_count + 8
    grad_gated, small, first_part = pl.pallas_call(
        functools.partial(grad_kernel, group),
        grid=grid,
        in_specs=[
            whole(length, width),
            whole(length, width),
            spectrum,
            spectrum,
            *table_specs,
            whole(1, width),
            whole(1, width),
            whole(length, width),
            whole(hidden_count, length),
            whole(width, hidden_count),
            whole(length, hidden_count),
            whole(band_total, length),
        ],
        out_specs=[
            whole(length, width),
            whole(small_rows, width),
            whole(band_total, hidden_count),
        ],
        out_shape=[
            jax.ShapeDtypeStruct((length, width), jnp.bfloat16),
            jax.ShapeDtypeStruct((small_rows, width), jnp.float32),
            jax.ShapeDtypeStruct((band_total, hidden_count), jnp.float32),
        ],
        scratch_shapes=[
            work,
            work,
            pltpu.VMEM((length, width), jnp.float32),
            pltpu.VMEM((2, 8, width), jnp.float32),
            split,
        ],
        compiler_params=params(),
        cost_estimate=estimate(3 * product_flops, length * width * 30),
    )(
        gated_in,
        gated_grad,
        filter_spectrum,
        in_spectrum,
        tables,
        twiddle,
        skip_mine,
        decay_mine,
        long_filter,
        hidden.T,
        w_mine.T,
        cosine,
        positional.T,
    )
    grad_back = exchange(grad_gated)
    gathered = lax.all_gather(small, "seq", axis=1, tiled=True)
    grad_first = lax.psum(first_part, ("seq", "tp"))
    grad_second = gathered[:hidden_count]
    grad_decay = gathered[hidden_count]
    grad_skip = gathered[hidden_count + 1]
    (grad_q,) = ungate(conv_back, [grad_out], seq_count)
    grad_k, grad_v = ungate(grad_back, [v_proj, k_proj], seq_count)
    return (grad_q, grad_k, grad_v, grad_first, grad_second, grad_decay, grad_skip)


def solution(mesh):
    return jax.shard_map(
        per_device,
        mesh=mesh,
        in_specs=(
            P("seq", "tp"),
            P("seq", "tp"),
            P("seq", "tp"),
            P("seq", "tp"),
            P(),
            P(None, "tp"),
            P("tp"),
            P("tp"),
        ),
        out_specs=(
            P("seq", "tp"),
            P("seq", "tp"),
            P("seq", "tp"),
            P(),
            P(None, "tp"),
            P("tp"),
            P("tp"),
        ),
        check_vma=False,
    )
```

```python
import functools
import math

import jax
import jax.numpy as jnp
import ml_dtypes
import numpy as np
from jax import lax
from jax.experimental import pallas as pl
from jax.experimental.pallas import tpu as pltpu
from jax.sharding import PartitionSpec as P

HIGH = lax.Precision.HIGHEST
MIB = 1024 * 1024


def positional_table(length, band_count):
    positions = jnp.arange(length, dtype=jnp.int32)
    band_index = jnp.arange(band_count, dtype=jnp.int32)
    frequency = 3 * (band_index + 1) * (band_index + 1) + band_index
    phase_index = positions[:, None] * frequency[None, :] % length
    angles = phase_index.astype(jnp.float32) * (2.0 * math.pi / length)
    return jnp.concatenate([jnp.sin(angles), jnp.cos(angles)], axis=1)


@functools.lru_cache(maxsize=None)
def transform_tables(length, height):
    j = np.arange(height)
    angles = (j[:, None] * j[None, :] % height) * (2.0 * np.pi / height)
    cosine, sine = np.cos(angles), np.sin(angles)
    forward = np.concatenate(
        [np.concatenate([cosine, sine], axis=1), np.concatenate([-sine, cosine], axis=1)], axis=0
    )
    return np.stack([forward, forward.T / length]).astype(np.float32)


@functools.lru_cache(maxsize=None)
def twiddle_table(length, height, lane):
    parts = length // height
    r = np.arange(parts)[:, None]
    j = np.arange(height)[None, :]
    angles = (j * (4 * r + 1) % (4 * length)) * (2.0 * np.pi / (4 * length))
    both = np.concatenate([np.cos(angles), -np.sin(angles)], axis=1).astype(np.float32)
    return np.repeat(both[:, :, None], lane, axis=2)


def turn(value, cosine, sine):
    real, imag = value
    return (real * cosine - imag * sine, real * sine + imag * cosine)


def small_fft(values, sign):
    count = len(values)
    if count == 1:
        return values
    even = small_fft(values[0::2], sign)
    odd = small_fft(values[1::2], sign)
    first, second = [], []
    for k in range(count // 2):
        real, imag = odd[k]
        if k == 0:
            pass
        elif 4 * k == count:
            real, imag = (-imag, real) if sign > 0 else (imag, -real)
        elif 8 * k == count:
            half = math.sqrt(0.5)
            if sign > 0:
                real, imag = (real - imag) * half, (real + imag) * half
            else:
                real, imag = (real + imag) * half, (imag - real) * half
        elif 8 * k == 3 * count:
            half = math.sqrt(0.5)
            if sign > 0:
                real, imag = (real + imag) * -half, (real - imag) * half
            else:
                real, imag = (imag - real) * half, (real + imag) * -half
        else:
            angle = sign * 2.0 * math.pi * k / count
            real, imag = turn((real, imag), math.cos(angle), math.sin(angle))
        base_real, base_imag = even[k]
        first.append((base_real + real, base_imag + imag))
        second.append((base_real - real, base_imag - imag))
    return first + second


def parts_forward(values):
    count = len(values)
    turned = []
    for p, value in enumerate(values):
        angle = 2.0 * math.pi * p / (4 * count)
        turned.append((value * math.cos(angle), value * -math.sin(angle)))
    return small_fft(turned, -1)


def parts_inverse(values):
    count = len(values)
    result = []
    for p, (real, imag) in enumerate(small_fft(values, 1)):
        angle = 2.0 * math.pi * p / (4 * count)
        result.append(real * math.cos(angle) - imag * math.sin(angle))
    return result


def split_table(table_ref, split_ref):
    table = table_ref[...]
    high = table.astype(jnp.bfloat16)
    split_ref[0] = high
    split_ref[1] = (table - high.astype(jnp.float32)).astype(jnp.bfloat16)


def dot_three(split_ref, direction, value):
    high, low = split_ref[0, direction], split_ref[1, direction]
    value_high = value.astype(jnp.bfloat16)
    value_low = (value - value_high.astype(jnp.float32)).astype(jnp.bfloat16)
    dot = functools.partial(jnp.dot, preferred_element_type=jnp.float32)
    return dot(high, value_high) + (dot(high, value_low) + dot(low, value_high))


def spectrum_product(left, right, height, conjugate):
    left_real, left_imag = left[:height], left[height:]
    right_real, right_imag = right[:height], right[height:]
    if conjugate:
        return jnp.concatenate(
            [
                left_real * right_real + left_imag * right_imag,
                left_real * right_imag - left_imag * right_real,
            ],
            axis=0,
        )
    return jnp.concatenate(
        [
            left_real * right_real - left_imag * right_imag,
            left_real * right_imag + left_imag * right_real,
        ],
        axis=0,
    )


def lane_slices(width):
    lane = min(width, 128)
    return [slice(at, at + lane) for at in range(0, width, lane)]


def first_chunk(load, work, twiddle_ref, index):
    parts, height = work.shape[0], work.shape[1] // 2
    row = pl.multiple_of(index * 16, 16)
    for lanes in lane_slices(work.shape[2]):
        values = [load(p, row, lanes) for p in range(parts)]
        for half in (0, 8):
            upper = pl.ds(row + half, 8)
            lower = pl.ds(height + row + half, 8)
            turned = parts_forward([value[half : half + 8] for value in values])
            for r, value in enumerate(turned):
                real, imag = turn(value, twiddle_ref[r, upper, :], twiddle_ref[r, lower, :])
                work[r, upper, lanes] = real
                work[r, lower, lanes] = imag


def last_chunk(store, work, twiddle_ref, index):
    parts, height = work.shape[0], work.shape[1] // 2
    row = pl.multiple_of(index * 16, 16)
    for lanes in lane_slices(work.shape[2]):
        halves = []
        for half in (0, 8):
            upper = pl.ds(row + half, 8)
            lower = pl.ds(height + row + half, 8)
            values = [
                turn(
                    (work[r, upper, lanes], work[r, lower, lanes]),
                    twiddle_ref[r, upper, :],
                    -twiddle_ref[r, lower, :],
                )
                for r in range(parts)
            ]
            halves.append(parts_inverse(values))
        for p in range(parts):
            store(p, row, lanes, jnp.concatenate([halves[0][p], halves[1][p]], axis=0))


def run_chunks(height, chunk, parts=0, block=None):
    chunks = height // 16
    group = parts // chunks if parts % chunks == 0 else 0

    def one(index, carry):
        for b in range(group):
            block(index * group + b)
        chunk(index)
        return carry

    lax.fori_loop(0, chunks, one, 0)
    if group == 0 and parts > 0:
        run_blocks(parts, block)


def run_blocks(parts, block):
    def one(index, carry):
        block(index)
        return carry

    lax.fori_loop(0, parts, one, 0)


def envelope_at(decay, row, length, shape):
    position = (row + lax.broadcasted_iota(jnp.int32, shape, 0)).astype(jnp.float32)
    fraction = position * (1.0 / length)
    return jnp.exp(-decay * fraction), fraction


def filter_kernel(
    hidden_ref, w_ref, decay_ref, table_ref, twiddle_ref, filter_ref, spectrum_ref, work, split
):
    parts, height = work.shape[0], work.shape[1] // 2
    length = filter_ref.shape[0]
    scale = length**-0.5
    split_table(table_ref, split)
    filter_ref[...] = jnp.dot(
        hidden_ref[...], w_ref[...], precision=HIGH, preferred_element_type=jnp.float32
    )

    def load(p, row, lanes):
        rows = pl.ds(pl.multiple_of(p * height + row, 16), 16)
        raw = filter_ref[rows, lanes]
        envelope, _ = envelope_at(decay_ref[:, lanes], p * height + row, length, raw.shape)
        value = raw * envelope * scale
        filter_ref[rows, lanes] = value
        return value

    def block(r):
        spectrum_ref[r] = dot_three(split, 0, work[r])

    run_chunks(height, lambda i: first_chunk(load, work, twiddle_ref, i))
    run_blocks(parts, block)


def main_kernel(
    both_ref,
    h_any,
    table_ref,
    twiddle_ref,
    skip_ref,
    back_ref,
    cross_any,
    work_in,
    work_grad,
    cross,
    h,
    split,
    sems,
):
    parts, height = work_in.shape[0], work_in.shape[1] // 2
    copy_in = pltpu.make_async_copy(h_any, h, sems.at[0])
    copy_in.start()
    split_table(table_ref, split)

    def load_from(which):
        def load(p, row, lanes):
            return both_ref[p, which, pl.ds(row, 16), lanes].astype(jnp.float32)

        return load

    def store_to(which):
        load = load_from(which)

        def store(p, row, lanes, value):
            value = value + skip_ref[:, lanes] * load(p, row, lanes)
            back_ref[p, which, pl.ds(row, 16), lanes] = value.astype(jnp.bfloat16)

        return store

    def block_in(r):
        spectrum = dot_three(split, 0, work_in[r])
        cross[r] = spectrum
        work_in[r] = dot_three(split, 1, spectrum_product(h[r], spectrum, height, False))

    def block_grad(r):
        spectrum = dot_three(split, 0, work_grad[r])
        cross[r] = spectrum_product(cross[r], spectrum, height, True)
        work_grad[r] = dot_three(split, 1, spectrum_product(h[r], spectrum, height, True))

    run_chunks(height, lambda i: first_chunk(load_from(0), work_in, twiddle_ref, i))
    copy_in.wait()
    run_chunks(
        height, lambda i: first_chunk(load_from(1), work_grad, twiddle_ref, i), parts, block_in
    )
    run_chunks(
        height, lambda i: last_chunk(store_to(0), work_in, twiddle_ref, i), parts, block_grad
    )
    copy_out = pltpu.make_async_copy(cross, cross_any, sems.at[1])
    copy_out.start()
    run_chunks(height, lambda i: last_chunk(store_to(1), work_grad, twiddle_ref, i))
    copy_out.wait()


def filter_grad_kernel(
    both_ref,
    cross_ref,
    table_ref,
    twiddle_ref,
    decay_ref,
    filter_ref,
    hidden_t_ref,
    w_t_ref,
    cosine_ref,
    positional_t_ref,
    small_ref,
    first_ref,
    work,
    raw,
    sums,
    split,
):
    parts, height = work.shape[0], work.shape[1] // 2
    length, width = raw.shape
    hidden_count = hidden_t_ref.shape[0]
    band_total = positional_t_ref.shape[0]
    scale = length**-0.5
    split_table(table_ref, split)
    sums[...] = jnp.zeros_like(sums)

    def block(r):
        work[r] = dot_three(split, 1, cross_ref[r])

    def store(p, row, lanes, value):
        rows = pl.ds(pl.multiple_of(p * height + row, 16), 16)
        envelope, fraction = envelope_at(
            decay_ref[:, lanes], p * height + row, length, value.shape
        )
        both = value * filter_ref[rows, lanes] * fraction
        sums[1, :, lanes] += both[:8] + both[8:]
        raw[rows, lanes] = value * envelope * scale
        left = both_ref[p, 0, pl.ds(row, 16), lanes].astype(jnp.float32)
        right = both_ref[p, 1, pl.ds(row, 16), lanes].astype(jnp.float32)
        both = left * right
        sums[0, :, lanes] += both[:8] + both[8:]

    run_blocks(parts, block)
    run_chunks(height, lambda i: last_chunk(store, work, twiddle_ref, i))

    dot = functools.partial(jnp.dot, precision=HIGH, preferred_element_type=jnp.float32)
    second = jnp.zeros((hidden_count, width), jnp.float32)
    first = jnp.zeros((band_total, hidden_count), jnp.float32)
    chunk = min(length, 512)
    for at in range(0, length, chunk):
        rows = slice(at, at + chunk)
        grad_raw = raw[rows, :]
        second += dot(hidden_t_ref[:, rows], grad_raw)
        hidden_part = dot(grad_raw, w_t_ref[...])
        first += dot(positional_t_ref[:, rows], hidden_part * cosine_ref[rows, :])

    def high_low(value):
        high = value.astype(jnp.bfloat16)
        low = (value - high.astype(jnp.float32)).astype(jnp.bfloat16)
        return high.astype(jnp.float32), low.astype(jnp.float32)

    high, low = high_low(first * scale)
    first_ref[:band_total, :] = high.astype(jnp.bfloat16)
    first_ref[band_total:, :] = low.astype(jnp.bfloat16)
    small_ref[:hidden_count, :] = (second * scale).astype(jnp.bfloat16)
    place = lax.broadcasted_iota(jnp.int32, (16, width), 0)
    tail = jnp.zeros((16, width), jnp.float32)
    decay_pair = high_low(jnp.sum(sums[1], axis=0, keepdims=True) * -scale)
    skip_pair = high_low(jnp.sum(sums[0], axis=0, keepdims=True) * scale)
    for at, row in enumerate(decay_pair + skip_pair):
        tail = jnp.where(place == at, row, tail)
    small_ref[hidden_count:, :] = tail.astype(jnp.bfloat16)


def params(limit):
    return pltpu.CompilerParams(vmem_limit_bytes=limit)


def estimate(flops, nbytes):
    return pl.CostEstimate(flops=flops, bytes_accessed=nbytes, transcendentals=0)


def gate_kernel(*refs):
    out_ref = refs[-1]
    width = out_ref.shape[3]
    for at in range(out_ref.shape[0]):
        lanes = slice(at * width, (at + 1) * width)
        for which in range(2):
            left = refs[2 * which][:, lanes].astype(jnp.float32)
            right = refs[2 * which + 1][:, lanes].astype(jnp.float32)
            out_ref[at, which] = (left * right).astype(jnp.bfloat16)


def gate(factors, count):
    rows, columns = factors[0].shape
    width = columns // count
    if width % 128 != 0:
        pairs = []
        for left, right in (factors[:2], factors[2:]):
            product = (left.astype(jnp.float32) * right.astype(jnp.float32)).astype(jnp.bfloat16)
            pairs.append(product.reshape(rows, count, width).transpose(1, 0, 2))
        return jnp.stack(pairs, axis=1)
    group = math.gcd(count, 4)
    return pl.pallas_call(
        gate_kernel,
        grid=(count // group,),
        in_specs=[pl.BlockSpec((rows, group * width), lambda i: (0, i))] * 4,
        out_specs=pl.BlockSpec((group, 2, rows, width), lambda i: (i, 0, 0, 0)),
        out_shape=jax.ShapeDtypeStruct((count, 2, rows, width), jnp.bfloat16),
        compiler_params=params(16 * MIB),
        cost_estimate=estimate(2 * rows * columns, rows * columns * 12),
    )(*factors)


def ungate_kernel(back_ref, g_ref, v_ref, k_ref, q_out, k_out, v_out):
    width = back_ref.shape[3]
    for at in range(back_ref.shape[0]):
        lanes = slice(at * width, (at + 1) * width)
        for which, factor_ref, out_ref in (
            (0, g_ref, q_out),
            (1, v_ref, k_out),
            (1, k_ref, v_out),
        ):
            back = back_ref[at, which].astype(jnp.float32)
            factor = factor_ref[:, lanes].astype(jnp.float32)
            out_ref[:, lanes] = (back * factor).astype(jnp.bfloat16)


def ungate(back, factors):
    count, _, rows, width = back.shape
    columns = count * width
    if width % 128 != 0:
        outs = []
        for which, factor in zip((0, 1, 1), factors):
            part = back[:, which].transpose(1, 0, 2).reshape(rows, columns).astype(jnp.float32)
            outs.append((part * factor.astype(jnp.float32)).astype(jnp.bfloat16))
        return outs
    group = math.gcd(count, 4)
    wide = pl.BlockSpec((rows, group * width), lambda i: (0, i))
    return pl.pallas_call(
        ungate_kernel,
        grid=(count // group,),
        in_specs=[pl.BlockSpec((group, 2, rows, width), lambda i: (i, 0, 0, 0))] + [wide] * 3,
        out_specs=[wide] * 3,
        out_shape=[jax.ShapeDtypeStruct((rows, columns), jnp.bfloat16)] * 3,
        compiler_params=params(16 * MIB),
        cost_estimate=estimate(3 * rows * columns, rows * columns * 16),
    )(back, *factors)


def per_device(q_proj, k_proj, v_proj, grad_out, w_first, w_second, decay_rate, skip_gain):
    height, chan_tp = q_proj.shape
    parts = lax.axis_size("seq")
    length = height * parts
    width = chan_tp // parts
    band_total, hidden_count = w_first.shape
    seq_index = lax.axis_index("seq")

    def exchange(values):
        return lax.all_to_all(values, "seq", split_axis=0, concat_axis=0, tiled=True)

    both = exchange(gate((k_proj, v_proj, grad_out, q_proj), parts))

    tables = jnp.asarray(transform_tables(length, height))
    twiddle = jnp.asarray(twiddle_table(length, height, min(width, 128)))
    positional = positional_table(length, band_total // 2)
    sine_input = jnp.dot(positional, w_first, precision=HIGH, preferred_element_type=jnp.float32)
    hidden = jnp.sin(sine_input)
    cosine = jnp.cos(sine_input)
    offset = seq_index * width
    w_mine = lax.dynamic_slice_in_dim(w_second, offset, width, 1)
    decay_mine = lax.dynamic_slice_in_dim(decay_rate, offset, width, 0)[None, :]
    skip_mine = lax.dynamic_slice_in_dim(skip_gain, offset, width, 0)[None, :]

    spectrum_shape = jax.ShapeDtypeStruct((parts, 2 * height, width), jnp.float32)
    work = pltpu.VMEM(spectrum_shape.shape, jnp.float32)
    split = pltpu.VMEM((2,) + tables.shape, jnp.bfloat16)
    anywhere = pl.BlockSpec(memory_space=pl.ANY)
    in_vmem = pl.BlockSpec(memory_space=pltpu.VMEM)
    product_flops = 2 * 3 * parts * 4 * height * height * width
    limit = 32 * MIB if length * max(width, 128) <= 2048 * 256 else 58 * MIB

    long_filter, filter_spectrum = pl.pallas_call(
        filter_kernel,
        in_specs=[in_vmem] * 5,
        out_specs=[in_vmem, in_vmem],
        out_shape=[jax.ShapeDtypeStruct((length, width), jnp.float32), spectrum_shape],
        scratch_shapes=[work, split],
        compiler_params=params(limit),
        cost_estimate=estimate(product_flops, length * width * 12),
    )(hidden, w_mine, decay_mine, tables, twiddle)

    back, cross = pl.pallas_call(
        main_kernel,
        in_specs=[in_vmem, anywhere, in_vmem, in_vmem, in_vmem],
        out_specs=[in_vmem, anywhere],
        out_shape=[jax.ShapeDtypeStruct(both.shape, jnp.bfloat16), spectrum_shape],
        scratch_shapes=[work, work, work, work, split, pltpu.SemaphoreType.DMA((2,))],
        compiler_params=params(limit),
        cost_estimate=estimate(4 * product_flops, length * width * 32),
    )(both, filter_spectrum, tables, twiddle, skip_mine)
    back = exchange(back)

    small, first_pair = pl.pallas_call(
        filter_grad_kernel,
        in_specs=[in_vmem] * 10,
        out_specs=[in_vmem, in_vmem],
        out_shape=[
            jax.ShapeDtypeStruct((hidden_count + 16, width), jnp.bfloat16),
            jax.ShapeDtypeStruct((2 * band_total, hidden_count), jnp.bfloat16),
        ],
        scratch_shapes=[
            work,
            pltpu.VMEM((length, width), jnp.float32),
            pltpu.VMEM((2, 8, width), jnp.float32),
            split,
        ],
        compiler_params=params(limit),
        cost_estimate=estimate(2 * product_flops, length * width * 30),
    )(
        both,
        cross,
        tables,
        twiddle,
        decay_mine,
        long_filter,
        hidden.T,
        w_mine.T,
        cosine,
        positional.T,
    )
    packed = jnp.concatenate([small, first_pair.reshape(-1, width)], axis=0)
    gathered = lax.all_gather(packed, "seq", axis=1, tiled=True).astype(jnp.float32)
    grad_second = gathered[:hidden_count]
    grad_decay = gathered[hidden_count] + gathered[hidden_count + 1]
    grad_skip = gathered[hidden_count + 2] + gathered[hidden_count + 3]
    first_rows = gathered[hidden_count + 16 :].reshape(-1, parts, width).sum(axis=1)
    grad_first = first_rows.reshape(2, band_total, hidden_count).sum(axis=0)
    if lax.axis_size("tp") == 2:
        grad_first = grad_first + lax.ppermute(grad_first, "tp", [(0, 1), (1, 0)])
    else:
        grad_first = lax.psum(grad_first, "tp")
    grad_q, grad_k, grad_v = ungate(back, (grad_out, v_proj, k_proj))
    return (grad_q, grad_k, grad_v, grad_first, grad_second, grad_decay, grad_skip)


def solution(mesh):
    return jax.shard_map(
        per_device,
        mesh=mesh,
        in_specs=(
            P("seq", "tp"),
            P("seq", "tp"),
            P("seq", "tp"),
            P("seq", "tp"),
            P(),
            P(None, "tp"),
            P("tp"),
            P("tp"),
        ),
        out_specs=(
            P("seq", "tp"),
            P("seq", "tp"),
            P("seq", "tp"),
            P(),
            P(None, "tp"),
            P("tp"),
            P("tp"),
        ),
        check_vma=False,
    )
```

```python
import functools
import math

import jax
import jax.numpy as jnp
import ml_dtypes
import numpy as np
from jax import lax
from jax.experimental import pallas as pl
from jax.experimental.pallas import tpu as pltpu
from jax.sharding import PartitionSpec as P

HIGH = lax.Precision.HIGHEST
MIB = 1024 * 1024


def positional_table(length, band_count):
    positions = jnp.arange(length, dtype=jnp.int32)
    band_index = jnp.arange(band_count, dtype=jnp.int32)
    frequency = 3 * (band_index + 1) * (band_index + 1) + band_index
    phase_index = frequency[:, None] * positions[None, :] % length
    angles = phase_index.astype(jnp.float32) * (2.0 * math.pi / length)
    return jnp.concatenate([jnp.sin(angles), jnp.cos(angles)], axis=0)


@functools.lru_cache(maxsize=None)
def transform_tables(length, height):
    j = np.arange(height)
    angles = (j[:, None] * j[None, :] % height) * (2.0 * np.pi / height)
    cosine, sine = np.cos(angles), np.sin(angles)
    forward = np.concatenate(
        [np.concatenate([cosine, -sine], axis=1), np.concatenate([sine, cosine], axis=1)], axis=0
    )
    return np.stack([forward, forward.T / length]).astype(np.float32)


@functools.lru_cache(maxsize=None)
def twiddle_table(length, height):
    parts = length // height
    r = np.arange(parts)[:, None]
    j = np.arange(height)[None, :]
    angles = (j * (4 * r + 1) % (4 * length)) * (2.0 * np.pi / (4 * length))
    return np.concatenate([np.cos(angles), -np.sin(angles)], axis=1).astype(np.float32)


def turn(value, cosine, sine):
    real, imag = value
    return (real * cosine - imag * sine, real * sine + imag * cosine)


def small_fft(values, sign):
    count = len(values)
    if count == 1:
        return values
    even = small_fft(values[0::2], sign)
    odd = small_fft(values[1::2], sign)
    first, second = [], []
    for k in range(count // 2):
        real, imag = odd[k]
        if k == 0:
            pass
        elif 4 * k == count:
            real, imag = (-imag, real) if sign > 0 else (imag, -real)
        elif 8 * k == count:
            half = math.sqrt(0.5)
            if sign > 0:
                real, imag = (real - imag) * half, (real + imag) * half
            else:
                real, imag = (real + imag) * half, (imag - real) * half
        elif 8 * k == 3 * count:
            half = math.sqrt(0.5)
            if sign > 0:
                real, imag = (real + imag) * -half, (real - imag) * half
            else:
                real, imag = (imag - real) * half, (real + imag) * -half
        else:
            angle = sign * 2.0 * math.pi * k / count
            real, imag = turn((real, imag), math.cos(angle), math.sin(angle))
        base_real, base_imag = even[k]
        first.append((base_real + real, base_imag + imag))
        second.append((base_real - real, base_imag - imag))
    return first + second


def parts_forward(values):
    count = len(values)
    turned = []
    for p, value in enumerate(values):
        angle = 2.0 * math.pi * p / (4 * count)
        turned.append((value * math.cos(angle), value * -math.sin(angle)))
    return small_fft(turned, -1)


def parts_inverse(values):
    count = len(values)
    result = []
    for p, (real, imag) in enumerate(small_fft(values, 1)):
        angle = 2.0 * math.pi * p / (4 * count)
        result.append(real * math.cos(angle) - imag * math.sin(angle))
    return result


def split_bf16(value):
    high = value.astype(jnp.bfloat16)
    return high, (value - high.astype(jnp.float32)).astype(jnp.bfloat16)


def split_table(table_ref, split):
    size = table_ref.shape[1]
    for direction in range(2):
        high, low = split_bf16(table_ref[direction])
        split[direction, :size] = high
        split[direction, size : 2 * size] = high
        split[direction, 2 * size :] = low


def transform(value, split, direction):
    high, low = split_bf16(value)
    return jnp.dot(
        jnp.concatenate([high, low, high], axis=1),
        split[direction],
        preferred_element_type=jnp.float32,
    )


def spectrum_product(left, right, conjugate):
    height = left.shape[1] // 2
    left_real, left_imag = left[:, :height], left[:, height:]
    right_real, right_imag = right[:, :height], right[:, height:]
    if conjugate:
        real = left_real * right_real + left_imag * right_imag
        imag = left_real * right_imag - left_imag * right_real
    else:
        real = left_real * right_real - left_imag * right_imag
        imag = left_real * right_imag + left_imag * right_real
    return jnp.concatenate([real, imag], axis=1)


def first_chunk(load, work, twiddle_ref, index):
    parts, height = work.shape[0], work.shape[2] // 2
    row = pl.multiple_of(index * 16, 16)
    values = [load(p, row) for p in range(parts)]
    for half in (0, 8):
        rows = pl.ds(row + half, 8)
        turned = parts_forward([value[half : half + 8] for value in values])
        for r, value in enumerate(turned):
            cosine = twiddle_ref[r : r + 1, :height]
            sine = twiddle_ref[r : r + 1, height:]
            work[r, rows, :height], work[r, rows, height:] = turn(value, cosine, sine)


def last_chunk(store, work, twiddle_ref, index):
    parts, height = work.shape[0], work.shape[2] // 2
    row = pl.multiple_of(index * 16, 16)
    halves = []
    for half in (0, 8):
        rows = pl.ds(row + half, 8)
        values = []
        for r in range(parts):
            cosine = twiddle_ref[r : r + 1, :height]
            sine = twiddle_ref[r : r + 1, height:]
            value = (work[r, rows, :height], work[r, rows, height:])
            values.append(turn(value, cosine, -sine))
        halves.append(parts_inverse(values))
    for p in range(parts):
        store(p, row, jnp.concatenate([halves[0][p], halves[1][p]], axis=0))


def run_chunks(width, chunk, parts=0, block=None):
    chunks = width // 16
    group = parts // chunks if parts % chunks == 0 and parts <= 4 * chunks else 0

    def one(index, carry):
        for b in range(group):
            block(index * group + b)
        chunk(index)
        return carry

    lax.fori_loop(0, chunks, one, 0)
    if group == 0 and parts > 0:
        run_blocks(parts, block)


def run_blocks(parts, block):
    def one(index, carry):
        block(index)
        return carry

    lax.fori_loop(0, parts, one, 0)


def envelope_at(decay, start, length, height):
    position = (start + lax.broadcasted_iota(jnp.int32, (1, height), 1)).astype(jnp.float32)
    fraction = position * (1.0 / length)
    return jnp.exp(-decay * fraction), fraction


def columns_of(p, height):
    return slice(p * height, (p + 1) * height)


def filter_kernel(
    w_t_ref, hidden_ref, decay_ref, table_ref, twiddle_ref, filter_ref, spectrum_ref, work, split
):
    parts, width, height = work.shape[0], work.shape[1], work.shape[2] // 2
    length = filter_ref.shape[1]
    scale = length**-0.5
    split_table(table_ref, split)
    filter_ref[...] = jnp.dot(
        w_t_ref[...], hidden_ref[...], precision=HIGH, preferred_element_type=jnp.float32
    )

    def load(p, row):
        rows, columns = pl.ds(row, 16), columns_of(p, height)
        envelope, _ = envelope_at(decay_ref[rows, :], p * height, length, height)
        value = filter_ref[rows, columns] * envelope * scale
        filter_ref[rows, columns] = value
        return value

    def block(r):
        spectrum_ref[r] = transform(work[r], split, 0)

    run_chunks(width, lambda i: first_chunk(load, work, twiddle_ref, i))
    run_blocks(parts, block)


def main_kernel(
    both_ref,
    h_any,
    table_ref,
    twiddle_ref,
    skip_ref,
    back_ref,
    cross_any,
    work_in,
    work_grad,
    cross,
    h,
    split,
    sems,
):
    parts, width = work_in.shape[0], work_in.shape[1]
    copy_in = pltpu.make_async_copy(h_any, h, sems.at[0])
    copy_in.start()
    split_table(table_ref, split)

    def load_from(which):
        def load(p, row):
            return both_ref[p, which, pl.ds(row, 16), :].astype(jnp.float32)

        return load

    def store_to(which):
        load = load_from(which)

        def store(p, row, value):
            value = value + skip_ref[pl.ds(row, 16), :] * load(p, row)
            back_ref[p, which, pl.ds(row, 16), :] = value.astype(jnp.bfloat16)

        return store

    def block_in(r):
        spectrum = transform(work_in[r], split, 0)
        cross[r] = spectrum
        work_in[r] = transform(spectrum_product(h[r], spectrum, False), split, 1)

    def block_grad(r):
        spectrum = transform(work_grad[r], split, 0)
        cross[r] = spectrum_product(cross[r], spectrum, True)
        work_grad[r] = transform(spectrum_product(h[r], spectrum, True), split, 1)

    run_chunks(width, lambda i: first_chunk(load_from(0), work_in, twiddle_ref, i))
    copy_in.wait()
    run_chunks(
        width, lambda i: first_chunk(load_from(1), work_grad, twiddle_ref, i), parts, block_in
    )
    run_chunks(
        width, lambda i: last_chunk(store_to(0), work_in, twiddle_ref, i), parts, block_grad
    )
    copy_out = pltpu.make_async_copy(cross, cross_any, sems.at[1])
    copy_out.start()
    run_chunks(width, lambda i: last_chunk(store_to(1), work_grad, twiddle_ref, i))
    copy_out.wait()


def filter_grad_kernel(
    both_ref,
    cross_ref,
    table_ref,
    twiddle_ref,
    decay_ref,
    filter_ref,
    hidden_ref,
    w_ref,
    cosine_ref,
    positional_ref,
    small_ref,
    first_ref,
    work,
    raw,
    sums,
    split,
):
    parts, height = work.shape[0], work.shape[2] // 2
    width, length = raw.shape
    hidden_count = hidden_ref.shape[0]
    band_total = positional_ref.shape[0]
    scale = length**-0.5
    split_table(table_ref, split)

    def block(r):
        work[r] = transform(cross_ref[r], split, 1)

    def store(p, row, value):
        rows, columns = pl.ds(row, 16), columns_of(p, height)
        envelope, fraction = envelope_at(decay_ref[rows, :], p * height, length, height)
        decay_part = value * filter_ref[rows, columns] * fraction
        left = both_ref[p, 0, rows, :].astype(jnp.float32)
        right = both_ref[p, 1, rows, :].astype(jnp.float32)
        skip_part = left * right
        raw[rows, columns] = value * envelope * scale
        if p > 0:
            decay_part = decay_part + sums[0, rows, :]
            skip_part = skip_part + sums[1, rows, :]
        sums[0, rows, :] = decay_part
        sums[1, rows, :] = skip_part

    run_blocks(parts, block)
    run_chunks(width, lambda i: last_chunk(store, work, twiddle_ref, i))

    def contract_last(left, right):
        return lax.dot_general(
            left,
            right,
            (((1,), (1,)), ((), ())),
            precision=HIGH,
            preferred_element_type=jnp.float32,
        )

    second = jnp.zeros((hidden_count, width), jnp.float32)
    first = jnp.zeros((band_total, hidden_count), jnp.float32)
    chunk = min(length, 512)
    for at in range(0, length, chunk):
        columns = slice(at, at + chunk)
        grad_raw = raw[:, columns]
        second += contract_last(hidden_ref[:, columns], grad_raw)
        hidden_part = jnp.dot(
            w_ref[...], grad_raw, precision=HIGH, preferred_element_type=jnp.float32
        )
        first += contract_last(positional_ref[:, columns], hidden_part * cosine_ref[:, columns])

    first_ref[:band_total, :], first_ref[band_total:, :] = split_bf16(first * scale)
    small_ref[:hidden_count, :] = (second * scale).astype(jnp.bfloat16)
    place = lax.broadcasted_iota(jnp.int32, (16, width), 0)
    tail = jnp.zeros((16, width), jnp.float32)
    decay_pair = split_bf16(jnp.sum(sums[0].T, axis=0, keepdims=True) * -scale)
    skip_pair = split_bf16(jnp.sum(sums[1].T, axis=0, keepdims=True) * scale)
    for at, row in enumerate(decay_pair + skip_pair):
        tail = jnp.where(place == at, row.astype(jnp.float32), tail)
    small_ref[hidden_count:, :] = tail.astype(jnp.bfloat16)


def params():
    return pltpu.CompilerParams(vmem_limit_bytes=56 * MIB)


def estimate(flops, nbytes):
    return pl.CostEstimate(flops=flops, bytes_accessed=nbytes, transcendentals=0)


def gate_kernel(*refs):
    out_ref = refs[-1]
    width = out_ref.shape[2]
    for at in range(out_ref.shape[0]):
        lanes = slice(at * width, (at + 1) * width)
        for which in range(2):
            left = refs[2 * which][:, lanes].astype(jnp.float32)
            right = refs[2 * which + 1][:, lanes].astype(jnp.float32)
            out_ref[at, which] = (left * right).T.astype(jnp.bfloat16)


def gate(factors, count):
    rows, columns = factors[0].shape
    width = columns // count
    if width % 128 != 0:
        pairs = []
        for left, right in (factors[:2], factors[2:]):
            product = (left.astype(jnp.float32) * right.astype(jnp.float32)).astype(jnp.bfloat16)
            pairs.append(product.reshape(rows, count, width).transpose(1, 2, 0))
        return jnp.stack(pairs, axis=1)
    group = math.gcd(count, 4)
    return pl.pallas_call(
        gate_kernel,
        grid=(count // group,),
        in_specs=[pl.BlockSpec((rows, group * width), lambda i: (0, i))] * 4,
        out_specs=pl.BlockSpec((group, 2, width, rows), lambda i: (i, 0, 0, 0)),
        out_shape=jax.ShapeDtypeStruct((count, 2, width, rows), jnp.bfloat16),
        compiler_params=params(),
        cost_estimate=estimate(2 * rows * columns, rows * columns * 12),
    )(*factors)


def ungate_kernel(back_ref, g_ref, v_ref, k_ref, q_out, k_out, v_out):
    width = back_ref.shape[2]
    for at in range(back_ref.shape[0]):
        lanes = slice(at * width, (at + 1) * width)
        conv = back_ref[at, 0].astype(jnp.float32).T
        grad = back_ref[at, 1].astype(jnp.float32).T
        for back, factor_ref, out_ref in (
            (conv, g_ref, q_out),
            (grad, v_ref, k_out),
            (grad, k_ref, v_out),
        ):
            factor = factor_ref[:, lanes].astype(jnp.float32)
            out_ref[:, lanes] = (back * factor).astype(jnp.bfloat16)


def ungate(back, factors):
    count, _, width, rows = back.shape
    columns = count * width
    if width % 128 != 0:
        outs = []
        for which, factor in zip((0, 1, 1), factors):
            part = back[:, which].transpose(2, 0, 1).reshape(rows, columns).astype(jnp.float32)
            outs.append((part * factor.astype(jnp.float32)).astype(jnp.bfloat16))
        return outs
    group = math.gcd(count, 4)
    wide = pl.BlockSpec((rows, group * width), lambda i: (0, i))
    return pl.pallas_call(
        ungate_kernel,
        grid=(count // group,),
        in_specs=[pl.BlockSpec((group, 2, width, rows), lambda i: (i, 0, 0, 0))] + [wide] * 3,
        out_specs=[wide] * 3,
        out_shape=[jax.ShapeDtypeStruct((rows, columns), jnp.bfloat16)] * 3,
        compiler_params=params(),
        cost_estimate=estimate(3 * rows * columns, rows * columns * 16),
    )(back, *factors)


def per_device(q_proj, k_proj, v_proj, grad_out, w_first, w_second, decay_rate, skip_gain):
    height, chan_tp = q_proj.shape
    parts = lax.axis_size("seq")
    length = height * parts
    width = chan_tp // parts
    band_total, hidden_count = w_first.shape
    seq_index = lax.axis_index("seq")

    def exchange(values):
        return lax.all_to_all(values, "seq", split_axis=0, concat_axis=0, tiled=True)

    both = exchange(gate((k_proj, v_proj, grad_out, q_proj), parts))

    tables = jnp.asarray(transform_tables(length, height))
    twiddle = jnp.asarray(twiddle_table(length, height))
    positional = positional_table(length, band_total // 2)
    sine_input = jnp.dot(
        w_first.T, positional, precision=HIGH, preferred_element_type=jnp.float32
    )
    hidden = jnp.sin(sine_input)
    cosine = jnp.cos(sine_input)
    offset = seq_index * width
    w_mine = lax.dynamic_slice_in_dim(w_second, offset, width, 1)
    decay_mine = lax.dynamic_slice_in_dim(decay_rate, offset, width, 0)[:, None]
    skip_mine = lax.dynamic_slice_in_dim(skip_gain, offset, width, 0)[:, None]

    spectrum_shape = jax.ShapeDtypeStruct((parts, width, 2 * height), jnp.float32)
    work = pltpu.VMEM(spectrum_shape.shape, jnp.float32)
    split = pltpu.VMEM((2, 6 * height, 2 * height), jnp.bfloat16)
    anywhere = pl.BlockSpec(memory_space=pl.ANY)
    in_vmem = pl.BlockSpec(memory_space=pltpu.VMEM)
    product_flops = 2 * 3 * parts * 4 * height * height * width

    long_filter, filter_spectrum = pl.pallas_call(
        filter_kernel,
        in_specs=[in_vmem] * 5,
        out_specs=[in_vmem, in_vmem],
        out_shape=[jax.ShapeDtypeStruct((width, length), jnp.float32), spectrum_shape],
        scratch_shapes=[work, split],
        compiler_params=params(),
        cost_estimate=estimate(product_flops, length * width * 12),
    )(w_mine.T, hidden, decay_mine, tables, twiddle)

    back, cross = pl.pallas_call(
        main_kernel,
        in_specs=[in_vmem, anywhere, in_vmem, in_vmem, in_vmem],
        out_specs=[in_vmem, anywhere],
        out_shape=[jax.ShapeDtypeStruct(both.shape, jnp.bfloat16), spectrum_shape],
        scratch_shapes=[work, work, work, work, split, pltpu.SemaphoreType.DMA((2,))],
        compiler_params=params(),
        cost_estimate=estimate(4 * product_flops, length * width * 32),
    )(both, filter_spectrum, tables, twiddle, skip_mine)
    back = exchange(back)

    small, first_pair = pl.pallas_call(
        filter_grad_kernel,
        in_specs=[in_vmem] * 10,
        out_specs=[in_vmem, in_vmem],
        out_shape=[
            jax.ShapeDtypeStruct((hidden_count + 16, width), jnp.bfloat16),
            jax.ShapeDtypeStruct((2 * band_total, hidden_count), jnp.bfloat16),
        ],
        scratch_shapes=[
            work,
            pltpu.VMEM((width, length), jnp.float32),
            pltpu.VMEM((2, width, height), jnp.float32),
            split,
        ],
        compiler_params=params(),
        cost_estimate=estimate(2 * product_flops, length * width * 30),
    )(
        both,
        cross,
        tables,
        twiddle,
        decay_mine,
        long_filter,
        hidden,
        w_mine,
        cosine,
        positional,
    )
    packed = jnp.concatenate([small, first_pair.reshape(-1, width)], axis=0)
    gathered = lax.all_gather(packed, "seq", axis=1, tiled=True)
    grad_second = gathered[:hidden_count].astype(jnp.float32)
    tail = gathered[hidden_count : hidden_count + 4].astype(jnp.float32)
    grad_decay = tail[0] + tail[1]
    grad_skip = tail[2] + tail[3]
    first_rows = gathered[hidden_count + 16 :].astype(jnp.float32)
    first_rows = first_rows.reshape(-1, parts, width).sum(axis=1)
    grad_first = first_rows.reshape(2, band_total, hidden_count).sum(axis=0)
    if lax.axis_size("tp") == 2:
        grad_first = grad_first + lax.ppermute(grad_first, "tp", [(0, 1), (1, 0)])
    else:
        grad_first = lax.psum(grad_first, "tp")
    grad_q, grad_k, grad_v = ungate(back, (grad_out, v_proj, k_proj))
    return (grad_q, grad_k, grad_v, grad_first, grad_second, grad_decay, grad_skip)


def solution(mesh):
    return jax.shard_map(
        per_device,
        mesh=mesh,
        in_specs=(
            P("seq", "tp"),
            P("seq", "tp"),
            P("seq", "tp"),
            P("seq", "tp"),
            P(),
            P(None, "tp"),
            P("tp"),
            P("tp"),
        ),
        out_specs=(
            P("seq", "tp"),
            P("seq", "tp"),
            P("seq", "tp"),
            P(),
            P(None, "tp"),
            P("tp"),
            P("tp"),
        ),
        check_vma=False,
    )
```

```python
import functools
import math

import jax
import jax.numpy as jnp
import ml_dtypes
import numpy as np
from jax import lax
from jax.experimental import pallas as pl
from jax.experimental.pallas import tpu as pltpu
from jax.sharding import PartitionSpec as P

HIGH = lax.Precision.HIGHEST
MIB = 1024 * 1024


def positional_table(length, band_count):
    positions = jnp.arange(length, dtype=jnp.int32)
    band_index = jnp.arange(band_count, dtype=jnp.int32)
    frequency = 3 * (band_index + 1) * (band_index + 1) + band_index
    phase_index = frequency[:, None] * positions[None, :] % length
    angles = phase_index.astype(jnp.float32) * (2.0 * math.pi / length)
    return jnp.concatenate([jnp.sin(angles), jnp.cos(angles)], axis=0)


@functools.lru_cache(maxsize=None)
def transform_tables(length, height):
    j = np.arange(height)
    angles = (j[:, None] * j[None, :] % height) * (2.0 * np.pi / height)
    cosine, sine = np.cos(angles), np.sin(angles)
    forward = np.concatenate(
        [np.concatenate([cosine, -sine], axis=1), np.concatenate([sine, cosine], axis=1)], axis=0
    )
    return np.stack([forward, forward.T / length]).astype(np.float32)


@functools.lru_cache(maxsize=None)
def twiddle_table(length, height):
    parts = length // height
    r = np.arange(parts)[:, None]
    j = np.arange(height)[None, :]
    angles = (j * (4 * r + 1) % (4 * length)) * (2.0 * np.pi / (4 * length))
    return np.concatenate([np.cos(angles), -np.sin(angles)], axis=1).astype(np.float32)


def turn(value, cosine, sine):
    real, imag = value
    return (real * cosine - imag * sine, real * sine + imag * cosine)


def small_fft(values, sign):
    count = len(values)
    if count == 1:
        return values
    even = small_fft(values[0::2], sign)
    odd = small_fft(values[1::2], sign)
    first, second = [], []
    for k in range(count // 2):
        real, imag = odd[k]
        if k == 0:
            pass
        elif 4 * k == count:
            real, imag = (-imag, real) if sign > 0 else (imag, -real)
        elif 8 * k == count:
            half = math.sqrt(0.5)
            if sign > 0:
                real, imag = (real - imag) * half, (real + imag) * half
            else:
                real, imag = (real + imag) * half, (imag - real) * half
        elif 8 * k == 3 * count:
            half = math.sqrt(0.5)
            if sign > 0:
                real, imag = (real + imag) * -half, (real - imag) * half
            else:
                real, imag = (imag - real) * half, (real + imag) * -half
        else:
            angle = sign * 2.0 * math.pi * k / count
            real, imag = turn((real, imag), math.cos(angle), math.sin(angle))
        base_real, base_imag = even[k]
        first.append((base_real + real, base_imag + imag))
        second.append((base_real - real, base_imag - imag))
    return first + second


def parts_forward(values):
    count = len(values)
    turned = []
    for p, value in enumerate(values):
        angle = 2.0 * math.pi * p / (4 * count)
        turned.append((value * math.cos(angle), value * -math.sin(angle)))
    return small_fft(turned, -1)


def parts_inverse(values):
    count = len(values)
    result = []
    for p, (real, imag) in enumerate(small_fft(values, 1)):
        angle = 2.0 * math.pi * p / (4 * count)
        result.append(real * math.cos(angle) - imag * math.sin(angle))
    return result


def split_bf16(value):
    high = value.astype(jnp.bfloat16)
    return high, (value - high.astype(jnp.float32)).astype(jnp.bfloat16)


def split_table(table_ref, split):
    size = table_ref.shape[1]
    for direction in range(2):
        high, low = split_bf16(table_ref[direction])
        split[direction, :size] = high
        split[direction, size : 2 * size] = high
        split[direction, 2 * size :] = low


def transform(value, split, direction):
    high, low = split_bf16(value)
    return jnp.dot(
        jnp.concatenate([high, low, high], axis=1),
        split[direction],
        preferred_element_type=jnp.float32,
    )


def spectrum_product(left, right, conjugate):
    height = left.shape[1] // 2
    left_real, left_imag = left[:, :height], left[:, height:]
    right_real, right_imag = right[:, :height], right[:, height:]
    if conjugate:
        real = left_real * right_real + left_imag * right_imag
        imag = left_real * right_imag - left_imag * right_real
    else:
        real = left_real * right_real - left_imag * right_imag
        imag = left_real * right_imag + left_imag * right_real
    return jnp.concatenate([real, imag], axis=1)


def first_chunk(load, work, twiddle_ref, index):
    parts, height = work.shape[0], work.shape[2] // 2
    row = pl.multiple_of(index * 16, 16)
    values = [load(p, row) for p in range(parts)]
    for half in (0, 8):
        rows = pl.ds(row + half, 8)
        turned = parts_forward([value[half : half + 8] for value in values])
        for r, value in enumerate(turned):
            cosine = twiddle_ref[r : r + 1, :height]
            sine = twiddle_ref[r : r + 1, height:]
            work[r, rows, :height], work[r, rows, height:] = turn(value, cosine, sine)


def last_chunk(store, work, twiddle_ref, index):
    parts, height = work.shape[0], work.shape[2] // 2
    row = pl.multiple_of(index * 16, 16)
    halves = []
    for half in (0, 8):
        rows = pl.ds(row + half, 8)
        values = []
        for r in range(parts):
            cosine = twiddle_ref[r : r + 1, :height]
            sine = twiddle_ref[r : r + 1, height:]
            value = (work[r, rows, :height], work[r, rows, height:])
            values.append(turn(value, cosine, -sine))
        halves.append(parts_inverse(values))
    for p in range(parts):
        store(p, row, jnp.concatenate([halves[0][p], halves[1][p]], axis=0))


GROUP = 4


def run_chunks(width, chunk, parts=0, block=None):
    chunks = width // 16
    per = math.gcd(chunks, GROUP)
    paired = parts * per == GROUP * chunks

    def one(index, carry):
        if paired:
            block(index * GROUP)
        for b in range(per):
            chunk(index * per + b)
        return carry

    lax.fori_loop(0, chunks // per, one, 0)
    if not paired and parts > 0:
        run_blocks(parts, block)


def run_blocks(parts, block):
    def one(index, carry):
        block(index * GROUP)
        return carry

    lax.fori_loop(0, parts // GROUP, one, 0)


def group_of(r):
    return pl.ds(pl.multiple_of(r, GROUP), GROUP)


def read_group(ref, r):
    _, width, columns = ref.shape
    return ref[group_of(r)].reshape(GROUP * width, columns)


def write_group(ref, r, value):
    ref[group_of(r)] = value.reshape((GROUP,) + ref.shape[1:])


def envelope_at(decay, start, length, height):
    position = (start + lax.broadcasted_iota(jnp.int32, (1, height), 1)).astype(jnp.float32)
    fraction = position * (1.0 / length)
    return jnp.exp(-decay * fraction), fraction


def columns_of(p, height):
    return slice(p * height, (p + 1) * height)


def filter_kernel(
    w_t_ref, hidden_ref, decay_ref, table_ref, twiddle_ref, filter_ref, spectrum_ref, work, split
):
    parts, width, height = work.shape[0], work.shape[1], work.shape[2] // 2
    length = filter_ref.shape[1]
    scale = length**-0.5
    split_table(table_ref, split)
    filter_ref[...] = jnp.dot(
        w_t_ref[...], hidden_ref[...], precision=HIGH, preferred_element_type=jnp.float32
    )

    def load(p, row):
        rows, columns = pl.ds(row, 16), columns_of(p, height)
        envelope, _ = envelope_at(decay_ref[rows, :], p * height, length, height)
        value = filter_ref[rows, columns] * envelope * scale
        filter_ref[rows, columns] = value
        return value

    def block(r):
        write_group(spectrum_ref, r, transform(read_group(work, r), split, 0))

    run_chunks(width, lambda i: first_chunk(load, work, twiddle_ref, i))
    run_blocks(parts, block)


def main_kernel(
    both_ref,
    h_any,
    table_ref,
    twiddle_ref,
    skip_ref,
    back_ref,
    cross_any,
    work_in,
    work_grad,
    cross,
    h,
    split,
    sems,
):
    parts, width = work_in.shape[0], work_in.shape[1]
    copy_in = pltpu.make_async_copy(h_any, h, sems.at[0])
    copy_in.start()
    split_table(table_ref, split)

    def load_from(which):
        def load(p, row):
            return both_ref[p, which, pl.ds(row, 16), :].astype(jnp.float32)

        return load

    def store_to(which):
        load = load_from(which)

        def store(p, row, value):
            value = value + skip_ref[pl.ds(row, 16), :] * load(p, row)
            back_ref[p, which, pl.ds(row, 16), :] = value.astype(jnp.bfloat16)

        return store

    def block_in(r):
        spectrum = transform(read_group(work_in, r), split, 0)
        write_group(cross, r, spectrum)
        product = spectrum_product(read_group(h, r), spectrum, False)
        write_group(work_in, r, transform(product, split, 1))

    def block_grad(r):
        spectrum = transform(read_group(work_grad, r), split, 0)
        write_group(cross, r, spectrum_product(read_group(cross, r), spectrum, True))
        product = spectrum_product(read_group(h, r), spectrum, True)
        write_group(work_grad, r, transform(product, split, 1))

    run_chunks(width, lambda i: first_chunk(load_from(0), work_in, twiddle_ref, i))
    copy_in.wait()
    run_chunks(
        width, lambda i: first_chunk(load_from(1), work_grad, twiddle_ref, i), parts, block_in
    )
    run_chunks(
        width, lambda i: last_chunk(store_to(0), work_in, twiddle_ref, i), parts, block_grad
    )
    copy_out = pltpu.make_async_copy(cross, cross_any, sems.at[1])
    copy_out.start()
    run_chunks(width, lambda i: last_chunk(store_to(1), work_grad, twiddle_ref, i))
    copy_out.wait()


def filter_grad_kernel(
    both_ref,
    cross_ref,
    table_ref,
    twiddle_ref,
    decay_ref,
    filter_ref,
    hidden_ref,
    w_ref,
    cosine_ref,
    positional_ref,
    small_ref,
    first_ref,
    work,
    raw,
    sums,
    split,
):
    parts, height = work.shape[0], work.shape[2] // 2
    width, length = raw.shape
    hidden_count = hidden_ref.shape[0]
    band_total = positional_ref.shape[0]
    scale = length**-0.5
    split_table(table_ref, split)

    def block(r):
        write_group(work, r, transform(read_group(cross_ref, r), split, 1))

    def store(p, row, value):
        rows, columns = pl.ds(row, 16), columns_of(p, height)
        envelope, fraction = envelope_at(decay_ref[rows, :], p * height, length, height)
        decay_part = value * filter_ref[rows, columns] * fraction
        left = both_ref[p, 0, rows, :].astype(jnp.float32)
        right = both_ref[p, 1, rows, :].astype(jnp.float32)
        skip_part = left * right
        raw[rows, columns] = value * envelope * scale
        if p > 0:
            decay_part = decay_part + sums[0, rows, :]
            skip_part = skip_part + sums[1, rows, :]
        sums[0, rows, :] = decay_part
        sums[1, rows, :] = skip_part

    run_blocks(parts, block)
    run_chunks(width, lambda i: last_chunk(store, work, twiddle_ref, i))

    def contract_last(left, right):
        return lax.dot_general(
            left,
            right,
            (((1,), (1,)), ((), ())),
            precision=HIGH,
            preferred_element_type=jnp.float32,
        )

    second = jnp.zeros((hidden_count, width), jnp.float32)
    first = jnp.zeros((band_total, hidden_count), jnp.float32)
    chunk = min(length, 512)
    for at in range(0, length, chunk):
        columns = slice(at, at + chunk)
        grad_raw = raw[:, columns]
        second += contract_last(hidden_ref[:, columns], grad_raw)
        hidden_part = jnp.dot(
            w_ref[...], grad_raw, precision=HIGH, preferred_element_type=jnp.float32
        )
        first += contract_last(positional_ref[:, columns], hidden_part * cosine_ref[:, columns])

    first_ref[:band_total, :], first_ref[band_total:, :] = split_bf16(first * scale)
    small_ref[:hidden_count, :] = (second * scale).astype(jnp.bfloat16)
    place = lax.broadcasted_iota(jnp.int32, (16, width), 0)
    tail = jnp.zeros((16, width), jnp.float32)
    decay_pair = split_bf16(jnp.sum(sums[0].T, axis=0, keepdims=True) * -scale)
    skip_pair = split_bf16(jnp.sum(sums[1].T, axis=0, keepdims=True) * scale)
    for at, row in enumerate(decay_pair + skip_pair):
        tail = jnp.where(place == at, row.astype(jnp.float32), tail)
    small_ref[hidden_count:, :] = tail.astype(jnp.bfloat16)


def params():
    return pltpu.CompilerParams(vmem_limit_bytes=56 * MIB)


def estimate(flops, nbytes):
    return pl.CostEstimate(flops=flops, bytes_accessed=nbytes, transcendentals=0)


def gate_kernel(*refs):
    out_ref = refs[-1]
    width = out_ref.shape[2]
    for at in range(out_ref.shape[0]):
        lanes = slice(at * width, (at + 1) * width)
        for which in range(2):
            left = refs[2 * which][:, lanes].astype(jnp.float32)
            right = refs[2 * which + 1][:, lanes].astype(jnp.float32)
            out_ref[at, which] = (left * right).T.astype(jnp.bfloat16)


def gate(factors, count):
    rows, columns = factors[0].shape
    width = columns // count
    if width % 128 != 0:
        pairs = []
        for left, right in (factors[:2], factors[2:]):
            product = (left.astype(jnp.float32) * right.astype(jnp.float32)).astype(jnp.bfloat16)
            pairs.append(product.reshape(rows, count, width).transpose(1, 2, 0))
        return jnp.stack(pairs, axis=1)
    group = math.gcd(count, 4)
    return pl.pallas_call(
        gate_kernel,
        grid=(count // group,),
        in_specs=[pl.BlockSpec((rows, group * width), lambda i: (0, i))] * 4,
        out_specs=pl.BlockSpec((group, 2, width, rows), lambda i: (i, 0, 0, 0)),
        out_shape=jax.ShapeDtypeStruct((count, 2, width, rows), jnp.bfloat16),
        compiler_params=params(),
        cost_estimate=estimate(2 * rows * columns, rows * columns * 12),
    )(*factors)


def ungate_kernel(back_ref, g_ref, v_ref, k_ref, q_out, k_out, v_out):
    width = back_ref.shape[2]
    for at in range(back_ref.shape[0]):
        lanes = slice(at * width, (at + 1) * width)
        conv = back_ref[at, 0].astype(jnp.float32).T
        grad = back_ref[at, 1].astype(jnp.float32).T
        for back, factor_ref, out_ref in (
            (conv, g_ref, q_out),
            (grad, v_ref, k_out),
            (grad, k_ref, v_out),
        ):
            factor = factor_ref[:, lanes].astype(jnp.float32)
            out_ref[:, lanes] = (back * factor).astype(jnp.bfloat16)


def ungate(back, factors):
    count, _, width, rows = back.shape
    columns = count * width
    if width % 128 != 0:
        outs = []
        for which, factor in zip((0, 1, 1), factors):
            part = back[:, which].transpose(2, 0, 1).reshape(rows, columns).astype(jnp.float32)
            outs.append((part * factor.astype(jnp.float32)).astype(jnp.bfloat16))
        return outs
    group = math.gcd(count, 4)
    wide = pl.BlockSpec((rows, group * width), lambda i: (0, i))
    return pl.pallas_call(
        ungate_kernel,
        grid=(count // group,),
        in_specs=[pl.BlockSpec((group, 2, width, rows), lambda i: (i, 0, 0, 0))] + [wide] * 3,
        out_specs=[wide] * 3,
        out_shape=[jax.ShapeDtypeStruct((rows, columns), jnp.bfloat16)] * 3,
        compiler_params=params(),
        cost_estimate=estimate(3 * rows * columns, rows * columns * 16),
    )(back, *factors)


def gather_all(block, count, index):
    held = block[None]
    bit = count // 2
    while bit > 0:
        pairs = [(i, i ^ bit) for i in range(count)]
        other = lax.ppermute(held, "seq", pairs)
        upper = (index // bit) % 2 == 1
        both = jnp.stack([jnp.where(upper, other, held), jnp.where(upper, held, other)], axis=1)
        held = both.reshape((2 * held.shape[0],) + block.shape)
        bit //= 2
    return held


def per_device(q_proj, k_proj, v_proj, grad_out, w_first, w_second, decay_rate, skip_gain):
    height, chan_tp = q_proj.shape
    parts = lax.axis_size("seq")
    length = height * parts
    width = chan_tp // parts
    band_total, hidden_count = w_first.shape
    seq_index = lax.axis_index("seq")

    def exchange(values):
        return lax.all_to_all(values, "seq", split_axis=0, concat_axis=0, tiled=True)

    both = exchange(gate((k_proj, v_proj, grad_out, q_proj), parts))

    tables = jnp.asarray(transform_tables(length, height))
    twiddle = jnp.asarray(twiddle_table(length, height))
    positional = positional_table(length, band_total // 2)
    sine_input = jnp.dot(
        w_first.T, positional, precision=HIGH, preferred_element_type=jnp.float32
    )
    hidden = jnp.sin(sine_input)
    cosine = jnp.cos(sine_input)
    offset = seq_index * width
    w_mine = lax.dynamic_slice_in_dim(w_second, offset, width, 1)
    decay_mine = lax.dynamic_slice_in_dim(decay_rate, offset, width, 0)[:, None]
    skip_mine = lax.dynamic_slice_in_dim(skip_gain, offset, width, 0)[:, None]

    spectrum_shape = jax.ShapeDtypeStruct((parts, width, 2 * height), jnp.float32)
    work = pltpu.VMEM(spectrum_shape.shape, jnp.float32)
    split = pltpu.VMEM((2, 6 * height, 2 * height), jnp.bfloat16)
    anywhere = pl.BlockSpec(memory_space=pl.ANY)
    in_vmem = pl.BlockSpec(memory_space=pltpu.VMEM)
    product_flops = 2 * 3 * parts * 4 * height * height * width

    long_filter, filter_spectrum = pl.pallas_call(
        filter_kernel,
        in_specs=[in_vmem] * 5,
        out_specs=[in_vmem, in_vmem],
        out_shape=[jax.ShapeDtypeStruct((width, length), jnp.float32), spectrum_shape],
        scratch_shapes=[work, split],
        compiler_params=params(),
        cost_estimate=estimate(1000, 1000),
    )(w_mine.T, hidden, decay_mine, tables, twiddle)

    back, cross = pl.pallas_call(
        main_kernel,
        in_specs=[in_vmem, anywhere, in_vmem, in_vmem, in_vmem],
        out_specs=[in_vmem, anywhere],
        out_shape=[jax.ShapeDtypeStruct(both.shape, jnp.bfloat16), spectrum_shape],
        scratch_shapes=[work, work, work, work, split, pltpu.SemaphoreType.DMA((2,))],
        compiler_params=params(),
        cost_estimate=estimate(4 * product_flops, length * width * 32),
    )(both, filter_spectrum, tables, twiddle, skip_mine)
    back = exchange(back)

    small, first_pair = pl.pallas_call(
        filter_grad_kernel,
        in_specs=[in_vmem] * 10,
        out_specs=[in_vmem, in_vmem],
        out_shape=[
            jax.ShapeDtypeStruct((hidden_count + 16, width), jnp.bfloat16),
            jax.ShapeDtypeStruct((2 * band_total, hidden_count), jnp.bfloat16),
        ],
        scratch_shapes=[
            work,
            pltpu.VMEM((width, length), jnp.float32),
            pltpu.VMEM((2, width, height), jnp.float32),
            split,
        ],
        compiler_params=params(),
        cost_estimate=estimate(1000, 1000),
    )(
        both,
        cross,
        tables,
        twiddle,
        decay_mine,
        long_filter,
        hidden,
        w_mine,
        cosine,
        positional,
    )
    packed = jnp.concatenate([small, first_pair.reshape(-1, width)], axis=0)
    gathered = gather_all(packed, parts, seq_index)
    second = gathered[:, :hidden_count].astype(jnp.float32)
    grad_second = second.transpose(1, 0, 2).reshape(hidden_count, chan_tp)
    tail = gathered[:, hidden_count : hidden_count + 4].astype(jnp.float32)
    grad_decay = (tail[:, 0] + tail[:, 1]).reshape(chan_tp)
    grad_skip = (tail[:, 2] + tail[:, 3]).reshape(chan_tp)
    first_rows = gathered[:, hidden_count + 16 :].astype(jnp.float32).sum(axis=0)
    grad_first = first_rows.reshape(2, band_total, hidden_count).sum(axis=0)
    if lax.axis_size("tp") == 2:
        grad_first = grad_first + lax.ppermute(grad_first, "tp", [(0, 1), (1, 0)])
    else:
        grad_first = lax.psum(grad_first, "tp")
    grad_q, grad_k, grad_v = ungate(back, (grad_out, v_proj, k_proj))
    return (grad_q, grad_k, grad_v, grad_first, grad_second, grad_decay, grad_skip)


def solution(mesh):
    return jax.shard_map(
        per_device,
        mesh=mesh,
        in_specs=(
            P("seq", "tp"),
            P("seq", "tp"),
            P("seq", "tp"),
            P("seq", "tp"),
            P(),
            P(None, "tp"),
            P("tp"),
            P("tp"),
        ),
        out_specs=(
            P("seq", "tp"),
            P("seq", "tp"),
            P("seq", "tp"),
            P(),
            P(None, "tp"),
            P("tp"),
            P("tp"),
        ),
        check_vma=False,
    )
```

```python
import functools
import math

import jax
import jax.numpy as jnp
import ml_dtypes
import numpy as np
from jax import lax
from jax.experimental import pallas as pl
from jax.experimental.pallas import tpu as pltpu
from jax.sharding import PartitionSpec as P

HIGH = lax.Precision.HIGHEST
MIB = 1024 * 1024


def positional_table(length, band_count):
    positions = jnp.arange(length, dtype=jnp.int32)
    band_index = jnp.arange(band_count, dtype=jnp.int32)
    frequency = 3 * (band_index + 1) * (band_index + 1) + band_index
    phase_index = frequency[:, None] * positions[None, :] % length
    angles = phase_index.astype(jnp.float32) * (2.0 * math.pi / length)
    return jnp.concatenate([jnp.sin(angles), jnp.cos(angles)], axis=0)


@functools.lru_cache(maxsize=None)
def transform_tables(length, height):
    j = np.arange(height)
    angles = (j[:, None] * j[None, :] % height) * (2.0 * np.pi / height)
    cosine, sine = np.cos(angles), np.sin(angles)
    forward = np.concatenate(
        [np.concatenate([cosine, -sine], axis=1), np.concatenate([sine, cosine], axis=1)], axis=0
    )
    return np.stack([forward, forward.T / length]).astype(np.float32)


@functools.lru_cache(maxsize=None)
def twiddle_table(length, height):
    parts = length // height
    r = np.arange(parts)[:, None]
    j = np.arange(height)[None, :]
    angles = (j * (4 * r + 1) % (4 * length)) * (2.0 * np.pi / (4 * length))
    return np.concatenate([np.cos(angles), -np.sin(angles)], axis=1).astype(np.float32)


def turn(value, cosine, sine):
    real, imag = value
    return (real * cosine - imag * sine, real * sine + imag * cosine)


def small_fft(values, sign):
    count = len(values)
    if count == 1:
        return values
    even = small_fft(values[0::2], sign)
    odd = small_fft(values[1::2], sign)
    first, second = [], []
    for k in range(count // 2):
        real, imag = odd[k]
        if k == 0:
            pass
        elif 4 * k == count:
            real, imag = (-imag, real) if sign > 0 else (imag, -real)
        elif 8 * k == count:
            half = math.sqrt(0.5)
            if sign > 0:
                real, imag = (real - imag) * half, (real + imag) * half
            else:
                real, imag = (real + imag) * half, (imag - real) * half
        elif 8 * k == 3 * count:
            half = math.sqrt(0.5)
            if sign > 0:
                real, imag = (real + imag) * -half, (real - imag) * half
            else:
                real, imag = (imag - real) * half, (real + imag) * -half
        else:
            angle = sign * 2.0 * math.pi * k / count
            real, imag = turn((real, imag), math.cos(angle), math.sin(angle))
        base_real, base_imag = even[k]
        first.append((base_real + real, base_imag + imag))
        second.append((base_real - real, base_imag - imag))
    return first + second


def parts_forward(values):
    count = len(values)
    turned = []
    for p, value in enumerate(values):
        angle = 2.0 * math.pi * p / (4 * count)
        turned.append((value * math.cos(angle), value * -math.sin(angle)))
    return small_fft(turned, -1)


def parts_inverse(values):
    count = len(values)
    result = []
    for p, (real, imag) in enumerate(small_fft(values, 1)):
        angle = 2.0 * math.pi * p / (4 * count)
        result.append(real * math.cos(angle) - imag * math.sin(angle))
    return result


def split_bf16(value):
    high = value.astype(jnp.bfloat16)
    return high, (value - high.astype(jnp.float32)).astype(jnp.bfloat16)


def split_table(table_ref, split):
    size = table_ref.shape[1]
    for direction in range(2):
        high, low = split_bf16(table_ref[direction])
        split[direction, :size] = high
        split[direction, size : 2 * size] = high
        split[direction, 2 * size :] = low


def transform(value, split, direction):
    high, low = split_bf16(value)
    return jnp.dot(
        jnp.concatenate([high, low, high], axis=1),
        split[direction],
        preferred_element_type=jnp.float32,
    )


def spectrum_product(left, right, conjugate):
    height = left.shape[1] // 2
    left_real, left_imag = left[:, :height], left[:, height:]
    right_real, right_imag = right[:, :height], right[:, height:]
    if conjugate:
        real = left_real * right_real + left_imag * right_imag
        imag = left_real * right_imag - left_imag * right_real
    else:
        real = left_real * right_real - left_imag * right_imag
        imag = left_real * right_imag + left_imag * right_real
    return jnp.concatenate([real, imag], axis=1)


def first_chunk(load, work, twiddle_ref, index):
    parts, height = work.shape[0], work.shape[2] // 2
    row = pl.multiple_of(index * 16, 16)
    values = [load(p, row) for p in range(parts)]
    for half in (0, 8):
        rows = pl.ds(row + half, 8)
        turned = parts_forward([value[half : half + 8] for value in values])
        for r, value in enumerate(turned):
            cosine = twiddle_ref[r : r + 1, :height]
            sine = twiddle_ref[r : r + 1, height:]
            work[r, rows, :height], work[r, rows, height:] = turn(value, cosine, sine)


def last_chunk(store, work, twiddle_ref, index):
    parts, height = work.shape[0], work.shape[2] // 2
    row = pl.multiple_of(index * 16, 16)
    halves = []
    for half in (0, 8):
        rows = pl.ds(row + half, 8)
        values = []
        for r in range(parts):
            cosine = twiddle_ref[r : r + 1, :height]
            sine = twiddle_ref[r : r + 1, height:]
            value = (work[r, rows, :height], work[r, rows, height:])
            values.append(turn(value, cosine, -sine))
        halves.append(parts_inverse(values))
    for p in range(parts):
        store(p, row, jnp.concatenate([halves[0][p], halves[1][p]], axis=0))


GROUP = 4


def run_chunks(width, chunk, parts=0, block=None):
    chunks = width // 16
    per = math.gcd(chunks, GROUP)
    paired = parts * per == GROUP * chunks

    def one(index, carry):
        if paired:
            block(index * GROUP)
        for b in range(per):
            chunk(index * per + b)
        return carry

    lax.fori_loop(0, chunks // per, one, 0)
    if not paired and parts > 0:
        run_blocks(parts, block)


def run_blocks(parts, block):
    def one(index, carry):
        block(index * GROUP)
        return carry

    lax.fori_loop(0, parts // GROUP, one, 0)


def group_of(r):
    return pl.ds(pl.multiple_of(r, GROUP), GROUP)


def read_group(ref, r):
    _, width, columns = ref.shape
    return ref[group_of(r)].reshape(GROUP * width, columns)


def write_group(ref, r, value):
    ref[group_of(r)] = value.reshape((GROUP,) + ref.shape[1:])


def envelope_at(decay, start, length, height):
    position = (start + lax.broadcasted_iota(jnp.int32, (1, height), 1)).astype(jnp.float32)
    fraction = position * (1.0 / length)
    return jnp.exp(-decay * fraction), fraction


def columns_of(p, height):
    return slice(p * height, (p + 1) * height)


def filter_kernel(
    w_t_ref, hidden_ref, decay_ref, table_ref, twiddle_ref, filter_ref, spectrum_ref, work, split
):
    parts, width, height = work.shape[0], work.shape[1], work.shape[2] // 2
    length = filter_ref.shape[1]
    scale = length**-0.5
    split_table(table_ref, split)
    filter_ref[...] = jnp.dot(
        w_t_ref[...], hidden_ref[...], precision=HIGH, preferred_element_type=jnp.float32
    )

    def load(p, row):
        rows, columns = pl.ds(row, 16), columns_of(p, height)
        envelope, _ = envelope_at(decay_ref[rows, :], p * height, length, height)
        value = filter_ref[rows, columns] * envelope * scale
        filter_ref[rows, columns] = value
        return value

    def block(r):
        write_group(spectrum_ref, r, transform(read_group(work, r), split, 0))

    run_chunks(width, lambda i: first_chunk(load, work, twiddle_ref, i))
    run_blocks(parts, block)


def load_from(ref):
    def load(p, row):
        return ref[p, pl.ds(row, 16), :].astype(jnp.float32)

    return load


def store_to(ref, skip_ref, load):
    def store(p, row, value):
        value = value + skip_ref[pl.ds(row, 16), :] * load(p, row)
        ref[p, pl.ds(row, 16), :] = value.astype(jnp.bfloat16)

    return store


def conv_kernel(
    x_ref, h_any, table_ref, twiddle_ref, skip_ref, y_ref, x_any, work, spectra, h, split, sems
):
    parts, width = work.shape[0], work.shape[1]
    copy_in = pltpu.make_async_copy(h_any, h, sems.at[0])
    copy_in.start()
    split_table(table_ref, split)
    load = load_from(x_ref)

    def block(r):
        spectrum = transform(read_group(work, r), split, 0)
        write_group(spectra, r, spectrum)
        product = spectrum_product(read_group(h, r), spectrum, False)
        write_group(work, r, transform(product, split, 1))

    run_chunks(width, lambda i: first_chunk(load, work, twiddle_ref, i))
    copy_in.wait()
    run_blocks(parts, block)
    copy_out = pltpu.make_async_copy(spectra, x_any, sems.at[1])
    copy_out.start()
    store = store_to(y_ref, skip_ref, load)
    run_chunks(width, lambda i: last_chunk(store, work, twiddle_ref, i))
    copy_out.wait()


def corr_kernel(
    g_ref, spectra_any, h_any, table_ref, twiddle_ref, skip_ref, z_ref, work, spectra, h, split, sems
):
    parts, width = work.shape[0], work.shape[1]
    copy_h = pltpu.make_async_copy(h_any, h, sems.at[0])
    copy_h.start()
    copy_in = pltpu.make_async_copy(spectra_any, spectra, sems.at[1])
    copy_in.start()
    split_table(table_ref, split)

    def block(r):
        product = spectrum_product(read_group(h, r), read_group(spectra, r), True)
        write_group(work, r, transform(product, split, 1))

    copy_h.wait()
    copy_in.wait()
    run_blocks(parts, block)
    store = store_to(z_ref, skip_ref, load_from(g_ref))
    run_chunks(width, lambda i: last_chunk(store, work, twiddle_ref, i))


def filter_grad_kernel(
    x_ref,
    g_ref,
    x_any,
    table_ref,
    twiddle_ref,
    decay_ref,
    filter_ref,
    hidden_ref,
    w_ref,
    cosine_ref,
    positional_ref,
    small_ref,
    first_ref,
    g_any,
    work,
    x_spectra,
    g_spectra,
    raw,
    sums,
    split,
    sems,
):
    parts, height = work.shape[0], work.shape[2] // 2
    width, length = raw.shape
    hidden_count = hidden_ref.shape[0]
    band_total = positional_ref.shape[0]
    scale = length**-0.5
    copy_in = pltpu.make_async_copy(x_any, x_spectra, sems.at[0])
    copy_in.start()
    split_table(table_ref, split)

    def block(r):
        spectrum = transform(read_group(work, r), split, 0)
        write_group(g_spectra, r, spectrum)
        product = spectrum_product(read_group(x_spectra, r), spectrum, True)
        write_group(work, r, transform(product, split, 1))

    def store(p, row, value):
        rows, columns = pl.ds(row, 16), columns_of(p, height)
        envelope, fraction = envelope_at(decay_ref[rows, :], p * height, length, height)
        decay_part = value * filter_ref[rows, columns] * fraction
        skip_part = load_from(x_ref)(p, row) * load_from(g_ref)(p, row)
        raw[rows, columns] = value * envelope * scale
        if p > 0:
            decay_part = decay_part + sums[0, rows, :]
            skip_part = skip_part + sums[1, rows, :]
        sums[0, rows, :] = decay_part
        sums[1, rows, :] = skip_part

    run_chunks(width, lambda i: first_chunk(load_from(g_ref), work, twiddle_ref, i))
    copy_in.wait()
    run_blocks(parts, block)
    copy_out = pltpu.make_async_copy(g_spectra, g_any, sems.at[1])
    copy_out.start()
    run_chunks(width, lambda i: last_chunk(store, work, twiddle_ref, i))

    def contract_last(left, right):
        return lax.dot_general(
            left,
            right,
            (((1,), (1,)), ((), ())),
            precision=HIGH,
            preferred_element_type=jnp.float32,
        )

    second = jnp.zeros((hidden_count, width), jnp.float32)
    first = jnp.zeros((band_total, hidden_count), jnp.float32)
    chunk = min(length, 512)
    for at in range(0, length, chunk):
        columns = slice(at, at + chunk)
        grad_raw = raw[:, columns]
        second += contract_last(hidden_ref[:, columns], grad_raw)
        hidden_part = jnp.dot(
            w_ref[...], grad_raw, precision=HIGH, preferred_element_type=jnp.float32
        )
        first += contract_last(positional_ref[:, columns], hidden_part * cosine_ref[:, columns])

    first_ref[...] = first * scale
    small_ref[:hidden_count, :] = second * scale
    place = lax.broadcasted_iota(jnp.int32, (8, width), 0)
    decay_row = jnp.sum(sums[0].T, axis=0, keepdims=True) * -scale
    skip_row = jnp.sum(sums[1].T, axis=0, keepdims=True) * scale
    tail = jnp.where(place == 1, skip_row, 0.0)
    small_ref[hidden_count:, :] = jnp.where(place == 0, decay_row, tail)
    copy_out.wait()


def params():
    return pltpu.CompilerParams(vmem_limit_bytes=56 * MIB)


def estimate(flops, nbytes):
    return pl.CostEstimate(flops=flops, bytes_accessed=nbytes, transcendentals=0)


def gate_kernel(left_ref, right_ref, out_ref):
    width = out_ref.shape[1]
    for at in range(out_ref.shape[0]):
        lanes = slice(at * width, (at + 1) * width)
        left = left_ref[:, lanes].astype(jnp.float32)
        right = right_ref[:, lanes].astype(jnp.float32)
        out_ref[at] = (left * right).T.astype(jnp.bfloat16)


def gate(left, right, count):
    rows, columns = left.shape
    width = columns // count
    if width % 128 != 0:
        product = (left.astype(jnp.float32) * right.astype(jnp.float32)).astype(jnp.bfloat16)
        return product.reshape(rows, count, width).transpose(1, 2, 0)
    group = math.gcd(count, 4)
    return pl.pallas_call(
        gate_kernel,
        grid=(count // group,),
        in_specs=[pl.BlockSpec((rows, group * width), lambda i: (0, i))] * 2,
        out_specs=pl.BlockSpec((group, width, rows), lambda i: (i, 0, 0)),
        out_shape=jax.ShapeDtypeStruct((count, width, rows), jnp.bfloat16),
        compiler_params=params(),
        cost_estimate=estimate(rows * columns, rows * columns * 6),
    )(left, right)


def ungate_kernel(back_ref, *refs):
    count = len(refs) // 2
    width = back_ref.shape[1]
    for at in range(back_ref.shape[0]):
        lanes = slice(at * width, (at + 1) * width)
        back = back_ref[at].astype(jnp.float32).T
        for factor_ref, out_ref in zip(refs[:count], refs[count:]):
            factor = factor_ref[:, lanes].astype(jnp.float32)
            out_ref[:, lanes] = (back * factor).astype(jnp.bfloat16)


def ungate(back, factors):
    count, width, rows = back.shape
    columns = count * width
    if width % 128 != 0:
        part = back.transpose(2, 0, 1).reshape(rows, columns).astype(jnp.float32)
        return [(part * factor.astype(jnp.float32)).astype(jnp.bfloat16) for factor in factors]
    group = math.gcd(count, 4)
    wide = pl.BlockSpec((rows, group * width), lambda i: (0, i))
    return pl.pallas_call(
        ungate_kernel,
        grid=(count // group,),
        in_specs=[pl.BlockSpec((group, width, rows), lambda i: (i, 0, 0))]
        + [wide] * len(factors),
        out_specs=[wide] * len(factors),
        out_shape=[jax.ShapeDtypeStruct((rows, columns), jnp.bfloat16)] * len(factors),
        compiler_params=params(),
        cost_estimate=estimate(rows * columns, rows * columns * (2 + 4 * len(factors))),
    )(back, *factors)


def per_device(q_proj, k_proj, v_proj, grad_out, w_first, w_second, decay_rate, skip_gain):
    height, chan_tp = q_proj.shape
    parts = lax.axis_size("seq")
    length = height * parts
    width = chan_tp // parts
    band_total, hidden_count = w_first.shape
    seq_index = lax.axis_index("seq")

    def exchange(values):
        return lax.all_to_all(values, "seq", split_axis=0, concat_axis=0, tiled=True)

    gated_in = exchange(gate(k_proj, v_proj, parts))
    gated_grad = gate(grad_out, q_proj, parts)

    tables = jnp.asarray(transform_tables(length, height))
    twiddle = jnp.asarray(twiddle_table(length, height))
    positional = positional_table(length, band_total // 2)
    sine_input = jnp.dot(
        w_first.T, positional, precision=HIGH, preferred_element_type=jnp.float32
    )
    hidden = jnp.sin(sine_input)
    cosine = jnp.cos(sine_input)
    offset = seq_index * width
    w_mine = lax.dynamic_slice_in_dim(w_second, offset, width, 1)
    decay_mine = lax.dynamic_slice_in_dim(decay_rate, offset, width, 0)[:, None]
    skip_mine = lax.dynamic_slice_in_dim(skip_gain, offset, width, 0)[:, None]

    spectrum_shape = jax.ShapeDtypeStruct((parts, width, 2 * height), jnp.float32)
    work = pltpu.VMEM(spectrum_shape.shape, jnp.float32)
    split = pltpu.VMEM((2, 6 * height, 2 * height), jnp.bfloat16)
    anywhere = pl.BlockSpec(memory_space=pl.ANY)
    in_vmem = pl.BlockSpec(memory_space=pltpu.VMEM)
    product_flops = 2 * 3 * parts * 4 * height * height * width

    long_filter, filter_spectrum = pl.pallas_call(
        filter_kernel,
        in_specs=[in_vmem] * 5,
        out_specs=[in_vmem, in_vmem],
        out_shape=[jax.ShapeDtypeStruct((width, length), jnp.float32), spectrum_shape],
        scratch_shapes=[work, split],
        compiler_params=params(),
        cost_estimate=estimate(1000, 1000),
    )(w_mine.T, hidden, decay_mine, tables, twiddle)

    gated_grad, long_filter, filter_spectrum = lax.optimization_barrier(
        (gated_grad, long_filter, filter_spectrum)
    )
    gated_grad = exchange(gated_grad)
    sems = pltpu.SemaphoreType.DMA((2,))
    block_shape = jax.ShapeDtypeStruct(gated_in.shape, jnp.bfloat16)

    convolved, in_spectrum = pl.pallas_call(
        conv_kernel,
        in_specs=[in_vmem, anywhere, in_vmem, in_vmem, in_vmem],
        out_specs=[in_vmem, anywhere],
        out_shape=[block_shape, spectrum_shape],
        scratch_shapes=[work, work, work, split, sems],
        compiler_params=params(),
        cost_estimate=estimate(2 * product_flops, length * width * 20),
    )(gated_in, filter_spectrum, tables, twiddle, skip_mine)
    conv_back = exchange(convolved)

    small, first_part, grad_spectrum = pl.pallas_call(
        filter_grad_kernel,
        in_specs=[in_vmem, in_vmem, anywhere] + [in_vmem] * 8,
        out_specs=[in_vmem, in_vmem, anywhere],
        out_shape=[
            jax.ShapeDtypeStruct((hidden_count + 8, width), jnp.float32),
            jax.ShapeDtypeStruct((band_total, hidden_count), jnp.float32),
            spectrum_shape,
        ],
        scratch_shapes=[
            work,
            work,
            work,
            pltpu.VMEM((width, length), jnp.float32),
            pltpu.VMEM((2, width, height), jnp.float32),
            split,
            sems,
        ],
        compiler_params=params(),
        cost_estimate=estimate(2 * product_flops, length * width * 20),
    )(
        gated_in,
        gated_grad,
        in_spectrum,
        tables,
        twiddle,
        decay_mine,
        long_filter,
        hidden,
        w_mine,
        cosine,
        positional,
    )
    grad_gated = pl.pallas_call(
        corr_kernel,
        in_specs=[in_vmem, anywhere, anywhere, in_vmem, in_vmem, in_vmem],
        out_specs=in_vmem,
        out_shape=block_shape,
        scratch_shapes=[work, work, work, split, sems],
        compiler_params=params(),
        cost_estimate=estimate(product_flops, length * width * 16),
    )(gated_grad, grad_spectrum, filter_spectrum, tables, twiddle, skip_mine)
    grad_back = exchange(grad_gated)

    packed = jnp.concatenate([small, first_part.reshape(-1, width)], axis=0)
    gathered = lax.all_gather(packed, "seq", axis=1, tiled=True)
    grad_second = gathered[:hidden_count]
    grad_decay = gathered[hidden_count]
    grad_skip = gathered[hidden_count + 1]
    first_rows = gathered[hidden_count + 8 :].reshape(-1, parts, width).sum(axis=1)
    grad_first = first_rows.reshape(band_total, hidden_count)
    if lax.axis_size("tp") == 2:
        grad_first = grad_first + lax.ppermute(grad_first, "tp", [(0, 1), (1, 0)])
    else:
        grad_first = lax.psum(grad_first, "tp")
    (grad_q,) = ungate(conv_back, (grad_out,))
    grad_k, grad_v = ungate(grad_back, (v_proj, k_proj))
    return (grad_q, grad_k, grad_v, grad_first, grad_second, grad_decay, grad_skip)


def solution(mesh):
    return jax.shard_map(
        per_device,
        mesh=mesh,
        in_specs=(
            P("seq", "tp"),
            P("seq", "tp"),
            P("seq", "tp"),
            P("seq", "tp"),
            P(),
            P(None, "tp"),
            P("tp"),
            P("tp"),
        ),
        out_specs=(
            P("seq", "tp"),
            P("seq", "tp"),
            P("seq", "tp"),
            P(),
            P(None, "tp"),
            P("tp"),
            P("tp"),
        ),
        check_vma=False,
    )
```

```python
import functools
import math

import jax
import jax.numpy as jnp
import ml_dtypes
import numpy as np
from jax import lax
from jax.experimental import pallas as pl
from jax.experimental.pallas import tpu as pltpu
from jax.sharding import PartitionSpec as P

HIGH = lax.Precision.HIGHEST
MIB = 1024 * 1024


def positional_table(length, band_count):
    positions = jnp.arange(length, dtype=jnp.int32)
    band_index = jnp.arange(band_count, dtype=jnp.int32)
    frequency = 3 * (band_index + 1) * (band_index + 1) + band_index
    phase_index = frequency[:, None] * positions[None, :] % length
    angles = phase_index.astype(jnp.float32) * (2.0 * math.pi / length)
    return jnp.concatenate([jnp.sin(angles), jnp.cos(angles)], axis=0)


@functools.lru_cache(maxsize=None)
def transform_tables(length, height):
    j = np.arange(height)
    angles = (j[:, None] * j[None, :] % height) * (2.0 * np.pi / height)
    cosine, sine = np.cos(angles), np.sin(angles)
    forward = np.concatenate(
        [np.concatenate([cosine, -sine], axis=1), np.concatenate([sine, cosine], axis=1)], axis=0
    )
    return np.stack([forward, forward.T / length]).astype(np.float32)


@functools.lru_cache(maxsize=None)
def twiddle_table(length, height):
    parts = length // height
    r = np.arange(parts)[:, None]
    j = np.arange(height)[None, :]
    angles = (j * (4 * r + 1) % (4 * length)) * (2.0 * np.pi / (4 * length))
    return np.concatenate([np.cos(angles), -np.sin(angles)], axis=1).astype(np.float32)


def turn(value, cosine, sine):
    real, imag = value
    return (real * cosine - imag * sine, real * sine + imag * cosine)


def small_fft(values, sign):
    count = len(values)
    if count == 1:
        return values
    even = small_fft(values[0::2], sign)
    odd = small_fft(values[1::2], sign)
    first, second = [], []
    for k in range(count // 2):
        real, imag = odd[k]
        if k == 0:
            pass
        elif 4 * k == count:
            real, imag = (-imag, real) if sign > 0 else (imag, -real)
        elif 8 * k == count:
            half = math.sqrt(0.5)
            if sign > 0:
                real, imag = (real - imag) * half, (real + imag) * half
            else:
                real, imag = (real + imag) * half, (imag - real) * half
        elif 8 * k == 3 * count:
            half = math.sqrt(0.5)
            if sign > 0:
                real, imag = (real + imag) * -half, (real - imag) * half
            else:
                real, imag = (imag - real) * half, (real + imag) * -half
        else:
            angle = sign * 2.0 * math.pi * k / count
            real, imag = turn((real, imag), math.cos(angle), math.sin(angle))
        base_real, base_imag = even[k]
        first.append((base_real + real, base_imag + imag))
        second.append((base_real - real, base_imag - imag))
    return first + second


def parts_forward(values):
    count = len(values)
    turned = []
    for p, value in enumerate(values):
        angle = 2.0 * math.pi * p / (4 * count)
        turned.append((value * math.cos(angle), value * -math.sin(angle)))
    return small_fft(turned, -1)


def parts_inverse(values):
    count = len(values)
    result = []
    for p, (real, imag) in enumerate(small_fft(values, 1)):
        angle = 2.0 * math.pi * p / (4 * count)
        result.append(real * math.cos(angle) - imag * math.sin(angle))
    return result


def split_bf16(value):
    high = value.astype(jnp.bfloat16)
    return high, (value - high.astype(jnp.float32)).astype(jnp.bfloat16)


def split_table(table_ref, split):
    size = table_ref.shape[1]
    for direction in range(2):
        high, low = split_bf16(table_ref[direction])
        split[direction, :size] = high
        split[direction, size : 2 * size] = high
        split[direction, 2 * size :] = low


def transform(value, split, direction):
    high, low = split_bf16(value)
    return jnp.dot(
        jnp.concatenate([high, low, high], axis=1),
        split[direction],
        preferred_element_type=jnp.float32,
    )


def spectrum_product(left, right, conjugate):
    height = left.shape[1] // 2
    left_real, left_imag = left[:, :height], left[:, height:]
    right_real, right_imag = right[:, :height], right[:, height:]
    if conjugate:
        real = left_real * right_real + left_imag * right_imag
        imag = left_real * right_imag - left_imag * right_real
    else:
        real = left_real * right_real - left_imag * right_imag
        imag = left_real * right_imag + left_imag * right_real
    return jnp.concatenate([real, imag], axis=1)


def first_chunk(load, work, twiddle_ref, index):
    parts, height = work.shape[0], work.shape[2] // 2
    row = pl.multiple_of(index * 16, 16)
    values = [load(p, row) for p in range(parts)]
    for half in (0, 8):
        rows = pl.ds(row + half, 8)
        turned = parts_forward([value[half : half + 8] for value in values])
        for r, value in enumerate(turned):
            cosine = twiddle_ref[r : r + 1, :height]
            sine = twiddle_ref[r : r + 1, height:]
            work[r, rows, :height], work[r, rows, height:] = turn(value, cosine, sine)


def last_chunk(store, work, twiddle_ref, index):
    parts, height = work.shape[0], work.shape[2] // 2
    row = pl.multiple_of(index * 16, 16)
    halves = []
    for half in (0, 8):
        rows = pl.ds(row + half, 8)
        values = []
        for r in range(parts):
            cosine = twiddle_ref[r : r + 1, :height]
            sine = twiddle_ref[r : r + 1, height:]
            value = (work[r, rows, :height], work[r, rows, height:])
            values.append(turn(value, cosine, -sine))
        halves.append(parts_inverse(values))
    for p in range(parts):
        store(p, row, jnp.concatenate([halves[0][p], halves[1][p]], axis=0))


GROUP = 4


def run_chunks(width, chunk, parts=0, block=None):
    chunks = width // 16
    per = math.gcd(chunks, GROUP)
    paired = parts * per == GROUP * chunks

    def one(index, carry):
        if paired:
            block(index * GROUP)
        for b in range(per):
            chunk(index * per + b)
        return carry

    lax.fori_loop(0, chunks // per, one, 0)
    if not paired and parts > 0:
        run_blocks(parts, block)


def run_blocks(parts, block):
    def one(index, carry):
        block(index * GROUP)
        return carry

    lax.fori_loop(0, parts // GROUP, one, 0)


def group_of(r):
    return pl.ds(pl.multiple_of(r, GROUP), GROUP)


def read_group(ref, r):
    _, width, columns = ref.shape
    return ref[group_of(r)].reshape(GROUP * width, columns)


def write_group(ref, r, value):
    ref[group_of(r)] = value.reshape((GROUP,) + ref.shape[1:])


def envelope_at(decay, start, length, height):
    position = (start + lax.broadcasted_iota(jnp.int32, (1, height), 1)).astype(jnp.float32)
    fraction = position * (1.0 / length)
    return jnp.exp(-decay * fraction), fraction


def columns_of(p, height):
    return slice(p * height, (p + 1) * height)


def filter_kernel(
    w_t_ref, hidden_ref, decay_ref, table_ref, twiddle_ref, filter_ref, spectrum_ref, work, split
):
    parts, width, height = work.shape[0], work.shape[1], work.shape[2] // 2
    length = filter_ref.shape[1]
    scale = length**-0.5
    split_table(table_ref, split)
    filter_ref[...] = jnp.dot(
        w_t_ref[...], hidden_ref[...], precision=HIGH, preferred_element_type=jnp.float32
    )

    def load(p, row):
        rows, columns = pl.ds(row, 16), columns_of(p, height)
        envelope, _ = envelope_at(decay_ref[rows, :], p * height, length, height)
        value = filter_ref[rows, columns] * envelope * scale
        filter_ref[rows, columns] = value
        return value

    def block(r):
        write_group(spectrum_ref, r, transform(read_group(work, r), split, 0))

    run_chunks(width, lambda i: first_chunk(load, work, twiddle_ref, i))
    run_blocks(parts, block)


def load_from(ref):
    def load(p, row):
        return ref[p, pl.ds(row, 16), :].astype(jnp.float32)

    return load


def store_to(ref, skip_ref, load):
    def store(p, row, value):
        value = value + skip_ref[pl.ds(row, 16), :] * load(p, row)
        ref[p, pl.ds(row, 16), :] = value.astype(jnp.bfloat16)

    return store


def conv_kernel(
    x_ref, h_any, table_ref, twiddle_ref, skip_ref, y_ref, x_any, work, spectra, h, split, sems
):
    parts, width = work.shape[0], work.shape[1]
    copy_in = pltpu.make_async_copy(h_any, h, sems.at[0])
    copy_in.start()
    split_table(table_ref, split)
    load = load_from(x_ref)

    def block(r):
        spectrum = transform(read_group(work, r), split, 0)
        write_group(spectra, r, spectrum)
        product = spectrum_product(read_group(h, r), spectrum, False)
        write_group(work, r, transform(product, split, 1))

    run_chunks(width, lambda i: first_chunk(load, work, twiddle_ref, i))
    copy_in.wait()
    run_blocks(parts, block)
    copy_out = pltpu.make_async_copy(spectra, x_any, sems.at[1])
    copy_out.start()
    store = store_to(y_ref, skip_ref, load)
    run_chunks(width, lambda i: last_chunk(store, work, twiddle_ref, i))
    copy_out.wait()


def grad_kernel(
    x_ref,
    g_ref,
    x_any,
    h_any,
    filter_any,
    table_ref,
    twiddle_ref,
    skip_ref,
    decay_ref,
    hidden_ref,
    w_ref,
    cosine_ref,
    positional_ref,
    z_ref,
    small_ref,
    first_ref,
    work,
    cross,
    h,
    raw,
    sums,
    split,
    sems,
):
    parts, height = work.shape[0], work.shape[2] // 2
    width, length = raw.shape
    hidden_count = hidden_ref.shape[0]
    scale = length**-0.5
    copies = [
        pltpu.make_async_copy(source, target, sems.at[at])
        for at, (source, target) in enumerate(((x_any, cross), (h_any, h), (filter_any, raw)))
    ]
    for copy in copies:
        copy.start()
    split_table(table_ref, split)
    load = load_from(g_ref)

    def block(r):
        spectrum = transform(read_group(work, r), split, 0)
        product = spectrum_product(read_group(h, r), spectrum, True)
        write_group(work, r, transform(product, split, 1))
        product = spectrum_product(read_group(cross, r), spectrum, True)
        write_group(cross, r, transform(product, split, 1))

    def store(p, row, value):
        rows, columns = pl.ds(row, 16), columns_of(p, height)
        envelope, fraction = envelope_at(decay_ref[rows, :], p * height, length, height)
        decay_part = value * raw[rows, columns] * fraction
        skip_part = load_from(x_ref)(p, row) * load(p, row)
        raw[rows, columns] = value * envelope * scale
        if p > 0:
            decay_part = decay_part + sums[0, rows, :]
            skip_part = skip_part + sums[1, rows, :]
        sums[0, rows, :] = decay_part
        sums[1, rows, :] = skip_part

    run_chunks(width, lambda i: first_chunk(load, work, twiddle_ref, i))
    for copy in copies:
        copy.wait()
    run_blocks(parts, block)
    store_z = store_to(z_ref, skip_ref, load)
    run_chunks(width, lambda i: last_chunk(store_z, work, twiddle_ref, i))
    run_chunks(width, lambda i: last_chunk(store, cross, twiddle_ref, i))

    def dot_pairs(left, right, along):
        def dot(one, two):
            return lax.dot_general(
                one, two, (((1,), (along,)), ((), ())), preferred_element_type=jnp.float32
            )

        return dot(left[0], right[0]) + (dot(left[0], right[1]) + dot(left[1], right[0]))

    second = jnp.zeros((hidden_count, width), jnp.float32)
    band_total = positional_ref.shape[0]
    first = jnp.zeros((band_total, hidden_count), jnp.float32)
    w_pair = split_bf16(w_ref[...])
    chunk = min(length, 512)
    for at in range(0, length, chunk):
        columns = slice(at, at + chunk)
        raw_pair = split_bf16(raw[:, columns])
        second += dot_pairs(split_bf16(hidden_ref[:, columns]), raw_pair, 1)
        hidden_part = dot_pairs(w_pair, raw_pair, 0) * cosine_ref[:, columns]
        first += dot_pairs(split_bf16(positional_ref[:, columns]), split_bf16(hidden_part), 1)

    first_ref[:band_total, :], first_ref[band_total:, :] = split_bf16(first * scale)
    small_ref[:hidden_count, :] = (second * scale).astype(jnp.bfloat16)
    place = lax.broadcasted_iota(jnp.int32, (16, width), 0)
    tail = jnp.zeros((16, width), jnp.float32)
    decay_pair = split_bf16(jnp.sum(sums[0].T, axis=0, keepdims=True) * -scale)
    skip_pair = split_bf16(jnp.sum(sums[1].T, axis=0, keepdims=True) * scale)
    for at, row in enumerate(decay_pair + skip_pair):
        tail = jnp.where(place == at, row.astype(jnp.float32), tail)
    small_ref[hidden_count:, :] = tail.astype(jnp.bfloat16)


def params():
    return pltpu.CompilerParams(vmem_limit_bytes=56 * MIB)


def estimate(flops, nbytes):
    return pl.CostEstimate(flops=flops, bytes_accessed=nbytes, transcendentals=0)


def gate_kernel(left_ref, right_ref, out_ref):
    width = out_ref.shape[1]
    for at in range(out_ref.shape[0]):
        lanes = slice(at * width, (at + 1) * width)
        left = left_ref[:, lanes].astype(jnp.float32)
        right = right_ref[:, lanes].astype(jnp.float32)
        out_ref[at] = (left * right).T.astype(jnp.bfloat16)


def gate(left, right, count):
    rows, columns = left.shape
    width = columns // count
    if width % 128 != 0:
        product = (left.astype(jnp.float32) * right.astype(jnp.float32)).astype(jnp.bfloat16)
        return product.reshape(rows, count, width).transpose(1, 2, 0)
    group = math.gcd(count, 4)
    return pl.pallas_call(
        gate_kernel,
        grid=(count // group,),
        in_specs=[pl.BlockSpec((rows, group * width), lambda i: (0, i))] * 2,
        out_specs=pl.BlockSpec((group, width, rows), lambda i: (i, 0, 0)),
        out_shape=jax.ShapeDtypeStruct((count, width, rows), jnp.bfloat16),
        compiler_params=params(),
        cost_estimate=estimate(rows * columns, rows * columns * 6),
    )(left, right)


def ungate_kernel(back_ref, *refs):
    count = len(refs) // 2
    width = back_ref.shape[1]
    for at in range(back_ref.shape[0]):
        lanes = slice(at * width, (at + 1) * width)
        back = back_ref[at].astype(jnp.float32).T
        for factor_ref, out_ref in zip(refs[:count], refs[count:]):
            factor = factor_ref[:, lanes].astype(jnp.float32)
            out_ref[:, lanes] = (back * factor).astype(jnp.bfloat16)


def ungate(back, factors):
    count, width, rows = back.shape
    columns = count * width
    if width % 128 != 0:
        part = back.transpose(2, 0, 1).reshape(rows, columns).astype(jnp.float32)
        return [(part * factor.astype(jnp.float32)).astype(jnp.bfloat16) for factor in factors]
    group = math.gcd(count, 4)
    wide = pl.BlockSpec((rows, group * width), lambda i: (0, i))
    return pl.pallas_call(
        ungate_kernel,
        grid=(count // group,),
        in_specs=[pl.BlockSpec((group, width, rows), lambda i: (i, 0, 0))]
        + [wide] * len(factors),
        out_specs=[wide] * len(factors),
        out_shape=[jax.ShapeDtypeStruct((rows, columns), jnp.bfloat16)] * len(factors),
        compiler_params=params(),
        cost_estimate=estimate(rows * columns, rows * columns * (2 + 4 * len(factors))),
    )(back, *factors)


def gather_all(block, count, index, inner):
    def swaps(held, masks):
        received = [held]
        for mask in masks:
            pairs = [(i, i ^ mask) for i in range(count)]
            received.append(lax.ppermute(held, "seq", pairs))
        return jnp.stack(received)

    across = swaps(block, range(inner, count, inner))
    held = swaps(across, range(1, inner))
    bits = count.bit_length() - 1
    inner_bits = inner.bit_length() - 1
    held = held.reshape((2,) * bits + block.shape)
    for axis in range(bits):
        bit = inner_bits - 1 - axis if axis < inner_bits else bits - 1 - (axis - inner_bits)
        held = jnp.where((index >> bit) % 2 == 1, jnp.flip(held, axis), held)
    held = held.reshape((inner, count // inner) + block.shape)
    return jnp.swapaxes(held, 0, 1).reshape((count,) + block.shape), across


def per_device(q_proj, k_proj, v_proj, grad_out, w_first, w_second, decay_rate, skip_gain):
    height, chan_tp = q_proj.shape
    parts = lax.axis_size("seq")
    length = height * parts
    width = chan_tp // parts
    band_total, hidden_count = w_first.shape
    seq_index = lax.axis_index("seq")

    def exchange(values):
        return lax.all_to_all(values, "seq", split_axis=0, concat_axis=0, tiled=True)

    gated_in = exchange(gate(k_proj, v_proj, parts))
    gated_grad = gate(grad_out, q_proj, parts)

    tables = jnp.asarray(transform_tables(length, height))
    twiddle = jnp.asarray(twiddle_table(length, height))
    positional = positional_table(length, band_total // 2)
    sine_input = jnp.dot(
        w_first.T, positional, precision=HIGH, preferred_element_type=jnp.float32
    )
    hidden = jnp.sin(sine_input)
    cosine = jnp.cos(sine_input)
    offset = seq_index * width
    w_mine = lax.dynamic_slice_in_dim(w_second, offset, width, 1)
    decay_mine = lax.dynamic_slice_in_dim(decay_rate, offset, width, 0)[:, None]
    skip_mine = lax.dynamic_slice_in_dim(skip_gain, offset, width, 0)[:, None]

    spectrum_shape = jax.ShapeDtypeStruct((parts, width, 2 * height), jnp.float32)
    work = pltpu.VMEM(spectrum_shape.shape, jnp.float32)
    split = pltpu.VMEM((2, 6 * height, 2 * height), jnp.bfloat16)
    anywhere = pl.BlockSpec(memory_space=pl.ANY)
    in_vmem = pl.BlockSpec(memory_space=pltpu.VMEM)
    product_flops = 2 * 3 * parts * 4 * height * height * width

    long_filter, filter_spectrum = pl.pallas_call(
        filter_kernel,
        in_specs=[in_vmem] * 5,
        out_specs=[in_vmem, in_vmem],
        out_shape=[jax.ShapeDtypeStruct((width, length), jnp.float32), spectrum_shape],
        scratch_shapes=[work, split],
        compiler_params=params(),
        cost_estimate=estimate(1000, 1000),
    )(w_mine.T, hidden, decay_mine, tables, twiddle)

    gated_grad, long_filter, filter_spectrum, w_mine, skip_mine, positional = (
        lax.optimization_barrier(
            (gated_grad, long_filter, filter_spectrum, w_mine, skip_mine, positional)
        )
    )
    gated_grad = exchange(gated_grad)
    sems = pltpu.SemaphoreType.DMA((2,))
    block_shape = jax.ShapeDtypeStruct(gated_in.shape, jnp.bfloat16)

    convolved, in_spectrum = pl.pallas_call(
        conv_kernel,
        in_specs=[in_vmem, anywhere, in_vmem, in_vmem, in_vmem],
        out_specs=[in_vmem, anywhere],
        out_shape=[block_shape, spectrum_shape],
        scratch_shapes=[work, work, work, split, sems],
        compiler_params=params(),
        cost_estimate=estimate(2 * product_flops, length * width * 20),
    )(gated_in, filter_spectrum, tables, twiddle, skip_mine)
    conv_back = exchange(convolved)

    grad_gated, small, first_pair = pl.pallas_call(
        grad_kernel,
        in_specs=[in_vmem, in_vmem, anywhere, anywhere, anywhere] + [in_vmem] * 8,
        out_specs=[in_vmem, in_vmem, in_vmem],
        out_shape=[
            block_shape,
            jax.ShapeDtypeStruct((hidden_count + 16, width), jnp.bfloat16),
            jax.ShapeDtypeStruct((2 * band_total, hidden_count), jnp.bfloat16),
        ],
        scratch_shapes=[
            work,
            work,
            work,
            pltpu.VMEM((width, length), jnp.float32),
            pltpu.VMEM((2, width, height), jnp.float32),
            split,
            pltpu.SemaphoreType.DMA((3,)),
        ],
        compiler_params=params(),
        cost_estimate=estimate(3 * product_flops, length * width * 20),
    )(
        gated_in,
        gated_grad,
        in_spectrum,
        filter_spectrum,
        long_filter,
        tables,
        twiddle,
        skip_mine,
        decay_mine,
        hidden,
        w_mine,
        cosine,
        positional,
    )
    packed = jnp.concatenate([small, first_pair.reshape(-1, width)], axis=0)
    gathered, across = gather_all(packed, parts, seq_index, math.gcd(parts, 4))
    grad_gated, _ = lax.optimization_barrier((grad_gated, across))
    grad_back = exchange(grad_gated)
    second = gathered[:, :hidden_count].astype(jnp.float32)
    grad_second = second.transpose(1, 0, 2).reshape(hidden_count, chan_tp)
    tail = gathered[:, hidden_count : hidden_count + 4].astype(jnp.float32)
    grad_decay = (tail[:, 0] + tail[:, 1]).reshape(chan_tp)
    grad_skip = (tail[:, 2] + tail[:, 3]).reshape(chan_tp)
    first_rows = gathered[:, hidden_count + 16 :].astype(jnp.float32).sum(axis=0)
    grad_first = first_rows.reshape(2, band_total, hidden_count).sum(axis=0)
    if lax.axis_size("tp") == 2:
        grad_first = grad_first + lax.ppermute(grad_first, "tp", [(0, 1), (1, 0)])
    else:
        grad_first = lax.psum(grad_first, "tp")
    (grad_q,) = ungate(conv_back, (grad_out,))
    grad_k, grad_v = ungate(grad_back, (v_proj, k_proj))
    return (grad_q, grad_k, grad_v, grad_first, grad_second, grad_decay, grad_skip)


def solution(mesh):
    return jax.shard_map(
        per_device,
        mesh=mesh,
        in_specs=(
            P("seq", "tp"),
            P("seq", "tp"),
            P("seq", "tp"),
            P("seq", "tp"),
            P(),
            P(None, "tp"),
            P("tp"),
            P("tp"),
        ),
        out_specs=(
            P("seq", "tp"),
            P("seq", "tp"),
            P("seq", "tp"),
            P(),
            P(None, "tp"),
            P("tp"),
            P("tp"),
        ),
        check_vma=False,
    )
```

```python
import functools
import math

import jax
import jax.numpy as jnp
import ml_dtypes
import numpy as np
from jax import lax
from jax.experimental import pallas as pl
from jax.experimental.pallas import tpu as pltpu
from jax.sharding import PartitionSpec as P

HIGH = lax.Precision.HIGHEST
MIB = 1024 * 1024


def positional_table(length, band_count):
    positions = jnp.arange(length, dtype=jnp.int32)
    band_index = jnp.arange(band_count, dtype=jnp.int32)
    frequency = 3 * (band_index + 1) * (band_index + 1) + band_index
    phase_index = frequency[:, None] * positions[None, :] % length
    angles = phase_index.astype(jnp.float32) * (2.0 * math.pi / length)
    return jnp.concatenate([jnp.sin(angles), jnp.cos(angles)], axis=0)


@functools.lru_cache(maxsize=None)
def transform_tables(length, height):
    j = np.arange(height)
    angles = (j[:, None] * j[None, :] % height) * (2.0 * np.pi / height)
    cosine, sine = np.cos(angles), np.sin(angles)
    forward = np.concatenate(
        [np.concatenate([cosine, -sine], axis=1), np.concatenate([sine, cosine], axis=1)], axis=0
    )
    return np.stack([forward, forward.T / length]).astype(np.float32)


@functools.lru_cache(maxsize=None)
def twiddle_table(length, height):
    parts = length // height
    r = np.arange(parts)[:, None]
    j = np.arange(height)[None, :]
    angles = (j * (4 * r + 1) % (4 * length)) * (2.0 * np.pi / (4 * length))
    return np.concatenate([np.cos(angles), -np.sin(angles)], axis=1).astype(np.float32)


def turn(value, cosine, sine):
    real, imag = value
    return (real * cosine - imag * sine, real * sine + imag * cosine)


def small_fft(values, sign):
    count = len(values)
    if count == 1:
        return values
    even = small_fft(values[0::2], sign)
    odd = small_fft(values[1::2], sign)
    first, second = [], []
    for k in range(count // 2):
        real, imag = odd[k]
        if k == 0:
            pass
        elif 4 * k == count:
            real, imag = (-imag, real) if sign > 0 else (imag, -real)
        elif 8 * k == count:
            half = math.sqrt(0.5)
            if sign > 0:
                real, imag = (real - imag) * half, (real + imag) * half
            else:
                real, imag = (real + imag) * half, (imag - real) * half
        elif 8 * k == 3 * count:
            half = math.sqrt(0.5)
            if sign > 0:
                real, imag = (real + imag) * -half, (real - imag) * half
            else:
                real, imag = (imag - real) * half, (real + imag) * -half
        else:
            angle = sign * 2.0 * math.pi * k / count
            real, imag = turn((real, imag), math.cos(angle), math.sin(angle))
        base_real, base_imag = even[k]
        first.append((base_real + real, base_imag + imag))
        second.append((base_real - real, base_imag - imag))
    return first + second


def parts_forward(values):
    count = len(values)
    turned = []
    for p, value in enumerate(values):
        angle = 2.0 * math.pi * p / (4 * count)
        turned.append((value * math.cos(angle), value * -math.sin(angle)))
    return small_fft(turned, -1)


def parts_inverse(values):
    count = len(values)
    result = []
    for p, (real, imag) in enumerate(small_fft(values, 1)):
        angle = 2.0 * math.pi * p / (4 * count)
        result.append(real * math.cos(angle) - imag * math.sin(angle))
    return result


def split_bf16(value):
    high = value.astype(jnp.bfloat16)
    return high, (value - high.astype(jnp.float32)).astype(jnp.bfloat16)


def split_table(table_ref, split):
    size = table_ref.shape[1]
    for direction in range(2):
        high, low = split_bf16(table_ref[direction])
        split[direction, :size] = high
        split[direction, size : 2 * size] = high
        split[direction, 2 * size :] = low


def transform(value, split, direction):
    high, low = split_bf16(value)
    return jnp.dot(
        jnp.concatenate([high, low, high], axis=1),
        split[direction],
        preferred_element_type=jnp.float32,
    )


def spectrum_product(left, right, conjugate):
    height = left.shape[1] // 2
    left_real, left_imag = left[:, :height], left[:, height:]
    right_real, right_imag = right[:, :height], right[:, height:]
    if conjugate:
        real = left_real * right_real + left_imag * right_imag
        imag = left_real * right_imag - left_imag * right_real
    else:
        real = left_real * right_real - left_imag * right_imag
        imag = left_real * right_imag + left_imag * right_real
    return jnp.concatenate([real, imag], axis=1)


def first_chunk(load, work, twiddle_ref, index):
    parts, height = work.shape[0], work.shape[2] // 2
    row = pl.multiple_of(index * 16, 16)
    values = [load(p, row) for p in range(parts)]
    for half in (0, 8):
        rows = pl.ds(row + half, 8)
        turned = parts_forward([value[half : half + 8] for value in values])
        for r, value in enumerate(turned):
            cosine = twiddle_ref[r : r + 1, :height]
            sine = twiddle_ref[r : r + 1, height:]
            work[r, rows, :height], work[r, rows, height:] = turn(value, cosine, sine)


def last_chunk(store, work, twiddle_ref, index):
    parts, height = work.shape[0], work.shape[2] // 2
    row = pl.multiple_of(index * 16, 16)
    halves = []
    for half in (0, 8):
        rows = pl.ds(row + half, 8)
        values = []
        for r in range(parts):
            cosine = twiddle_ref[r : r + 1, :height]
            sine = twiddle_ref[r : r + 1, height:]
            value = (work[r, rows, :height], work[r, rows, height:])
            values.append(turn(value, cosine, -sine))
        halves.append(parts_inverse(values))
    for p in range(parts):
        store(p, row, jnp.concatenate([halves[0][p], halves[1][p]], axis=0))


GROUP = 4


def run_chunks(width, chunk, parts=0, block=None):
    chunks = width // 16
    per = math.gcd(chunks, GROUP)
    paired = parts * per == GROUP * chunks

    def one(index, carry):
        if paired:
            block(index * GROUP)
        for b in range(per):
            chunk(index * per + b)
        return carry

    lax.fori_loop(0, chunks // per, one, 0)
    if not paired and parts > 0:
        run_blocks(parts, block)


def run_blocks(parts, block):
    def one(index, carry):
        block(index * GROUP)
        return carry

    lax.fori_loop(0, parts // GROUP, one, 0)


def group_of(r):
    return pl.ds(pl.multiple_of(r, GROUP), GROUP)


def read_group(ref, r):
    _, width, columns = ref.shape
    return ref[group_of(r)].reshape(GROUP * width, columns)


def write_group(ref, r, value):
    ref[group_of(r)] = value.reshape((GROUP,) + ref.shape[1:])


def envelope_at(decay, start, length, height):
    position = (start + lax.broadcasted_iota(jnp.int32, (1, height), 1)).astype(jnp.float32)
    fraction = position * (1.0 / length)
    return jnp.exp(-decay * fraction), fraction


def columns_of(p, height):
    return slice(p * height, (p + 1) * height)


def filter_kernel(
    w_t_ref, hidden_ref, decay_ref, table_ref, twiddle_ref, filter_ref, spectrum_ref, work, split
):
    parts, width, height = work.shape[0], work.shape[1], work.shape[2] // 2
    length = filter_ref.shape[1]
    scale = length**-0.5
    split_table(table_ref, split)
    filter_ref[...] = jnp.dot(
        w_t_ref[...], hidden_ref[...], precision=HIGH, preferred_element_type=jnp.float32
    )

    def load(p, row):
        rows, columns = pl.ds(row, 16), columns_of(p, height)
        envelope, _ = envelope_at(decay_ref[rows, :], p * height, length, height)
        value = filter_ref[rows, columns] * envelope * scale
        filter_ref[rows, columns] = value
        return value

    def block(r):
        write_group(spectrum_ref, r, transform(read_group(work, r), split, 0))

    run_chunks(width, lambda i: first_chunk(load, work, twiddle_ref, i))
    run_blocks(parts, block)


def load_from(ref):
    def load(p, row):
        return ref[p, pl.ds(row, 16), :].astype(jnp.float32)

    return load


def store_to(ref, skip_ref, load):
    def store(p, row, value):
        value = value + skip_ref[pl.ds(row, 16), :] * load(p, row)
        ref[p, pl.ds(row, 16), :] = value.astype(jnp.bfloat16)

    return store


def conv_kernel(
    x_ref, h_any, table_ref, twiddle_ref, skip_ref, y_ref, x_any, work, spectra, h, split, sems
):
    parts, width = work.shape[0], work.shape[1]
    copy_in = pltpu.make_async_copy(h_any, h, sems.at[0])
    copy_in.start()
    split_table(table_ref, split)
    load = load_from(x_ref)

    def block(r):
        spectrum = transform(read_group(work, r), split, 0)
        write_group(spectra, r, spectrum)
        product = spectrum_product(read_group(h, r), spectrum, False)
        write_group(work, r, transform(product, split, 1))

    run_chunks(width, lambda i: first_chunk(load, work, twiddle_ref, i))
    copy_in.wait()
    run_blocks(parts, block)
    copy_out = pltpu.make_async_copy(spectra, x_any, sems.at[1])
    copy_out.start()
    store = store_to(y_ref, skip_ref, load)
    run_chunks(width, lambda i: last_chunk(store, work, twiddle_ref, i))
    copy_out.wait()


def grad_kernel(
    x_ref,
    g_ref,
    x_any,
    h_any,
    filter_any,
    table_ref,
    twiddle_ref,
    skip_ref,
    decay_ref,
    hidden_ref,
    w_ref,
    cosine_ref,
    positional_ref,
    z_ref,
    small_ref,
    first_ref,
    work,
    cross,
    h,
    raw,
    sums,
    split,
    sems,
):
    parts, height = work.shape[0], work.shape[2] // 2
    width, length = raw.shape
    hidden_count = hidden_ref.shape[0]
    scale = length**-0.5
    copies = [
        pltpu.make_async_copy(source, target, sems.at[at])
        for at, (source, target) in enumerate(((x_any, cross), (h_any, h), (filter_any, raw)))
    ]
    for copy in copies:
        copy.start()
    split_table(table_ref, split)
    load = load_from(g_ref)

    def block(r):
        spectrum = transform(read_group(work, r), split, 0)
        product = spectrum_product(read_group(h, r), spectrum, True)
        write_group(work, r, transform(product, split, 1))
        product = spectrum_product(read_group(cross, r), spectrum, True)
        write_group(cross, r, transform(product, split, 1))

    def store(p, row, value):
        rows, columns = pl.ds(row, 16), columns_of(p, height)
        envelope, fraction = envelope_at(decay_ref[rows, :], p * height, length, height)
        decay_part = value * raw[rows, columns] * fraction
        skip_part = load_from(x_ref)(p, row) * load(p, row)
        raw[rows, columns] = value * envelope * scale
        if p > 0:
            decay_part = decay_part + sums[0, rows, :]
            skip_part = skip_part + sums[1, rows, :]
        sums[0, rows, :] = decay_part
        sums[1, rows, :] = skip_part

    run_chunks(width, lambda i: first_chunk(load, work, twiddle_ref, i))
    for copy in copies:
        copy.wait()
    run_blocks(parts, block)
    store_z = store_to(z_ref, skip_ref, load)
    run_chunks(width, lambda i: last_chunk(store_z, work, twiddle_ref, i))
    run_chunks(width, lambda i: last_chunk(store, cross, twiddle_ref, i))

    def dot_pairs(left, right, along):
        def dot(one, two):
            return lax.dot_general(
                one, two, (((1,), (along,)), ((), ())), preferred_element_type=jnp.float32
            )

        return dot(left[0], right[0]) + (dot(left[0], right[1]) + dot(left[1], right[0]))

    second = jnp.zeros((hidden_count, width), jnp.float32)
    band_total = positional_ref.shape[0]
    first = jnp.zeros((band_total, hidden_count), jnp.float32)
    w_pair = split_bf16(w_ref[...])
    chunk = min(length, 512)
    for at in range(0, length, chunk):
        columns = slice(at, at + chunk)
        raw_pair = split_bf16(raw[:, columns])
        second += dot_pairs(split_bf16(hidden_ref[:, columns]), raw_pair, 1)
        hidden_part = dot_pairs(w_pair, raw_pair, 0) * cosine_ref[:, columns]
        first += dot_pairs(split_bf16(positional_ref[:, columns]), split_bf16(hidden_part), 1)

    first_ref[:band_total, :], first_ref[band_total:, :] = split_bf16(first * scale)
    small_ref[:hidden_count, :] = (second * scale).astype(jnp.bfloat16)
    place = lax.broadcasted_iota(jnp.int32, (16, width), 0)
    tail = jnp.zeros((16, width), jnp.float32)
    decay_pair = split_bf16(jnp.sum(sums[0].T, axis=0, keepdims=True) * -scale)
    skip_pair = split_bf16(jnp.sum(sums[1].T, axis=0, keepdims=True) * scale)
    for at, row in enumerate(decay_pair + skip_pair):
        tail = jnp.where(place == at, row.astype(jnp.float32), tail)
    small_ref[hidden_count:, :] = tail.astype(jnp.bfloat16)


def params(limit=56):
    return pltpu.CompilerParams(vmem_limit_bytes=limit * MIB)


def estimate(flops, nbytes):
    return pl.CostEstimate(flops=flops, bytes_accessed=nbytes, transcendentals=0)


def chunk_copies(pairs, sems, first):
    return [
        [
            pltpu.make_async_copy(source, target, sems.at[first + at * len(chunk) + which])
            for which, (source, target) in enumerate(chunk)
        ]
        for at, chunk in enumerate(pairs)
    ]


def run_streams(blocks, group, width, shared, wide_in, wide_out, shared_out, sems, work):
    def part(refs, at):
        return [ref.at[pl.ds(at * group, group)] for ref in refs]

    def lanes(refs, at):
        return [ref.at[:, pl.ds(at * group * width, group * width)] for ref in refs]

    chunks = range(blocks // group)
    incoming, outgoing = [], []
    for at in chunks:
        pairs = [tuple(part(pair, at)) for pair in shared]
        incoming.append(pairs + [tuple(lanes(pair, at)) for pair in wide_in])
        pairs = [tuple(part(pair, at)) for pair in shared_out]
        outgoing.append(pairs + [tuple(lanes(pair, at)) for pair in wide_out])
    arrivals = chunk_copies(incoming, sems, 0)
    departures = chunk_copies(outgoing, sems, len(arrivals) * len(arrivals[0]))
    for chunk in arrivals:
        for copy in chunk:
            copy.start()
    for at in chunks:
        for copy in arrivals[at]:
            copy.wait()
        for block in range(at * group, (at + 1) * group):
            work(block, slice(block * width, (block + 1) * width))
        for copy in departures[at]:
            copy.start()
    for chunk in departures:
        for copy in chunk:
            copy.wait()


def gate_kernel(group, left_any, right_any, out_any, left_ref, right_ref, out_ref, sems):
    count, width, _ = out_ref.shape

    def work(block, lanes):
        left = left_ref[:, lanes].astype(jnp.float32)
        right = right_ref[:, lanes].astype(jnp.float32)
        out_ref[block] = (left * right).T.astype(jnp.bfloat16)

    wide = [(left_any, left_ref), (right_any, right_ref)]
    run_streams(count, group, width, [], wide, [], [(out_ref, out_any)], sems, work)


def gate(left, right, count):
    rows, columns = left.shape
    width = columns // count
    if width % 128 != 0:
        product = (left.astype(jnp.float32) * right.astype(jnp.float32)).astype(jnp.bfloat16)
        return product.reshape(rows, count, width).transpose(1, 2, 0)
    group = math.gcd(count, 2)
    out = jax.ShapeDtypeStruct((count, width, rows), jnp.bfloat16)
    wide = pltpu.VMEM((rows, columns), jnp.bfloat16)
    return pl.pallas_call(
        functools.partial(gate_kernel, group),
        in_specs=[pl.BlockSpec(memory_space=pl.ANY)] * 2,
        out_specs=pl.BlockSpec(memory_space=pl.ANY),
        out_shape=out,
        scratch_shapes=[
            wide,
            wide,
            pltpu.VMEM(out.shape, jnp.bfloat16),
            pltpu.SemaphoreType.DMA((3 * count // group,)),
        ],
        compiler_params=params(16),
        cost_estimate=estimate(rows * columns, rows * columns * 6),
    )(left, right)


def ungate_kernel(group, factors, *refs):
    back_any, factor_anys = refs[0], refs[1 : factors + 1]
    out_anys = refs[factors + 1 : 2 * factors + 1]
    back_ref, *rest = refs[2 * factors + 1 :]
    factor_refs, out_refs, sems = rest[:factors], rest[factors:-1], rest[-1]
    count, width, _ = back_ref.shape

    def work(block, lanes):
        back = back_ref[block].astype(jnp.float32).T
        for factor_ref, out_ref in zip(factor_refs, out_refs):
            factor = factor_ref[:, lanes].astype(jnp.float32)
            out_ref[:, lanes] = (back * factor).astype(jnp.bfloat16)

    shared = [(back_any, back_ref)]
    wide_in = list(zip(factor_anys, factor_refs))
    wide_out = list(zip(out_refs, out_anys))
    run_streams(count, group, width, shared, wide_in, wide_out, [], sems, work)


def ungate(back, factors):
    count, width, rows = back.shape
    columns = count * width
    if width % 128 != 0:
        part = back.transpose(2, 0, 1).reshape(rows, columns).astype(jnp.float32)
        return [(part * factor.astype(jnp.float32)).astype(jnp.bfloat16) for factor in factors]
    group = math.gcd(count, 2)
    anywhere = pl.BlockSpec(memory_space=pl.ANY)
    wide = pltpu.VMEM((rows, columns), jnp.bfloat16)
    copies = (1 + 2 * len(factors)) * count // group
    return pl.pallas_call(
        functools.partial(ungate_kernel, group, len(factors)),
        in_specs=[anywhere] * (1 + len(factors)),
        out_specs=[anywhere] * len(factors),
        out_shape=[jax.ShapeDtypeStruct((rows, columns), jnp.bfloat16)] * len(factors),
        scratch_shapes=[pltpu.VMEM(back.shape, jnp.bfloat16)]
        + [wide] * (2 * len(factors))
        + [pltpu.SemaphoreType.DMA((copies,))],
        compiler_params=params(16),
        cost_estimate=estimate(rows * columns, rows * columns * (2 + 4 * len(factors))),
    )(back, *factors)


def gather_all(block, count, index, inner):
    def swaps(held, masks):
        received = [held]
        for mask in masks:
            pairs = [(i, i ^ mask) for i in range(count)]
            received.append(lax.ppermute(held, "seq", pairs))
        return jnp.stack(received)

    across = swaps(block, range(inner, count, inner))
    held = swaps(across, range(1, inner))
    bits = count.bit_length() - 1
    inner_bits = inner.bit_length() - 1
    held = held.reshape((2,) * bits + block.shape)
    for axis in range(bits):
        bit = inner_bits - 1 - axis if axis < inner_bits else bits - 1 - (axis - inner_bits)
        held = jnp.where((index >> bit) % 2 == 1, jnp.flip(held, axis), held)
    held = held.reshape((inner, count // inner) + block.shape)
    return jnp.swapaxes(held, 0, 1).reshape((count,) + block.shape), across


def per_device(q_proj, k_proj, v_proj, grad_out, w_first, w_second, decay_rate, skip_gain):
    height, chan_tp = q_proj.shape
    parts = lax.axis_size("seq")
    length = height * parts
    width = chan_tp // parts
    band_total, hidden_count = w_first.shape
    seq_index = lax.axis_index("seq")

    def exchange(values):
        return lax.all_to_all(values, "seq", split_axis=0, concat_axis=0, tiled=True)

    gated_in = exchange(gate(k_proj, v_proj, parts))
    gated_grad = gate(grad_out, q_proj, parts)

    tables = jnp.asarray(transform_tables(length, height))
    twiddle = jnp.asarray(twiddle_table(length, height))
    positional = positional_table(length, band_total // 2)
    sine_input = jnp.dot(
        w_first.T, positional, precision=HIGH, preferred_element_type=jnp.float32
    )
    hidden = jnp.sin(sine_input)
    cosine = jnp.cos(sine_input)
    offset = seq_index * width
    w_mine = lax.dynamic_slice_in_dim(w_second, offset, width, 1)
    decay_mine = lax.dynamic_slice_in_dim(decay_rate, offset, width, 0)[:, None]
    skip_mine = lax.dynamic_slice_in_dim(skip_gain, offset, width, 0)[:, None]

    spectrum_shape = jax.ShapeDtypeStruct((parts, width, 2 * height), jnp.float32)
    work = pltpu.VMEM(spectrum_shape.shape, jnp.float32)
    split = pltpu.VMEM((2, 6 * height, 2 * height), jnp.bfloat16)
    anywhere = pl.BlockSpec(memory_space=pl.ANY)
    in_vmem = pl.BlockSpec(memory_space=pltpu.VMEM)
    product_flops = 2 * 3 * parts * 4 * height * height * width

    long_filter, filter_spectrum = pl.pallas_call(
        filter_kernel,
        in_specs=[in_vmem] * 5,
        out_specs=[in_vmem, in_vmem],
        out_shape=[jax.ShapeDtypeStruct((width, length), jnp.float32), spectrum_shape],
        scratch_shapes=[work, split],
        compiler_params=params(),
        cost_estimate=estimate(1000, 1000),
    )(w_mine.T, hidden, decay_mine, tables, twiddle)

    gated_grad, long_filter, filter_spectrum, w_mine, skip_mine, positional = (
        lax.optimization_barrier(
            (gated_grad, long_filter, filter_spectrum, w_mine, skip_mine, positional)
        )
    )
    gated_grad = exchange(gated_grad)
    sems = pltpu.SemaphoreType.DMA((2,))
    block_shape = jax.ShapeDtypeStruct(gated_in.shape, jnp.bfloat16)

    convolved, in_spectrum = pl.pallas_call(
        conv_kernel,
        in_specs=[in_vmem, anywhere, in_vmem, in_vmem, in_vmem],
        out_specs=[in_vmem, anywhere],
        out_shape=[block_shape, spectrum_shape],
        scratch_shapes=[work, work, work, split, sems],
        compiler_params=params(),
        cost_estimate=estimate(2 * product_flops, length * width * 20),
    )(gated_in, filter_spectrum, tables, twiddle, skip_mine)
    conv_back = exchange(convolved)

    grad_gated, small, first_pair = pl.pallas_call(
        grad_kernel,
        in_specs=[in_vmem, in_vmem, anywhere, anywhere, anywhere] + [in_vmem] * 8,
        out_specs=[in_vmem, in_vmem, in_vmem],
        out_shape=[
            block_shape,
            jax.ShapeDtypeStruct((hidden_count + 16, width), jnp.bfloat16),
            jax.ShapeDtypeStruct((2 * band_total, hidden_count), jnp.bfloat16),
        ],
        scratch_shapes=[
            work,
            work,
            work,
            pltpu.VMEM((width, length), jnp.float32),
            pltpu.VMEM((2, width, height), jnp.float32),
            split,
            pltpu.SemaphoreType.DMA((3,)),
        ],
        compiler_params=params(),
        cost_estimate=estimate(3 * product_flops, length * width * 20),
    )(
        gated_in,
        gated_grad,
        in_spectrum,
        filter_spectrum,
        long_filter,
        tables,
        twiddle,
        skip_mine,
        decay_mine,
        hidden,
        w_mine,
        cosine,
        positional,
    )
    packed = jnp.concatenate([small, first_pair.reshape(-1, width)], axis=0)
    gathered, across = gather_all(packed, parts, seq_index, math.gcd(parts, 4))
    grad_gated, _ = lax.optimization_barrier((grad_gated, across))
    grad_back = exchange(grad_gated)
    second = gathered[:, :hidden_count].astype(jnp.float32)
    grad_second = second.transpose(1, 0, 2).reshape(hidden_count, chan_tp)
    tail = gathered[:, hidden_count : hidden_count + 4].astype(jnp.float32)
    grad_decay = (tail[:, 0] + tail[:, 1]).reshape(chan_tp)
    grad_skip = (tail[:, 2] + tail[:, 3]).reshape(chan_tp)
    first_rows = gathered[:, hidden_count + 16 :].astype(jnp.float32).sum(axis=0)
    grad_first = first_rows.reshape(2, band_total, hidden_count).sum(axis=0)
    if lax.axis_size("tp") == 2:
        grad_first = grad_first + lax.ppermute(grad_first, "tp", [(0, 1), (1, 0)])
    else:
        grad_first = lax.psum(grad_first, "tp")
    (grad_q,) = ungate(conv_back, (grad_out,))
    grad_k, grad_v = ungate(grad_back, (v_proj, k_proj))
    return (grad_q, grad_k, grad_v, grad_first, grad_second, grad_decay, grad_skip)


def solution(mesh):
    return jax.shard_map(
        per_device,
        mesh=mesh,
        in_specs=(
            P("seq", "tp"),
            P("seq", "tp"),
            P("seq", "tp"),
            P("seq", "tp"),
            P(),
            P(None, "tp"),
            P("tp"),
            P("tp"),
        ),
        out_specs=(
            P("seq", "tp"),
            P("seq", "tp"),
            P("seq", "tp"),
            P(),
            P(None, "tp"),
            P("tp"),
            P("tp"),
        ),
        check_vma=False,
    )
```

```python
import functools
import math

import jax
import jax.numpy as jnp
import ml_dtypes
import numpy as np
from jax import lax
from jax.experimental import pallas as pl
from jax.experimental.pallas import tpu as pltpu
from jax.sharding import PartitionSpec as P

HIGH = lax.Precision.HIGHEST
MIB = 1024 * 1024


def positional_table(length, band_count):
    positions = jnp.arange(length, dtype=jnp.int32)
    band_index = jnp.arange(band_count, dtype=jnp.int32)
    frequency = 3 * (band_index + 1) * (band_index + 1) + band_index
    phase_index = frequency[:, None] * positions[None, :] % length
    angles = phase_index.astype(jnp.float32) * (2.0 * math.pi / length)
    return jnp.concatenate([jnp.sin(angles), jnp.cos(angles)], axis=0)


@functools.lru_cache(maxsize=None)
def transform_tables(length, height):
    j = np.arange(height)
    angles = (j[:, None] * j[None, :] % height) * (2.0 * np.pi / height)
    cosine, sine = np.cos(angles), np.sin(angles)
    forward = np.concatenate(
        [np.concatenate([cosine, -sine], axis=1), np.concatenate([sine, cosine], axis=1)], axis=0
    )
    return np.stack([forward, forward.T / length]).astype(np.float32)


@functools.lru_cache(maxsize=None)
def twiddle_table(length, height):
    parts = length // height
    r = np.arange(parts)[:, None]
    j = np.arange(height)[None, :]
    angles = (j * (4 * r + 1) % (4 * length)) * (2.0 * np.pi / (4 * length))
    return np.concatenate([np.cos(angles), -np.sin(angles)], axis=1).astype(np.float32)


def turn(value, cosine, sine):
    real, imag = value
    return (real * cosine - imag * sine, real * sine + imag * cosine)


def small_fft(values, sign):
    count = len(values)
    if count == 1:
        return values
    even = small_fft(values[0::2], sign)
    odd = small_fft(values[1::2], sign)
    first, second = [], []
    for k in range(count // 2):
        real, imag = odd[k]
        if k == 0:
            pass
        elif 4 * k == count:
            real, imag = (-imag, real) if sign > 0 else (imag, -real)
        elif 8 * k == count:
            half = math.sqrt(0.5)
            if sign > 0:
                real, imag = (real - imag) * half, (real + imag) * half
            else:
                real, imag = (real + imag) * half, (imag - real) * half
        elif 8 * k == 3 * count:
            half = math.sqrt(0.5)
            if sign > 0:
                real, imag = (real + imag) * -half, (real - imag) * half
            else:
                real, imag = (imag - real) * half, (real + imag) * -half
        else:
            angle = sign * 2.0 * math.pi * k / count
            real, imag = turn((real, imag), math.cos(angle), math.sin(angle))
        base_real, base_imag = even[k]
        first.append((base_real + real, base_imag + imag))
        second.append((base_real - real, base_imag - imag))
    return first + second


def parts_forward(values):
    count = len(values)
    turned = []
    for p, value in enumerate(values):
        angle = 2.0 * math.pi * p / (4 * count)
        turned.append((value * math.cos(angle), value * -math.sin(angle)))
    return small_fft(turned, -1)


def parts_inverse(values):
    count = len(values)
    result = []
    for p, (real, imag) in enumerate(small_fft(values, 1)):
        angle = 2.0 * math.pi * p / (4 * count)
        result.append(real * math.cos(angle) - imag * math.sin(angle))
    return result


def split_bf16(value):
    high = value.astype(jnp.bfloat16)
    return high, (value - high.astype(jnp.float32)).astype(jnp.bfloat16)


def split_table(table_ref, split):
    size = table_ref.shape[1]
    for direction in range(2):
        high, low = split_bf16(table_ref[direction])
        split[direction, :size] = high
        split[direction, size : 2 * size] = high
        split[direction, 2 * size :] = low


def transform(value, split, direction):
    high, low = split_bf16(value)
    return jnp.dot(
        jnp.concatenate([high, low, high], axis=1),
        split[direction],
        preferred_element_type=jnp.float32,
    )


def spectrum_product(left, right, conjugate):
    height = left.shape[1] // 2
    left_real, left_imag = left[:, :height], left[:, height:]
    right_real, right_imag = right[:, :height], right[:, height:]
    if conjugate:
        real = left_real * right_real + left_imag * right_imag
        imag = left_real * right_imag - left_imag * right_real
    else:
        real = left_real * right_real - left_imag * right_imag
        imag = left_real * right_imag + left_imag * right_real
    return jnp.concatenate([real, imag], axis=1)


def first_chunk(load, work, twiddle_ref, index):
    parts, height = work.shape[0], work.shape[2] // 2
    row = pl.multiple_of(index * 16, 16)
    values = [load(p, row) for p in range(parts)]
    for half in (0, 8):
        rows = pl.ds(row + half, 8)
        turned = parts_forward([value[half : half + 8] for value in values])
        for r, value in enumerate(turned):
            cosine = twiddle_ref[r : r + 1, :height]
            sine = twiddle_ref[r : r + 1, height:]
            work[r, rows, :height], work[r, rows, height:] = turn(value, cosine, sine)


def last_chunk(store, work, twiddle_ref, index):
    parts, height = work.shape[0], work.shape[2] // 2
    row = pl.multiple_of(index * 16, 16)
    halves = []
    for half in (0, 8):
        rows = pl.ds(row + half, 8)
        values = []
        for r in range(parts):
            cosine = twiddle_ref[r : r + 1, :height]
            sine = twiddle_ref[r : r + 1, height:]
            value = (work[r, rows, :height], work[r, rows, height:])
            values.append(turn(value, cosine, -sine))
        halves.append(parts_inverse(values))
    for p in range(parts):
        store(p, row, jnp.concatenate([halves[0][p], halves[1][p]], axis=0))


GROUP = 4


def run_chunks(width, chunk, parts=0, block=None):
    chunks = width // 16
    per = math.gcd(chunks, GROUP)
    paired = parts * per == GROUP * chunks

    def one(index, carry):
        if paired:
            block(index * GROUP)
        for b in range(per):
            chunk(index * per + b)
        return carry

    lax.fori_loop(0, chunks // per, one, 0)
    if not paired and parts > 0:
        run_blocks(parts, block)


def run_blocks(parts, block):
    def one(index, carry):
        block(index * GROUP)
        return carry

    lax.fori_loop(0, parts // GROUP, one, 0)


def group_of(r):
    return pl.ds(pl.multiple_of(r, GROUP), GROUP)


def read_group(ref, r):
    _, width, columns = ref.shape
    return ref[group_of(r)].reshape(GROUP * width, columns)


def write_group(ref, r, value):
    ref[group_of(r)] = value.reshape((GROUP,) + ref.shape[1:])


def envelope_at(decay, start, length, height):
    position = (start + lax.broadcasted_iota(jnp.int32, (1, height), 1)).astype(jnp.float32)
    fraction = position * (1.0 / length)
    return jnp.exp(-decay * fraction), fraction


def columns_of(p, height):
    return slice(p * height, (p + 1) * height)


def filter_kernel(
    w_t_ref, hidden_ref, decay_ref, table_ref, twiddle_ref, filter_ref, spectrum_ref, work, split
):
    parts, width, height = work.shape[0], work.shape[1], work.shape[2] // 2
    length = filter_ref.shape[1]
    scale = length**-0.5
    split_table(table_ref, split)
    filter_ref[...] = jnp.dot(
        w_t_ref[...], hidden_ref[...], precision=HIGH, preferred_element_type=jnp.float32
    )

    def load(p, row):
        rows, columns = pl.ds(row, 16), columns_of(p, height)
        envelope, _ = envelope_at(decay_ref[rows, :], p * height, length, height)
        value = filter_ref[rows, columns] * envelope * scale
        filter_ref[rows, columns] = value
        return value

    def block(r):
        write_group(spectrum_ref, r, transform(read_group(work, r), split, 0))

    run_chunks(width, lambda i: first_chunk(load, work, twiddle_ref, i))
    run_blocks(parts, block)


def load_from(ref):
    def load(p, row):
        return ref[p, pl.ds(row, 16), :].astype(jnp.float32)

    return load


def store_to(ref, skip_ref, load):
    def store(p, row, value):
        value = value + skip_ref[pl.ds(row, 16), :] * load(p, row)
        ref[p, pl.ds(row, 16), :] = value.astype(jnp.bfloat16)

    return store


def conv_kernel(
    x_ref, h_any, table_ref, twiddle_ref, skip_ref, y_ref, x_any, work, spectra, h, split, sems
):
    parts, width = work.shape[0], work.shape[1]
    copy_in = pltpu.make_async_copy(h_any, h, sems.at[0])
    copy_in.start()
    split_table(table_ref, split)
    load = load_from(x_ref)

    def block(r):
        spectrum = transform(read_group(work, r), split, 0)
        write_group(spectra, r, spectrum)
        product = spectrum_product(read_group(h, r), spectrum, False)
        write_group(work, r, transform(product, split, 1))

    run_chunks(width, lambda i: first_chunk(load, work, twiddle_ref, i))
    copy_in.wait()
    run_blocks(parts, block)
    copy_out = pltpu.make_async_copy(spectra, x_any, sems.at[1])
    copy_out.start()
    store = store_to(y_ref, skip_ref, load)
    run_chunks(width, lambda i: last_chunk(store, work, twiddle_ref, i))
    copy_out.wait()


def grad_kernel(
    x_ref,
    g_ref,
    x_any,
    h_any,
    filter_any,
    table_ref,
    twiddle_ref,
    skip_ref,
    decay_ref,
    hidden_ref,
    w_ref,
    cosine_ref,
    positional_ref,
    z_ref,
    small_ref,
    first_ref,
    work,
    cross,
    h,
    raw,
    sums,
    split,
    sems,
):
    parts, height = work.shape[0], work.shape[2] // 2
    width, length = raw.shape
    hidden_count = hidden_ref.shape[0]
    scale = length**-0.5
    copies = [
        pltpu.make_async_copy(source, target, sems.at[at])
        for at, (source, target) in enumerate(((x_any, cross), (h_any, h), (filter_any, raw)))
    ]
    for copy in copies:
        copy.start()
    split_table(table_ref, split)
    load = load_from(g_ref)

    def block(r):
        spectrum = transform(read_group(work, r), split, 0)
        product = spectrum_product(read_group(h, r), spectrum, True)
        write_group(work, r, transform(product, split, 1))
        product = spectrum_product(read_group(cross, r), spectrum, True)
        write_group(cross, r, transform(product, split, 1))

    def store(p, row, value):
        rows, columns = pl.ds(row, 16), columns_of(p, height)
        envelope, fraction = envelope_at(decay_ref[rows, :], p * height, length, height)
        decay_part = value * raw[rows, columns] * fraction
        skip_part = load_from(x_ref)(p, row) * load(p, row)
        raw[rows, columns] = value * envelope * scale
        if p > 0:
            decay_part = decay_part + sums[0, rows, :]
            skip_part = skip_part + sums[1, rows, :]
        sums[0, rows, :] = decay_part
        sums[1, rows, :] = skip_part

    run_chunks(width, lambda i: first_chunk(load, work, twiddle_ref, i))
    for copy in copies:
        copy.wait()
    run_blocks(parts, block)
    store_z = store_to(z_ref, skip_ref, load)
    run_chunks(width, lambda i: last_chunk(store_z, work, twiddle_ref, i))
    run_chunks(width, lambda i: last_chunk(store, cross, twiddle_ref, i))

    def dot_pairs(left, right, along):
        def dot(one, two):
            return lax.dot_general(
                one, two, (((1,), (along,)), ((), ())), preferred_element_type=jnp.float32
            )

        return dot(left[0], right[0]) + (dot(left[0], right[1]) + dot(left[1], right[0]))

    second = jnp.zeros((hidden_count, width), jnp.float32)
    band_total = positional_ref.shape[0]
    first = jnp.zeros((band_total, hidden_count), jnp.float32)
    w_pair = split_bf16(w_ref[...])
    chunk = min(length, 512)
    for at in range(0, length, chunk):
        columns = slice(at, at + chunk)
        raw_pair = split_bf16(raw[:, columns])
        second += dot_pairs(split_bf16(hidden_ref[:, columns]), raw_pair, 1)
        hidden_part = dot_pairs(w_pair, raw_pair, 0) * cosine_ref[:, columns]
        first += dot_pairs(split_bf16(positional_ref[:, columns]), split_bf16(hidden_part), 1)

    first_ref[:band_total, :], first_ref[band_total:, :] = split_bf16(first * scale)
    small_ref[:hidden_count, :] = (second * scale).astype(jnp.bfloat16)
    place = lax.broadcasted_iota(jnp.int32, (16, width), 0)
    tail = jnp.zeros((16, width), jnp.float32)
    decay_pair = split_bf16(jnp.sum(sums[0].T, axis=0, keepdims=True) * -scale)
    skip_pair = split_bf16(jnp.sum(sums[1].T, axis=0, keepdims=True) * scale)
    for at, row in enumerate(decay_pair + skip_pair):
        tail = jnp.where(place == at, row.astype(jnp.float32), tail)
    small_ref[hidden_count:, :] = tail.astype(jnp.bfloat16)


def params(limit=56):
    return pltpu.CompilerParams(vmem_limit_bytes=limit * MIB)


def estimate(flops, nbytes):
    return pl.CostEstimate(flops=flops, bytes_accessed=nbytes, transcendentals=0)


def chunk_copies(pairs, sems, first):
    return [
        [
            pltpu.make_async_copy(source, target, sems.at[first + at * len(chunk) + which])
            for which, (source, target) in enumerate(chunk)
        ]
        for at, chunk in enumerate(pairs)
    ]


def run_streams(blocks, group, width, shared, wide_in, wide_out, shared_out, sems, work):
    def part(refs, at):
        return [ref.at[pl.ds(at * group, group)] for ref in refs]

    def lanes(refs, at):
        return [ref.at[:, pl.ds(at * group * width, group * width)] for ref in refs]

    chunks = range(blocks // group)
    incoming, outgoing = [], []
    for at in chunks:
        pairs = [tuple(part(pair, at)) for pair in shared]
        incoming.append(pairs + [tuple(lanes(pair, at)) for pair in wide_in])
        pairs = [tuple(part(pair, at)) for pair in shared_out]
        outgoing.append(pairs + [tuple(lanes(pair, at)) for pair in wide_out])
    arrivals = chunk_copies(incoming, sems, 0)
    departures = chunk_copies(outgoing, sems, len(arrivals) * len(arrivals[0]))
    for chunk in arrivals:
        for copy in chunk:
            copy.start()
    for at in chunks:
        for copy in arrivals[at]:
            copy.wait()
        for block in range(at * group, (at + 1) * group):
            work(block, slice(block * width, (block + 1) * width))
        for copy in departures[at]:
            copy.start()
    for chunk in departures:
        for copy in chunk:
            copy.wait()


def gate_kernel(group, left_any, right_any, out_any, left_ref, right_ref, out_ref, sems):
    count, width, _ = out_ref.shape

    def work(block, lanes):
        left = left_ref[:, lanes].astype(jnp.float32)
        right = right_ref[:, lanes].astype(jnp.float32)
        out_ref[block] = (left * right).T.astype(jnp.bfloat16)

    wide = [(left_any, left_ref), (right_any, right_ref)]
    run_streams(count, group, width, [], wide, [], [(out_ref, out_any)], sems, work)


def gate(left, right, count):
    rows, columns = left.shape
    width = columns // count
    if width % 128 != 0:
        product = (left.astype(jnp.float32) * right.astype(jnp.float32)).astype(jnp.bfloat16)
        return product.reshape(rows, count, width).transpose(1, 2, 0)
    group = math.gcd(count, 2)
    out = jax.ShapeDtypeStruct((count, width, rows), jnp.bfloat16)
    wide = pltpu.VMEM((rows, columns), jnp.bfloat16)
    return pl.pallas_call(
        functools.partial(gate_kernel, group),
        in_specs=[pl.BlockSpec(memory_space=pl.ANY)] * 2,
        out_specs=pl.BlockSpec(memory_space=pl.ANY),
        out_shape=out,
        scratch_shapes=[
            wide,
            wide,
            pltpu.VMEM(out.shape, jnp.bfloat16),
            pltpu.SemaphoreType.DMA((3 * count // group,)),
        ],
        compiler_params=params(),
        cost_estimate=estimate(rows * columns, rows * columns * 6),
    )(left, right)


def ungate_kernel(group, factors, *refs):
    back_any, factor_anys = refs[0], refs[1 : factors + 1]
    out_anys = refs[factors + 1 : 2 * factors + 1]
    back_ref, *rest = refs[2 * factors + 1 :]
    factor_refs, out_refs, sems = rest[:factors], rest[factors:-1], rest[-1]
    count, width, _ = back_ref.shape

    def work(block, lanes):
        back = back_ref[block].astype(jnp.float32).T
        for factor_ref, out_ref in zip(factor_refs, out_refs):
            factor = factor_ref[:, lanes].astype(jnp.float32)
            out_ref[:, lanes] = (back * factor).astype(jnp.bfloat16)

    shared = [(back_any, back_ref)]
    wide_in = list(zip(factor_anys, factor_refs))
    wide_out = list(zip(out_refs, out_anys))
    run_streams(count, group, width, shared, wide_in, wide_out, [], sems, work)


def ungate(back, factors):
    count, width, rows = back.shape
    columns = count * width
    if width % 128 != 0:
        part = back.transpose(2, 0, 1).reshape(rows, columns).astype(jnp.float32)
        return [(part * factor.astype(jnp.float32)).astype(jnp.bfloat16) for factor in factors]
    group = math.gcd(count, 2)
    anywhere = pl.BlockSpec(memory_space=pl.ANY)
    wide = pltpu.VMEM((rows, columns), jnp.bfloat16)
    copies = (1 + 2 * len(factors)) * count // group
    return pl.pallas_call(
        functools.partial(ungate_kernel, group, len(factors)),
        in_specs=[anywhere] * (1 + len(factors)),
        out_specs=[anywhere] * len(factors),
        out_shape=[jax.ShapeDtypeStruct((rows, columns), jnp.bfloat16)] * len(factors),
        scratch_shapes=[pltpu.VMEM(back.shape, jnp.bfloat16)]
        + [wide] * (2 * len(factors))
        + [pltpu.SemaphoreType.DMA((copies,))],
        compiler_params=params(),
        cost_estimate=estimate(rows * columns, rows * columns * (2 + 4 * len(factors))),
    )(back, *factors)


def gather_all(block, count, index, inner):
    def swaps(held, masks):
        received = [held]
        for mask in masks:
            pairs = [(i, i ^ mask) for i in range(count)]
            received.append(lax.ppermute(held, "seq", pairs))
        return jnp.stack(received)

    across = swaps(block, range(inner, count, inner))
    held = swaps(across, range(1, inner))
    bits = count.bit_length() - 1
    inner_bits = inner.bit_length() - 1
    held = held.reshape((2,) * bits + block.shape)
    for axis in range(bits):
        bit = inner_bits - 1 - axis if axis < inner_bits else bits - 1 - (axis - inner_bits)
        held = jnp.where((index >> bit) % 2 == 1, jnp.flip(held, axis), held)
    held = held.reshape((inner, count // inner) + block.shape)
    return jnp.swapaxes(held, 0, 1).reshape((count,) + block.shape), across


def per_device(q_proj, k_proj, v_proj, grad_out, w_first, w_second, decay_rate, skip_gain):
    height, chan_tp = q_proj.shape
    parts = lax.axis_size("seq")
    length = height * parts
    width = chan_tp // parts
    band_total, hidden_count = w_first.shape
    seq_index = lax.axis_index("seq")

    def exchange(values):
        return lax.all_to_all(values, "seq", split_axis=0, concat_axis=0, tiled=True)

    gated_in = exchange(gate(k_proj, v_proj, parts))
    gated_grad = gate(grad_out, q_proj, parts)

    tables = jnp.asarray(transform_tables(length, height))
    twiddle = jnp.asarray(twiddle_table(length, height))
    positional = positional_table(length, band_total // 2)
    sine_input = jnp.dot(
        w_first.T, positional, precision=HIGH, preferred_element_type=jnp.float32
    )
    hidden = jnp.sin(sine_input)
    cosine = jnp.cos(sine_input)
    offset = seq_index * width
    w_mine = lax.dynamic_slice_in_dim(w_second, offset, width, 1)
    decay_mine = lax.dynamic_slice_in_dim(decay_rate, offset, width, 0)[:, None]
    skip_mine = lax.dynamic_slice_in_dim(skip_gain, offset, width, 0)[:, None]

    spectrum_shape = jax.ShapeDtypeStruct((parts, width, 2 * height), jnp.float32)
    work = pltpu.VMEM(spectrum_shape.shape, jnp.float32)
    split = pltpu.VMEM((2, 6 * height, 2 * height), jnp.bfloat16)
    anywhere = pl.BlockSpec(memory_space=pl.ANY)
    in_vmem = pl.BlockSpec(memory_space=pltpu.VMEM)
    product_flops = 2 * 3 * parts * 4 * height * height * width

    long_filter, filter_spectrum = pl.pallas_call(
        filter_kernel,
        in_specs=[in_vmem] * 5,
        out_specs=[in_vmem, in_vmem],
        out_shape=[jax.ShapeDtypeStruct((width, length), jnp.float32), spectrum_shape],
        scratch_shapes=[work, split],
        compiler_params=params(),
        cost_estimate=estimate(1000, 1000),
    )(w_mine.T, hidden, decay_mine, tables, twiddle)

    gated_grad, long_filter, filter_spectrum, w_mine, skip_mine, positional = (
        lax.optimization_barrier(
            (gated_grad, long_filter, filter_spectrum, w_mine, skip_mine, positional)
        )
    )
    gated_grad = exchange(gated_grad)
    sems = pltpu.SemaphoreType.DMA((2,))
    block_shape = jax.ShapeDtypeStruct(gated_in.shape, jnp.bfloat16)

    convolved, in_spectrum = pl.pallas_call(
        conv_kernel,
        in_specs=[in_vmem, anywhere, in_vmem, in_vmem, in_vmem],
        out_specs=[in_vmem, anywhere],
        out_shape=[block_shape, spectrum_shape],
        scratch_shapes=[work, work, work, split, sems],
        compiler_params=params(),
        cost_estimate=estimate(2 * product_flops, length * width * 20),
    )(gated_in, filter_spectrum, tables, twiddle, skip_mine)
    conv_back = exchange(convolved)

    grad_gated, small, first_pair = pl.pallas_call(
        grad_kernel,
        in_specs=[in_vmem, in_vmem, anywhere, anywhere, anywhere] + [in_vmem] * 8,
        out_specs=[in_vmem, in_vmem, in_vmem],
        out_shape=[
            block_shape,
            jax.ShapeDtypeStruct((hidden_count + 16, width), jnp.bfloat16),
            jax.ShapeDtypeStruct((2 * band_total, hidden_count), jnp.bfloat16),
        ],
        scratch_shapes=[
            work,
            work,
            work,
            pltpu.VMEM((width, length), jnp.float32),
            pltpu.VMEM((2, width, height), jnp.float32),
            split,
            pltpu.SemaphoreType.DMA((3,)),
        ],
        compiler_params=params(),
        cost_estimate=estimate(3 * product_flops, length * width * 20),
    )(
        gated_in,
        gated_grad,
        in_spectrum,
        filter_spectrum,
        long_filter,
        tables,
        twiddle,
        skip_mine,
        decay_mine,
        hidden,
        w_mine,
        cosine,
        positional,
    )
    packed = jnp.concatenate([small, first_pair.reshape(-1, width)], axis=0)
    gathered, across = gather_all(packed, parts, seq_index, math.gcd(parts, 4))
    grad_gated, _ = lax.optimization_barrier((grad_gated, across))
    grad_back = exchange(grad_gated)
    second = gathered[:, :hidden_count].astype(jnp.float32)
    grad_second = second.transpose(1, 0, 2).reshape(hidden_count, chan_tp)
    tail = gathered[:, hidden_count : hidden_count + 4].astype(jnp.float32)
    grad_decay = (tail[:, 0] + tail[:, 1]).reshape(chan_tp)
    grad_skip = (tail[:, 2] + tail[:, 3]).reshape(chan_tp)
    first_rows = gathered[:, hidden_count + 16 :].astype(jnp.float32).sum(axis=0)
    grad_first = first_rows.reshape(2, band_total, hidden_count).sum(axis=0)
    if lax.axis_size("tp") == 2:
        grad_first = grad_first + lax.ppermute(grad_first, "tp", [(0, 1), (1, 0)])
    else:
        grad_first = lax.psum(grad_first, "tp")
    (grad_q,) = ungate(conv_back, (grad_out,))
    grad_k, grad_v = ungate(grad_back, (v_proj, k_proj))
    return (grad_q, grad_k, grad_v, grad_first, grad_second, grad_decay, grad_skip)


def solution(mesh):
    return jax.shard_map(
        per_device,
        mesh=mesh,
        in_specs=(
            P("seq", "tp"),
            P("seq", "tp"),
            P("seq", "tp"),
            P("seq", "tp"),
            P(),
            P(None, "tp"),
            P("tp"),
            P("tp"),
        ),
        out_specs=(
            P("seq", "tp"),
            P("seq", "tp"),
            P("seq", "tp"),
            P(),
            P(None, "tp"),
            P("tp"),
            P("tp"),
        ),
        check_vma=False,
    )
```

```python
import functools
import math

import jax
import jax.numpy as jnp
import ml_dtypes
import numpy as np
from jax import lax
from jax.experimental import pallas as pl
from jax.experimental.pallas import tpu as pltpu
from jax.sharding import PartitionSpec as P

HIGH = lax.Precision.HIGHEST
MIB = 1024 * 1024


def positional_table(length, band_count):
    positions = jnp.arange(length, dtype=jnp.int32)
    band_index = jnp.arange(band_count, dtype=jnp.int32)
    frequency = 3 * (band_index + 1) * (band_index + 1) + band_index
    phase_index = frequency[:, None] * positions[None, :] % length
    angles = phase_index.astype(jnp.float32) * (2.0 * math.pi / length)
    return jnp.concatenate([jnp.sin(angles), jnp.cos(angles)], axis=0)


@functools.lru_cache(maxsize=None)
def transform_tables(length, height):
    j = np.arange(height)
    angles = (j[:, None] * j[None, :] % height) * (2.0 * np.pi / height)
    cosine, sine = np.cos(angles), np.sin(angles)
    forward = np.concatenate(
        [np.concatenate([cosine, -sine], axis=1), np.concatenate([sine, cosine], axis=1)], axis=0
    )
    return np.stack([forward, forward.T / length]).astype(np.float32)


@functools.lru_cache(maxsize=None)
def twiddle_table(length, height):
    parts = length // height
    r = np.arange(parts)[:, None]
    j = np.arange(height)[None, :]
    angles = (j * (4 * r + 1) % (4 * length)) * (2.0 * np.pi / (4 * length))
    return np.concatenate([np.cos(angles), -np.sin(angles)], axis=1).astype(np.float32)


def turn(value, cosine, sine):
    real, imag = value
    return (real * cosine - imag * sine, real * sine + imag * cosine)


def small_fft(values, sign):
    count = len(values)
    if count == 1:
        return values
    even = small_fft(values[0::2], sign)
    odd = small_fft(values[1::2], sign)
    first, second = [], []
    for k in range(count // 2):
        real, imag = odd[k]
        if k == 0:
            pass
        elif 4 * k == count:
            real, imag = (-imag, real) if sign > 0 else (imag, -real)
        elif 8 * k == count:
            half = math.sqrt(0.5)
            if sign > 0:
                real, imag = (real - imag) * half, (real + imag) * half
            else:
                real, imag = (real + imag) * half, (imag - real) * half
        elif 8 * k == 3 * count:
            half = math.sqrt(0.5)
            if sign > 0:
                real, imag = (real + imag) * -half, (real - imag) * half
            else:
                real, imag = (imag - real) * half, (real + imag) * -half
        else:
            angle = sign * 2.0 * math.pi * k / count
            real, imag = turn((real, imag), math.cos(angle), math.sin(angle))
        base_real, base_imag = even[k]
        first.append((base_real + real, base_imag + imag))
        second.append((base_real - real, base_imag - imag))
    return first + second


def parts_forward(values):
    count = len(values)
    turned = []
    for p, value in enumerate(values):
        angle = 2.0 * math.pi * p / (4 * count)
        turned.append((value * math.cos(angle), value * -math.sin(angle)))
    return small_fft(turned, -1)


def parts_inverse(values):
    count = len(values)
    result = []
    for p, (real, imag) in enumerate(small_fft(values, 1)):
        angle = 2.0 * math.pi * p / (4 * count)
        result.append(real * math.cos(angle) - imag * math.sin(angle))
    return result


def split_bf16(value):
    high = value.astype(jnp.bfloat16)
    return high, (value - high.astype(jnp.float32)).astype(jnp.bfloat16)


def split_table(table_ref, split):
    size = table_ref.shape[1]
    for direction in range(2):
        high, low = split_bf16(table_ref[direction])
        split[direction, :size] = high
        split[direction, size : 2 * size] = high
        split[direction, 2 * size :] = low


def transform(value, split, direction):
    high, low = split_bf16(value)
    return jnp.dot(
        jnp.concatenate([high, low, high], axis=1),
        split[direction],
        preferred_element_type=jnp.float32,
    )


def spectrum_product(left, right, conjugate):
    height = left.shape[1] // 2
    left_real, left_imag = left[:, :height], left[:, height:]
    right_real, right_imag = right[:, :height], right[:, height:]
    if conjugate:
        real = left_real * right_real + left_imag * right_imag
        imag = left_real * right_imag - left_imag * right_real
    else:
        real = left_real * right_real - left_imag * right_imag
        imag = left_real * right_imag + left_imag * right_real
    return jnp.concatenate([real, imag], axis=1)


def first_chunk(load, work, twiddle_ref, index):
    parts, height = work.shape[0], work.shape[2] // 2
    row = pl.multiple_of(index * 16, 16)
    values = [load(p, row) for p in range(parts)]
    for half in (0, 8):
        rows = pl.ds(row + half, 8)
        turned = parts_forward([value[half : half + 8] for value in values])
        for r, value in enumerate(turned):
            cosine = twiddle_ref[r : r + 1, :height]
            sine = twiddle_ref[r : r + 1, height:]
            work[r, rows, :height], work[r, rows, height:] = turn(value, cosine, sine)


def last_chunk(store, work, twiddle_ref, index):
    parts, height = work.shape[0], work.shape[2] // 2
    row = pl.multiple_of(index * 16, 16)
    halves = []
    for half in (0, 8):
        rows = pl.ds(row + half, 8)
        values = []
        for r in range(parts):
            cosine = twiddle_ref[r : r + 1, :height]
            sine = twiddle_ref[r : r + 1, height:]
            value = (work[r, rows, :height], work[r, rows, height:])
            values.append(turn(value, cosine, -sine))
        halves.append(parts_inverse(values))
    for p in range(parts):
        store(p, row, jnp.concatenate([halves[0][p], halves[1][p]], axis=0))


GROUP = 4


def run_chunks(width, chunk, parts=0, block=None):
    chunks = width // 16
    per = math.gcd(chunks, GROUP)
    paired = parts * per == GROUP * chunks

    def one(index, carry):
        if paired:
            block(index * GROUP)
        for b in range(per):
            chunk(index * per + b)
        return carry

    lax.fori_loop(0, chunks // per, one, 0)
    if not paired and parts > 0:
        run_blocks(parts, block)


def run_blocks(parts, block):
    def one(index, carry):
        block(index * GROUP)
        return carry

    lax.fori_loop(0, parts // GROUP, one, 0)


def group_of(r):
    return pl.ds(pl.multiple_of(r, GROUP), GROUP)


def read_group(ref, r):
    _, width, columns = ref.shape
    return ref[group_of(r)].reshape(GROUP * width, columns)


def write_group(ref, r, value):
    ref[group_of(r)] = value.reshape((GROUP,) + ref.shape[1:])


def envelope_at(decay, start, length, height):
    position = (start + lax.broadcasted_iota(jnp.int32, (1, height), 1)).astype(jnp.float32)
    fraction = position * (1.0 / length)
    return jnp.exp(-decay * fraction), fraction


def columns_of(p, height):
    return slice(p * height, (p + 1) * height)


def filter_kernel(
    w_t_ref, hidden_ref, decay_ref, table_ref, twiddle_ref, filter_ref, spectrum_ref, work, split
):
    parts, width, height = work.shape[0], work.shape[1], work.shape[2] // 2
    length = filter_ref.shape[1]
    scale = length**-0.5
    split_table(table_ref, split)
    filter_ref[...] = jnp.dot(
        w_t_ref[...], hidden_ref[...], precision=HIGH, preferred_element_type=jnp.float32
    )

    def load(p, row):
        rows, columns = pl.ds(row, 16), columns_of(p, height)
        envelope, _ = envelope_at(decay_ref[rows, :], p * height, length, height)
        value = filter_ref[rows, columns] * envelope * scale
        filter_ref[rows, columns] = value
        return value

    def block(r):
        write_group(spectrum_ref, r, transform(read_group(work, r), split, 0))

    run_chunks(width, lambda i: first_chunk(load, work, twiddle_ref, i))
    run_blocks(parts, block)


def load_from(ref):
    def load(p, row):
        return ref[p, pl.ds(row, 16), :].astype(jnp.float32)

    return load


def store_to(ref, skip_ref, load):
    def store(p, row, value):
        value = value + skip_ref[pl.ds(row, 16), :] * load(p, row)
        ref[p, pl.ds(row, 16), :] = value.astype(jnp.bfloat16)

    return store


def conv_kernel(
    x_ref, h_any, table_ref, twiddle_ref, skip_ref, y_ref, x_any, work, spectra, h, split, sems
):
    parts, width = work.shape[0], work.shape[1]
    copy_in = pltpu.make_async_copy(h_any, h, sems.at[0])
    copy_in.start()
    split_table(table_ref, split)
    load = load_from(x_ref)

    def block(r):
        spectrum = transform(read_group(work, r), split, 0)
        write_group(spectra, r, spectrum)
        product = spectrum_product(read_group(h, r), spectrum, False)
        write_group(work, r, transform(product, split, 1))

    run_chunks(width, lambda i: first_chunk(load, work, twiddle_ref, i))
    copy_in.wait()
    run_blocks(parts, block)
    copy_out = pltpu.make_async_copy(spectra, x_any, sems.at[1])
    copy_out.start()
    store = store_to(y_ref, skip_ref, load)
    run_chunks(width, lambda i: last_chunk(store, work, twiddle_ref, i))
    copy_out.wait()


def grad_kernel(
    x_ref,
    g_ref,
    x_any,
    h_any,
    filter_any,
    table_ref,
    twiddle_ref,
    skip_ref,
    decay_ref,
    hidden_ref,
    w_ref,
    cosine_ref,
    positional_ref,
    z_ref,
    small_ref,
    first_ref,
    work,
    cross,
    h,
    raw,
    sums,
    split,
    sems,
):
    parts, height = work.shape[0], work.shape[2] // 2
    width, length = raw.shape
    hidden_count = hidden_ref.shape[0]
    scale = length**-0.5
    copies = [
        pltpu.make_async_copy(source, target, sems.at[at])
        for at, (source, target) in enumerate(((x_any, cross), (h_any, h), (filter_any, raw)))
    ]
    for copy in copies:
        copy.start()
    split_table(table_ref, split)
    load = load_from(g_ref)

    def block(r):
        spectrum = transform(read_group(work, r), split, 0)
        product = spectrum_product(read_group(h, r), spectrum, True)
        write_group(work, r, transform(product, split, 1))
        product = spectrum_product(read_group(cross, r), spectrum, True)
        write_group(cross, r, transform(product, split, 1))

    def store(p, row, value):
        rows, columns = pl.ds(row, 16), columns_of(p, height)
        envelope, fraction = envelope_at(decay_ref[rows, :], p * height, length, height)
        decay_part = value * raw[rows, columns] * fraction
        skip_part = load_from(x_ref)(p, row) * load(p, row)
        raw[rows, columns] = value * envelope * scale
        if p > 0:
            decay_part = decay_part + sums[0, rows, :]
            skip_part = skip_part + sums[1, rows, :]
        sums[0, rows, :] = decay_part
        sums[1, rows, :] = skip_part

    run_chunks(width, lambda i: first_chunk(load, work, twiddle_ref, i))
    for copy in copies:
        copy.wait()
    run_blocks(parts, block)
    store_z = store_to(z_ref, skip_ref, load)
    run_chunks(width, lambda i: last_chunk(store_z, work, twiddle_ref, i))
    run_chunks(width, lambda i: last_chunk(store, cross, twiddle_ref, i))

    def dot_pairs(left, right, along):
        def dot(one, two):
            return lax.dot_general(
                one, two, (((1,), (along,)), ((), ())), preferred_element_type=jnp.float32
            )

        return dot(left[0], right[0]) + (dot(left[0], right[1]) + dot(left[1], right[0]))

    second = jnp.zeros((hidden_count, width), jnp.float32)
    band_total = positional_ref.shape[0]
    first = jnp.zeros((band_total, hidden_count), jnp.float32)
    w_pair = split_bf16(w_ref[...])
    chunk = min(length, 512)
    for at in range(0, length, chunk):
        columns = slice(at, at + chunk)
        raw_pair = split_bf16(raw[:, columns])
        second += dot_pairs(split_bf16(hidden_ref[:, columns]), raw_pair, 1)
        hidden_part = dot_pairs(w_pair, raw_pair, 0) * cosine_ref[:, columns]
        first += dot_pairs(split_bf16(positional_ref[:, columns]), split_bf16(hidden_part), 1)

    first_pair = split_bf16(first * scale)
    first_ref[:band_total, :], first_ref[band_total:, :] = first_pair
    rows = small_ref.shape[0] - hidden_count - 16
    if rows > 0:
        stacked = jnp.concatenate([part.astype(jnp.float32) for part in first_pair], axis=0)
        pieces = [stacked[at : at + rows] for at in range(0, 2 * band_total, rows)]
        small_ref[hidden_count + 16 :, :] = jnp.concatenate(pieces, axis=1).astype(jnp.bfloat16)
    small_ref[:hidden_count, :] = (second * scale).astype(jnp.bfloat16)
    place = lax.broadcasted_iota(jnp.int32, (16, width), 0)
    tail = jnp.zeros((16, width), jnp.float32)
    decay_pair = split_bf16(jnp.sum(sums[0].T, axis=0, keepdims=True) * -scale)
    skip_pair = split_bf16(jnp.sum(sums[1].T, axis=0, keepdims=True) * scale)
    for at, row in enumerate(decay_pair + skip_pair):
        tail = jnp.where(place == at, row.astype(jnp.float32), tail)
    small_ref[hidden_count : hidden_count + 16, :] = tail.astype(jnp.bfloat16)


def params(limit=63):
    return pltpu.CompilerParams(vmem_limit_bytes=limit * MIB)


def estimate(flops, nbytes):
    return pl.CostEstimate(flops=flops, bytes_accessed=nbytes, transcendentals=0)


def chunk_copies(pairs, sems, first):
    return [
        [
            pltpu.make_async_copy(source, target, sems.at[first + at * len(chunk) + which])
            for which, (source, target) in enumerate(chunk)
        ]
        for at, chunk in enumerate(pairs)
    ]


def run_streams(blocks, group, width, shared, wide_in, wide_out, shared_out, sems, work):
    def part(refs, at):
        return [ref.at[pl.ds(at * group, group)] for ref in refs]

    def lanes(refs, at):
        return [ref.at[:, pl.ds(at * group * width, group * width)] for ref in refs]

    chunks = range(blocks // group)
    incoming, outgoing = [], []
    for at in chunks:
        pairs = [tuple(part(pair, at)) for pair in shared]
        incoming.append(pairs + [tuple(lanes(pair, at)) for pair in wide_in])
        pairs = [tuple(part(pair, at)) for pair in shared_out]
        outgoing.append(pairs + [tuple(lanes(pair, at)) for pair in wide_out])
    arrivals = chunk_copies(incoming, sems, 0)
    departures = chunk_copies(outgoing, sems, len(arrivals) * len(arrivals[0]))
    for chunk in arrivals:
        for copy in chunk:
            copy.start()
    for at in chunks:
        for copy in arrivals[at]:
            copy.wait()
        for block in range(at * group, (at + 1) * group):
            work(block, slice(block * width, (block + 1) * width))
        for copy in departures[at]:
            copy.start()
    for chunk in departures:
        for copy in chunk:
            copy.wait()


def gate_kernel(group, left_any, right_any, out_any, left_ref, right_ref, out_ref, sems):
    count, width, _ = out_ref.shape

    def work(block, lanes):
        left = left_ref[:, lanes].astype(jnp.float32)
        right = right_ref[:, lanes].astype(jnp.float32)
        out_ref[block] = (left * right).T.astype(jnp.bfloat16)

    wide = [(left_any, left_ref), (right_any, right_ref)]
    run_streams(count, group, width, [], wide, [], [(out_ref, out_any)], sems, work)


def gate(left, right, count):
    rows, columns = left.shape
    width = columns // count
    if width % 128 != 0:
        product = (left.astype(jnp.float32) * right.astype(jnp.float32)).astype(jnp.bfloat16)
        return product.reshape(rows, count, width).transpose(1, 2, 0)
    group = math.gcd(count, 2)
    out = jax.ShapeDtypeStruct((count, width, rows), jnp.bfloat16)
    wide = pltpu.VMEM((rows, columns), jnp.bfloat16)
    return pl.pallas_call(
        functools.partial(gate_kernel, group),
        in_specs=[pl.BlockSpec(memory_space=pl.ANY)] * 2,
        out_specs=pl.BlockSpec(memory_space=pl.ANY),
        out_shape=out,
        scratch_shapes=[
            wide,
            wide,
            pltpu.VMEM(out.shape, jnp.bfloat16),
            pltpu.SemaphoreType.DMA((3 * count // group,)),
        ],
        compiler_params=params(),
        cost_estimate=estimate(rows * columns, rows * columns * 6),
    )(left, right)


def ungate_kernel(group, factors, *refs):
    back_any, factor_anys = refs[0], refs[1 : factors + 1]
    out_anys = refs[factors + 1 : 2 * factors + 1]
    back_ref, *rest = refs[2 * factors + 1 :]
    factor_refs, out_refs, sems = rest[:factors], rest[factors:-1], rest[-1]
    count, width, _ = back_ref.shape

    def work(block, lanes):
        back = back_ref[block].astype(jnp.float32).T
        for factor_ref, out_ref in zip(factor_refs, out_refs):
            factor = factor_ref[:, lanes].astype(jnp.float32)
            out_ref[:, lanes] = (back * factor).astype(jnp.bfloat16)

    shared = [(back_any, back_ref)]
    wide_in = list(zip(factor_anys, factor_refs))
    wide_out = list(zip(out_refs, out_anys))
    run_streams(count, group, width, shared, wide_in, wide_out, [], sems, work)


def ungate(back, factors):
    count, width, rows = back.shape
    columns = count * width
    if width % 128 != 0:
        part = back.transpose(2, 0, 1).reshape(rows, columns).astype(jnp.float32)
        return [(part * factor.astype(jnp.float32)).astype(jnp.bfloat16) for factor in factors]
    group = math.gcd(count, 2)
    anywhere = pl.BlockSpec(memory_space=pl.ANY)
    wide = pltpu.VMEM((rows, columns), jnp.bfloat16)
    copies = (1 + 2 * len(factors)) * count // group
    return pl.pallas_call(
        functools.partial(ungate_kernel, group, len(factors)),
        in_specs=[anywhere] * (1 + len(factors)),
        out_specs=[anywhere] * len(factors),
        out_shape=[jax.ShapeDtypeStruct((rows, columns), jnp.bfloat16)] * len(factors),
        scratch_shapes=[pltpu.VMEM(back.shape, jnp.bfloat16)]
        + [wide] * (2 * len(factors))
        + [pltpu.SemaphoreType.DMA((copies,))],
        compiler_params=params(),
        cost_estimate=estimate(rows * columns, rows * columns * (2 + 4 * len(factors))),
    )(back, *factors)


def gather_all(block, count, index, inner):
    def swaps(held, masks):
        received = [held]
        for mask in masks:
            pairs = [(i, i ^ mask) for i in range(count)]
            received.append(lax.ppermute(held, "seq", pairs))
        return jnp.stack(received)

    across = swaps(block, range(inner, count, inner))
    held = swaps(across, range(1, inner))
    bits = count.bit_length() - 1
    inner_bits = inner.bit_length() - 1
    held = held.reshape((2,) * bits + block.shape)
    for axis in range(bits):
        bit = inner_bits - 1 - axis if axis < inner_bits else bits - 1 - (axis - inner_bits)
        held = jnp.where((index >> bit) % 2 == 1, jnp.flip(held, axis), held)
    held = held.reshape((inner, count // inner) + block.shape)
    return jnp.swapaxes(held, 0, 1).reshape((count,) + block.shape), across


def per_device(q_proj, k_proj, v_proj, grad_out, w_first, w_second, decay_rate, skip_gain):
    height, chan_tp = q_proj.shape
    parts = lax.axis_size("seq")
    length = height * parts
    width = chan_tp // parts
    band_total, hidden_count = w_first.shape
    seq_index = lax.axis_index("seq")

    def exchange(values):
        return lax.all_to_all(values, "seq", split_axis=0, concat_axis=0, tiled=True)

    gated_in = exchange(gate(k_proj, v_proj, parts))
    gated_grad = gate(grad_out, q_proj, parts)

    tables = jnp.asarray(transform_tables(length, height))
    twiddle = jnp.asarray(twiddle_table(length, height))
    positional = positional_table(length, band_total // 2)
    sine_input = jnp.dot(
        w_first.T, positional, precision=HIGH, preferred_element_type=jnp.float32
    )
    hidden = jnp.sin(sine_input)
    cosine = jnp.cos(sine_input)
    offset = seq_index * width
    w_mine = lax.dynamic_slice_in_dim(w_second, offset, width, 1)
    decay_mine = lax.dynamic_slice_in_dim(decay_rate, offset, width, 0)[:, None]
    skip_mine = lax.dynamic_slice_in_dim(skip_gain, offset, width, 0)[:, None]

    spectrum_shape = jax.ShapeDtypeStruct((parts, width, 2 * height), jnp.float32)
    work = pltpu.VMEM(spectrum_shape.shape, jnp.float32)
    split = pltpu.VMEM((2, 6 * height, 2 * height), jnp.bfloat16)
    anywhere = pl.BlockSpec(memory_space=pl.ANY)
    in_vmem = pl.BlockSpec(memory_space=pltpu.VMEM)
    product_flops = 2 * 3 * parts * 4 * height * height * width

    long_filter, filter_spectrum = pl.pallas_call(
        filter_kernel,
        in_specs=[in_vmem] * 5,
        out_specs=[in_vmem, in_vmem],
        out_shape=[jax.ShapeDtypeStruct((width, length), jnp.float32), spectrum_shape],
        scratch_shapes=[work, split],
        compiler_params=params(),
        cost_estimate=estimate(1000, 1000),
    )(w_mine.T, hidden, decay_mine, tables, twiddle)

    gated_grad, long_filter, filter_spectrum, w_mine, skip_mine, positional = (
        lax.optimization_barrier(
            (gated_grad, long_filter, filter_spectrum, w_mine, skip_mine, positional)
        )
    )
    gated_grad = exchange(gated_grad)
    sems = pltpu.SemaphoreType.DMA((2,))
    block_shape = jax.ShapeDtypeStruct(gated_in.shape, jnp.bfloat16)

    convolved, in_spectrum = pl.pallas_call(
        conv_kernel,
        in_specs=[in_vmem, anywhere, in_vmem, in_vmem, in_vmem],
        out_specs=[in_vmem, anywhere],
        out_shape=[block_shape, spectrum_shape],
        scratch_shapes=[work, work, work, split, sems],
        compiler_params=params(),
        cost_estimate=estimate(2 * product_flops, length * width * 20),
    )(gated_in, filter_spectrum, tables, twiddle, skip_mine)
    conv_back = exchange(convolved)

    pieces = width // hidden_count
    packs = width % hidden_count == 0 and 2 * band_total % (16 * pieces) == 0
    first_count = 2 * band_total // pieces if packs else 0
    grad_gated, small, first_pair = pl.pallas_call(
        grad_kernel,
        in_specs=[in_vmem, in_vmem, anywhere, anywhere, anywhere] + [in_vmem] * 8,
        out_specs=[in_vmem, in_vmem, in_vmem],
        out_shape=[
            block_shape,
            jax.ShapeDtypeStruct((hidden_count + 16 + first_count, width), jnp.bfloat16),
            jax.ShapeDtypeStruct((2 * band_total, hidden_count), jnp.bfloat16),
        ],
        scratch_shapes=[
            work,
            work,
            work,
            pltpu.VMEM((width, length), jnp.float32),
            pltpu.VMEM((2, width, height), jnp.float32),
            split,
            pltpu.SemaphoreType.DMA((3,)),
        ],
        compiler_params=params(),
        cost_estimate=estimate(3 * product_flops, length * width * 20),
    )(
        gated_in,
        gated_grad,
        in_spectrum,
        filter_spectrum,
        long_filter,
        tables,
        twiddle,
        skip_mine,
        decay_mine,
        hidden,
        w_mine,
        cosine,
        positional,
    )
    packed = small
    if not packs:
        packed = jnp.concatenate([small, first_pair.reshape(-1, width)], axis=0)
    gathered, across = gather_all(packed, parts, seq_index, math.gcd(parts, 4))
    grad_gated, _ = lax.optimization_barrier((grad_gated, across))
    grad_back = exchange(grad_gated)
    second = gathered[:, :hidden_count].astype(jnp.float32)
    grad_second = second.transpose(1, 0, 2).reshape(hidden_count, chan_tp)
    tail = gathered[:, hidden_count : hidden_count + 4].astype(jnp.float32)
    grad_decay = (tail[:, 0] + tail[:, 1]).reshape(chan_tp)
    grad_skip = (tail[:, 2] + tail[:, 3]).reshape(chan_tp)
    first_rows = gathered[:, hidden_count + 16 :].astype(jnp.float32).sum(axis=0)
    if packs:
        first_rows = first_rows.reshape(first_count, pieces, hidden_count).transpose(1, 0, 2)
    grad_first = first_rows.reshape(2, band_total, hidden_count).sum(axis=0)
    if lax.axis_size("tp") == 2:
        grad_first = grad_first + lax.ppermute(grad_first, "tp", [(0, 1), (1, 0)])
    else:
        grad_first = lax.psum(grad_first, "tp")
    (grad_q,) = ungate(conv_back, (grad_out,))
    grad_k, grad_v = ungate(grad_back, (v_proj, k_proj))
    return (grad_q, grad_k, grad_v, grad_first, grad_second, grad_decay, grad_skip)


def solution(mesh):
    return jax.shard_map(
        per_device,
        mesh=mesh,
        in_specs=(
            P("seq", "tp"),
            P("seq", "tp"),
            P("seq", "tp"),
            P("seq", "tp"),
            P(),
            P(None, "tp"),
            P("tp"),
            P("tp"),
        ),
        out_specs=(
            P("seq", "tp"),
            P("seq", "tp"),
            P("seq", "tp"),
            P(),
            P(None, "tp"),
            P("tp"),
            P("tp"),
        ),
        check_vma=False,
    )
```

```python
import functools
import math

import jax
import jax.numpy as jnp
import ml_dtypes
import numpy as np
from jax import lax
from jax.experimental import pallas as pl
from jax.experimental.pallas import tpu as pltpu
from jax.sharding import PartitionSpec as P

HIGH = lax.Precision.HIGHEST
MIB = 1024 * 1024


def positional_table(length, band_count):
    positions = jnp.arange(length, dtype=jnp.int32)
    band_index = jnp.arange(band_count, dtype=jnp.int32)
    frequency = 3 * (band_index + 1) * (band_index + 1) + band_index
    phase_index = frequency[:, None] * positions[None, :] % length
    angles = phase_index.astype(jnp.float32) * (2.0 * math.pi / length)
    return jnp.concatenate([jnp.sin(angles), jnp.cos(angles)], axis=0)


@functools.lru_cache(maxsize=None)
def transform_tables(length, height):
    j = np.arange(height)
    angles = (j[:, None] * j[None, :] % height) * (2.0 * np.pi / height)
    cosine, sine = np.cos(angles), np.sin(angles)
    forward = np.concatenate(
        [np.concatenate([cosine, -sine], axis=1), np.concatenate([sine, cosine], axis=1)], axis=0
    )
    return np.stack([forward, forward.T / length]).astype(np.float32)


@functools.lru_cache(maxsize=None)
def twiddle_table(length, height):
    parts = length // height
    r = np.arange(parts)[:, None]
    j = np.arange(height)[None, :]
    angles = (j * (4 * r + 1) % (4 * length)) * (2.0 * np.pi / (4 * length))
    return np.concatenate([np.cos(angles), -np.sin(angles)], axis=1).astype(np.float32)


def turn(value, cosine, sine):
    real, imag = value
    return (real * cosine - imag * sine, real * sine + imag * cosine)


def small_fft(values, sign):
    count = len(values)
    if count == 1:
        return values
    even = small_fft(values[0::2], sign)
    odd = small_fft(values[1::2], sign)
    first, second = [], []
    for k in range(count // 2):
        real, imag = odd[k]
        if k == 0:
            pass
        elif 4 * k == count:
            real, imag = (-imag, real) if sign > 0 else (imag, -real)
        elif 8 * k == count:
            half = math.sqrt(0.5)
            if sign > 0:
                real, imag = (real - imag) * half, (real + imag) * half
            else:
                real, imag = (real + imag) * half, (imag - real) * half
        elif 8 * k == 3 * count:
            half = math.sqrt(0.5)
            if sign > 0:
                real, imag = (real + imag) * -half, (real - imag) * half
            else:
                real, imag = (imag - real) * half, (real + imag) * -half
        else:
            angle = sign * 2.0 * math.pi * k / count
            real, imag = turn((real, imag), math.cos(angle), math.sin(angle))
        base_real, base_imag = even[k]
        first.append((base_real + real, base_imag + imag))
        second.append((base_real - real, base_imag - imag))
    return first + second


def parts_forward(values):
    count = len(values)
    turned = []
    for p, value in enumerate(values):
        angle = 2.0 * math.pi * p / (4 * count)
        turned.append((value * math.cos(angle), value * -math.sin(angle)))
    return small_fft(turned, -1)


def parts_inverse(values):
    count = len(values)
    result = []
    for p, (real, imag) in enumerate(small_fft(values, 1)):
        angle = 2.0 * math.pi * p / (4 * count)
        result.append(real * math.cos(angle) - imag * math.sin(angle))
    return result


def split_bf16(value):
    high = value.astype(jnp.bfloat16)
    return high, (value - high.astype(jnp.float32)).astype(jnp.bfloat16)


def split_table(table_ref, split):
    size = table_ref.shape[1]
    for direction in range(2):
        high, low = split_bf16(table_ref[direction])
        split[direction, :size] = high
        split[direction, size : 2 * size] = high
        split[direction, 2 * size :] = low


def transform(value, split, direction):
    high, low = split_bf16(value)
    return jnp.dot(
        jnp.concatenate([high, low, high], axis=1),
        split[direction],
        preferred_element_type=jnp.float32,
    )


def spectrum_product(left, right, conjugate):
    height = left.shape[1] // 2
    left_real, left_imag = left[:, :height], left[:, height:]
    right_real, right_imag = right[:, :height], right[:, height:]
    if conjugate:
        real = left_real * right_real + left_imag * right_imag
        imag = left_real * right_imag - left_imag * right_real
    else:
        real = left_real * right_real - left_imag * right_imag
        imag = left_real * right_imag + left_imag * right_real
    return jnp.concatenate([real, imag], axis=1)


def first_chunk(load, work, twiddle_ref, index):
    parts, height = work.shape[0], work.shape[2] // 2
    row = pl.multiple_of(index * 16, 16)
    values = [load(p, row) for p in range(parts)]
    for half in (0, 8):
        rows = pl.ds(row + half, 8)
        turned = parts_forward([value[half : half + 8] for value in values])
        for r, value in enumerate(turned):
            cosine = twiddle_ref[r : r + 1, :height]
            sine = twiddle_ref[r : r + 1, height:]
            work[r, rows, :height], work[r, rows, height:] = turn(value, cosine, sine)


def last_chunk(store, work, twiddle_ref, index):
    parts, height = work.shape[0], work.shape[2] // 2
    row = pl.multiple_of(index * 16, 16)
    halves = []
    for half in (0, 8):
        rows = pl.ds(row + half, 8)
        values = []
        for r in range(parts):
            cosine = twiddle_ref[r : r + 1, :height]
            sine = twiddle_ref[r : r + 1, height:]
            value = (work[r, rows, :height], work[r, rows, height:])
            values.append(turn(value, cosine, -sine))
        halves.append(parts_inverse(values))
    for p in range(parts):
        store(p, row, jnp.concatenate([halves[0][p], halves[1][p]], axis=0))


GROUP = 4


def run_chunks(width, chunk, parts=0, block=None):
    chunks = width // 16
    per = math.gcd(chunks, GROUP)
    paired = parts * per == GROUP * chunks

    def one(index, carry):
        if paired:
            block(index * GROUP)
        for b in range(per):
            chunk(index * per + b)
        return carry

    lax.fori_loop(0, chunks // per, one, 0)
    if not paired and parts > 0:
        run_blocks(parts, block)


def run_blocks(parts, block):
    def one(index, carry):
        block(index * GROUP)
        return carry

    lax.fori_loop(0, parts // GROUP, one, 0)


def group_of(r):
    return pl.ds(pl.multiple_of(r, GROUP), GROUP)


def read_group(ref, r):
    _, width, columns = ref.shape
    return ref[group_of(r)].reshape(GROUP * width, columns)


def write_group(ref, r, value):
    ref[group_of(r)] = value.reshape((GROUP,) + ref.shape[1:])


def envelope_at(decay, start, length, height):
    position = (start + lax.broadcasted_iota(jnp.int32, (1, height), 1)).astype(jnp.float32)
    fraction = position * (1.0 / length)
    return jnp.exp(-decay * fraction), fraction


def columns_of(p, height):
    return slice(p * height, (p + 1) * height)


def filter_kernel(
    w_t_ref, hidden_ref, decay_ref, table_ref, twiddle_ref, filter_ref, spectrum_ref, work, split
):
    parts, width, height = work.shape[0], work.shape[1], work.shape[2] // 2
    length = filter_ref.shape[1]
    scale = length**-0.5
    split_table(table_ref, split)
    filter_ref[...] = jnp.dot(
        w_t_ref[...], hidden_ref[...], precision=HIGH, preferred_element_type=jnp.float32
    )

    def load(p, row):
        rows, columns = pl.ds(row, 16), columns_of(p, height)
        envelope, _ = envelope_at(decay_ref[rows, :], p * height, length, height)
        value = filter_ref[rows, columns] * envelope * scale
        filter_ref[rows, columns] = value
        return value

    def block(r):
        write_group(spectrum_ref, r, transform(read_group(work, r), split, 0))

    run_chunks(width, lambda i: first_chunk(load, work, twiddle_ref, i))
    run_blocks(parts, block)


def load_from(ref):
    def load(p, row):
        return ref[p, pl.ds(row, 16), :].astype(jnp.float32)

    return load


def store_to(ref, skip_ref, load):
    def store(p, row, value):
        value = value + skip_ref[pl.ds(row, 16), :] * load(p, row)
        ref[p, pl.ds(row, 16), :] = value.astype(jnp.bfloat16)

    return store


def conv_kernel(
    x_ref, h_any, table_ref, twiddle_ref, skip_ref, y_ref, x_any, work, spectra, h, split, sems
):
    parts, width = work.shape[0], work.shape[1]
    copy_in = pltpu.make_async_copy(h_any, h, sems.at[0])
    copy_in.start()
    split_table(table_ref, split)
    load = load_from(x_ref)

    def block(r):
        spectrum = transform(read_group(work, r), split, 0)
        write_group(spectra, r, spectrum)
        product = spectrum_product(read_group(h, r), spectrum, False)
        write_group(work, r, transform(product, split, 1))

    run_chunks(width, lambda i: first_chunk(load, work, twiddle_ref, i))
    copy_in.wait()
    run_blocks(parts, block)
    copy_out = pltpu.make_async_copy(spectra, x_any, sems.at[1])
    copy_out.start()
    store = store_to(y_ref, skip_ref, load)
    run_chunks(width, lambda i: last_chunk(store, work, twiddle_ref, i))
    copy_out.wait()


def grad_kernel(
    x_ref,
    g_ref,
    x_any,
    h_any,
    filter_any,
    table_ref,
    twiddle_ref,
    skip_ref,
    decay_ref,
    hidden_ref,
    w_ref,
    cosine_ref,
    positional_ref,
    z_ref,
    small_ref,
    first_ref,
    work,
    cross,
    h,
    raw,
    sums,
    split,
    sems,
):
    parts, height = work.shape[0], work.shape[2] // 2
    width, length = raw.shape
    hidden_count = hidden_ref.shape[0]
    scale = length**-0.5
    copies = [
        pltpu.make_async_copy(source, target, sems.at[at])
        for at, (source, target) in enumerate(((x_any, cross), (h_any, h), (filter_any, raw)))
    ]
    for copy in copies:
        copy.start()
    split_table(table_ref, split)
    load = load_from(g_ref)

    def block(r):
        spectrum = transform(read_group(work, r), split, 0)
        product = spectrum_product(read_group(h, r), spectrum, True)
        write_group(work, r, transform(product, split, 1))
        product = spectrum_product(read_group(cross, r), spectrum, True)
        write_group(cross, r, transform(product, split, 1))

    def store(p, row, value):
        rows, columns = pl.ds(row, 16), columns_of(p, height)
        envelope, fraction = envelope_at(decay_ref[rows, :], p * height, length, height)
        decay_part = value * raw[rows, columns] * fraction
        skip_part = load_from(x_ref)(p, row) * load(p, row)
        raw[rows, columns] = value * envelope * scale
        if p > 0:
            decay_part = decay_part + sums[0, rows, :]
            skip_part = skip_part + sums[1, rows, :]
        sums[0, rows, :] = decay_part
        sums[1, rows, :] = skip_part

    run_chunks(width, lambda i: first_chunk(load, work, twiddle_ref, i))
    for copy in copies:
        copy.wait()
    run_blocks(parts, block)
    store_z = store_to(z_ref, skip_ref, load)
    run_chunks(width, lambda i: last_chunk(store_z, work, twiddle_ref, i))
    run_chunks(width, lambda i: last_chunk(store, cross, twiddle_ref, i))

    def dot_pairs(left, right, along):
        def dot(one, two):
            return lax.dot_general(
                one, two, (((1,), (along,)), ((), ())), preferred_element_type=jnp.float32
            )

        return dot(left[0], right[0]) + (dot(left[0], right[1]) + dot(left[1], right[0]))

    second = jnp.zeros((hidden_count, width), jnp.float32)
    band_total = positional_ref.shape[0]
    first = jnp.zeros((band_total, hidden_count), jnp.float32)
    w_pair = split_bf16(w_ref[...])
    chunk = min(length, 512)
    for at in range(0, length, chunk):
        columns = slice(at, at + chunk)
        raw_pair = split_bf16(raw[:, columns])
        second += dot_pairs(split_bf16(hidden_ref[:, columns]), raw_pair, 1)
        hidden_part = dot_pairs(w_pair, raw_pair, 0) * cosine_ref[:, columns]
        first += dot_pairs(split_bf16(positional_ref[:, columns]), split_bf16(hidden_part), 1)

    first_pair = split_bf16(first * scale)
    first_ref[:band_total, :], first_ref[band_total:, :] = first_pair
    rows = small_ref.shape[0] - hidden_count - 16
    if rows > 0:
        stacked = jnp.concatenate([part.astype(jnp.float32) for part in first_pair], axis=0)
        pieces = [stacked[at : at + rows] for at in range(0, 2 * band_total, rows)]
        small_ref[hidden_count + 16 :, :] = jnp.concatenate(pieces, axis=1).astype(jnp.bfloat16)
    small_ref[:hidden_count, :] = (second * scale).astype(jnp.bfloat16)
    place = lax.broadcasted_iota(jnp.int32, (16, width), 0)
    tail = jnp.zeros((16, width), jnp.float32)
    decay_pair = split_bf16(jnp.sum(sums[0].T, axis=0, keepdims=True) * -scale)
    skip_pair = split_bf16(jnp.sum(sums[1].T, axis=0, keepdims=True) * scale)
    for at, row in enumerate(decay_pair + skip_pair):
        tail = jnp.where(place == at, row.astype(jnp.float32), tail)
    small_ref[hidden_count : hidden_count + 16, :] = tail.astype(jnp.bfloat16)


def params(limit=63):
    return pltpu.CompilerParams(vmem_limit_bytes=limit * MIB)


def estimate(flops, nbytes):
    return pl.CostEstimate(flops=flops, bytes_accessed=nbytes, transcendentals=0)


def chunk_copies(pairs, sems, first):
    return [
        [
            pltpu.make_async_copy(source, target, sems.at[first + at * len(chunk) + which])
            for which, (source, target) in enumerate(chunk)
        ]
        for at, chunk in enumerate(pairs)
    ]


def run_streams(blocks, group, width, shared, wide_in, wide_out, shared_out, sems, work):
    def part(refs, at):
        return [ref.at[pl.ds(at * group, group)] for ref in refs]

    def lanes(refs, at):
        return [ref.at[:, pl.ds(at * group * width, group * width)] for ref in refs]

    chunks = range(blocks // group)
    incoming, outgoing = [], []
    for at in chunks:
        pairs = [tuple(part(pair, at)) for pair in shared]
        incoming.append(pairs + [tuple(lanes(pair, at)) for pair in wide_in])
        pairs = [tuple(part(pair, at)) for pair in shared_out]
        outgoing.append(pairs + [tuple(lanes(pair, at)) for pair in wide_out])
    arrivals = chunk_copies(incoming, sems, 0)
    departures = chunk_copies(outgoing, sems, len(arrivals) * len(arrivals[0]))
    for chunk in arrivals:
        for copy in chunk:
            copy.start()
    for at in chunks:
        for copy in arrivals[at]:
            copy.wait()
        for block in range(at * group, (at + 1) * group):
            work(block, slice(block * width, (block + 1) * width))
        for copy in departures[at]:
            copy.start()
    for chunk in departures:
        for copy in chunk:
            copy.wait()


def gate_kernel(group, left_any, right_any, out_any, left_ref, right_ref, out_ref, sems):
    count, width, _ = out_ref.shape

    def work(block, lanes):
        left = left_ref[:, lanes].astype(jnp.float32)
        right = right_ref[:, lanes].astype(jnp.float32)
        out_ref[block] = (left * right).T.astype(jnp.bfloat16)

    wide = [(left_any, left_ref), (right_any, right_ref)]
    run_streams(count, group, width, [], wide, [], [(out_ref, out_any)], sems, work)


def gate(left, right, count):
    rows, columns = left.shape
    width = columns // count
    if width % 128 != 0:
        product = (left.astype(jnp.float32) * right.astype(jnp.float32)).astype(jnp.bfloat16)
        return product.reshape(rows, count, width).transpose(1, 2, 0)
    group = math.gcd(count, 2)
    out = jax.ShapeDtypeStruct((count, width, rows), jnp.bfloat16)
    wide = pltpu.VMEM((rows, columns), jnp.bfloat16)
    return pl.pallas_call(
        functools.partial(gate_kernel, group),
        in_specs=[pl.BlockSpec(memory_space=pl.ANY)] * 2,
        out_specs=pl.BlockSpec(memory_space=pl.ANY),
        out_shape=out,
        scratch_shapes=[
            wide,
            wide,
            pltpu.VMEM(out.shape, jnp.bfloat16),
            pltpu.SemaphoreType.DMA((3 * count // group,)),
        ],
        compiler_params=params(),
        cost_estimate=estimate(rows * columns, rows * columns * 6),
    )(left, right)


def ungate_kernel(group, factors, *refs):
    back_any, factor_anys = refs[0], refs[1 : factors + 1]
    out_anys = refs[factors + 1 : 2 * factors + 1]
    back_ref, *rest = refs[2 * factors + 1 :]
    factor_refs, out_refs, sems = rest[:factors], rest[factors:-1], rest[-1]
    count, width, _ = back_ref.shape

    def work(block, lanes):
        back = back_ref[block].astype(jnp.float32).T
        for factor_ref, out_ref in zip(factor_refs, out_refs):
            factor = factor_ref[:, lanes].astype(jnp.float32)
            out_ref[:, lanes] = (back * factor).astype(jnp.bfloat16)

    shared = [(back_any, back_ref)]
    wide_in = list(zip(factor_anys, factor_refs))
    wide_out = list(zip(out_refs, out_anys))
    run_streams(count, group, width, shared, wide_in, wide_out, [], sems, work)


def ungate(back, factors):
    count, width, rows = back.shape
    columns = count * width
    if width % 128 != 0:
        part = back.transpose(2, 0, 1).reshape(rows, columns).astype(jnp.float32)
        return [(part * factor.astype(jnp.float32)).astype(jnp.bfloat16) for factor in factors]
    group = math.gcd(count, 2)
    anywhere = pl.BlockSpec(memory_space=pl.ANY)
    wide = pltpu.VMEM((rows, columns), jnp.bfloat16)
    copies = (1 + 2 * len(factors)) * count // group
    return pl.pallas_call(
        functools.partial(ungate_kernel, group, len(factors)),
        in_specs=[anywhere] * (1 + len(factors)),
        out_specs=[anywhere] * len(factors),
        out_shape=[jax.ShapeDtypeStruct((rows, columns), jnp.bfloat16)] * len(factors),
        scratch_shapes=[pltpu.VMEM(back.shape, jnp.bfloat16)]
        + [wide] * (2 * len(factors))
        + [pltpu.SemaphoreType.DMA((copies,))],
        compiler_params=params(),
        cost_estimate=estimate(1000, 1000),
    )(back, *factors)


def gather_all(block, count, index, inner):
    def swaps(held, masks):
        received = [held]
        for mask in masks:
            pairs = [(i, i ^ mask) for i in range(count)]
            received.append(lax.ppermute(held, "seq", pairs))
        return jnp.stack(received)

    across = swaps(block, range(inner, count, inner))
    held = swaps(across, range(1, inner))
    bits = count.bit_length() - 1
    inner_bits = inner.bit_length() - 1
    held = held.reshape((2,) * bits + block.shape)
    for axis in range(bits):
        bit = inner_bits - 1 - axis if axis < inner_bits else bits - 1 - (axis - inner_bits)
        held = jnp.where((index >> bit) % 2 == 1, jnp.flip(held, axis), held)
    held = held.reshape((inner, count // inner) + block.shape)
    return jnp.swapaxes(held, 0, 1).reshape((count,) + block.shape), across


def per_device(q_proj, k_proj, v_proj, grad_out, w_first, w_second, decay_rate, skip_gain):
    height, chan_tp = q_proj.shape
    parts = lax.axis_size("seq")
    length = height * parts
    width = chan_tp // parts
    band_total, hidden_count = w_first.shape
    seq_index = lax.axis_index("seq")

    def exchange(values):
        return lax.all_to_all(values, "seq", split_axis=0, concat_axis=0, tiled=True)

    gated_in = exchange(gate(k_proj, v_proj, parts))
    gated_grad = gate(grad_out, q_proj, parts)

    tables = jnp.asarray(transform_tables(length, height))
    twiddle = jnp.asarray(twiddle_table(length, height))
    positional = positional_table(length, band_total // 2)
    sine_input = jnp.dot(
        w_first.T, positional, precision=HIGH, preferred_element_type=jnp.float32
    )
    hidden = jnp.sin(sine_input)
    cosine = jnp.cos(sine_input)
    offset = seq_index * width
    w_mine = lax.dynamic_slice_in_dim(w_second, offset, width, 1)
    decay_mine = lax.dynamic_slice_in_dim(decay_rate, offset, width, 0)[:, None]
    skip_mine = lax.dynamic_slice_in_dim(skip_gain, offset, width, 0)[:, None]

    spectrum_shape = jax.ShapeDtypeStruct((parts, width, 2 * height), jnp.float32)
    work = pltpu.VMEM(spectrum_shape.shape, jnp.float32)
    split = pltpu.VMEM((2, 6 * height, 2 * height), jnp.bfloat16)
    anywhere = pl.BlockSpec(memory_space=pl.ANY)
    in_vmem = pl.BlockSpec(memory_space=pltpu.VMEM)
    product_flops = 2 * 3 * parts * 4 * height * height * width

    long_filter, filter_spectrum = pl.pallas_call(
        filter_kernel,
        in_specs=[in_vmem] * 5,
        out_specs=[in_vmem, in_vmem],
        out_shape=[jax.ShapeDtypeStruct((width, length), jnp.float32), spectrum_shape],
        scratch_shapes=[work, split],
        compiler_params=params(),
        cost_estimate=estimate(1000, 1000),
    )(w_mine.T, hidden, decay_mine, tables, twiddle)

    gated_grad, long_filter, filter_spectrum, w_mine, skip_mine, positional = (
        lax.optimization_barrier(
            (gated_grad, long_filter, filter_spectrum, w_mine, skip_mine, positional)
        )
    )
    gated_grad = exchange(gated_grad)
    sems = pltpu.SemaphoreType.DMA((2,))
    block_shape = jax.ShapeDtypeStruct(gated_in.shape, jnp.bfloat16)

    convolved, in_spectrum = pl.pallas_call(
        conv_kernel,
        in_specs=[in_vmem, anywhere, in_vmem, in_vmem, in_vmem],
        out_specs=[in_vmem, anywhere],
        out_shape=[block_shape, spectrum_shape],
        scratch_shapes=[work, work, work, split, sems],
        compiler_params=params(),
        cost_estimate=estimate(2 * product_flops, length * width * 20),
    )(gated_in, filter_spectrum, tables, twiddle, skip_mine)
    conv_back = exchange(convolved)

    pieces = width // hidden_count
    packs = width % hidden_count == 0 and 2 * band_total % (16 * pieces) == 0
    first_count = 2 * band_total // pieces if packs else 0
    grad_gated, small, first_pair = pl.pallas_call(
        grad_kernel,
        in_specs=[in_vmem, in_vmem, anywhere, anywhere, anywhere] + [in_vmem] * 8,
        out_specs=[in_vmem, in_vmem, in_vmem],
        out_shape=[
            block_shape,
            jax.ShapeDtypeStruct((hidden_count + 16 + first_count, width), jnp.bfloat16),
            jax.ShapeDtypeStruct((2 * band_total, hidden_count), jnp.bfloat16),
        ],
        scratch_shapes=[
            work,
            work,
            work,
            pltpu.VMEM((width, length), jnp.float32),
            pltpu.VMEM((2, width, height), jnp.float32),
            split,
            pltpu.SemaphoreType.DMA((3,)),
        ],
        compiler_params=params(),
        cost_estimate=estimate(3 * product_flops, length * width * 20),
    )(
        gated_in,
        gated_grad,
        in_spectrum,
        filter_spectrum,
        long_filter,
        tables,
        twiddle,
        skip_mine,
        decay_mine,
        hidden,
        w_mine,
        cosine,
        positional,
    )
    packed = small
    if not packs:
        packed = jnp.concatenate([small, first_pair.reshape(-1, width)], axis=0)
    gathered, across = gather_all(packed, parts, seq_index, math.gcd(parts, 4))
    grad_gated, _ = lax.optimization_barrier((grad_gated, across))
    grad_back = exchange(grad_gated)
    second = gathered[:, :hidden_count].astype(jnp.float32)
    grad_second = second.transpose(1, 0, 2).reshape(hidden_count, chan_tp)
    tail = gathered[:, hidden_count : hidden_count + 4].astype(jnp.float32)
    grad_decay = (tail[:, 0] + tail[:, 1]).reshape(chan_tp)
    grad_skip = (tail[:, 2] + tail[:, 3]).reshape(chan_tp)
    first_rows = gathered[:, hidden_count + 16 :].astype(jnp.float32).sum(axis=0)
    if packs:
        first_rows = first_rows.reshape(first_count, pieces, hidden_count).transpose(1, 0, 2)
    grad_first = first_rows.reshape(2, band_total, hidden_count).sum(axis=0)
    if lax.axis_size("tp") == 2:
        grad_first = grad_first + lax.ppermute(grad_first, "tp", [(0, 1), (1, 0)])
    else:
        grad_first = lax.psum(grad_first, "tp")
    (grad_q,) = ungate(conv_back, (grad_out,))
    grad_k, grad_v = ungate(grad_back, (v_proj, k_proj))
    return (grad_q, grad_k, grad_v, grad_first, grad_second, grad_decay, grad_skip)


def solution(mesh):
    return jax.shard_map(
        per_device,
        mesh=mesh,
        in_specs=(
            P("seq", "tp"),
            P("seq", "tp"),
            P("seq", "tp"),
            P("seq", "tp"),
            P(),
            P(None, "tp"),
            P("tp"),
            P("tp"),
        ),
        out_specs=(
            P("seq", "tp"),
            P("seq", "tp"),
            P("seq", "tp"),
            P(),
            P(None, "tp"),
            P("tp"),
            P("tp"),
        ),
        check_vma=False,
    )
```

```python
import functools
import math

import jax
import jax.numpy as jnp
import ml_dtypes
import numpy as np
from jax import lax
from jax.experimental import pallas as pl
from jax.experimental.pallas import tpu as pltpu
from jax.sharding import PartitionSpec as P

HIGH = lax.Precision.HIGHEST
MIB = 1024 * 1024


def positional_table(length, band_count):
    positions = jnp.arange(length, dtype=jnp.int32)
    band_index = jnp.arange(band_count, dtype=jnp.int32)
    frequency = 3 * (band_index + 1) * (band_index + 1) + band_index
    phase_index = frequency[:, None] * positions[None, :] % length
    angles = phase_index.astype(jnp.float32) * (2.0 * math.pi / length)
    return jnp.concatenate([jnp.sin(angles), jnp.cos(angles)], axis=0)


@functools.lru_cache(maxsize=None)
def transform_tables(length, height):
    j = np.arange(height)
    angles = (j[:, None] * j[None, :] % height) * (2.0 * np.pi / height)
    cosine, sine = np.cos(angles), np.sin(angles)
    forward = np.concatenate(
        [np.concatenate([cosine, -sine], axis=1), np.concatenate([sine, cosine], axis=1)], axis=0
    )
    return np.stack([forward, forward.T / length]).astype(np.float32)


@functools.lru_cache(maxsize=None)
def twiddle_table(length, height):
    parts = length // height
    r = np.arange(parts)[:, None]
    j = np.arange(height)[None, :]
    angles = (j * (4 * r + 1) % (4 * length)) * (2.0 * np.pi / (4 * length))
    return np.concatenate([np.cos(angles), -np.sin(angles)], axis=1).astype(np.float32)


def turn(value, cosine, sine):
    real, imag = value
    return (real * cosine - imag * sine, real * sine + imag * cosine)


def small_fft(values, sign):
    count = len(values)
    if count == 1:
        return values
    even = small_fft(values[0::2], sign)
    odd = small_fft(values[1::2], sign)
    first, second = [], []
    for k in range(count // 2):
        real, imag = odd[k]
        if k == 0:
            pass
        elif 4 * k == count:
            real, imag = (-imag, real) if sign > 0 else (imag, -real)
        elif 8 * k == count:
            half = math.sqrt(0.5)
            if sign > 0:
                real, imag = (real - imag) * half, (real + imag) * half
            else:
                real, imag = (real + imag) * half, (imag - real) * half
        elif 8 * k == 3 * count:
            half = math.sqrt(0.5)
            if sign > 0:
                real, imag = (real + imag) * -half, (real - imag) * half
            else:
                real, imag = (imag - real) * half, (real + imag) * -half
        else:
            angle = sign * 2.0 * math.pi * k / count
            real, imag = turn((real, imag), math.cos(angle), math.sin(angle))
        base_real, base_imag = even[k]
        first.append((base_real + real, base_imag + imag))
        second.append((base_real - real, base_imag - imag))
    return first + second


def parts_forward(values):
    count = len(values)
    turned = []
    for p, value in enumerate(values):
        angle = 2.0 * math.pi * p / (4 * count)
        turned.append((value * math.cos(angle), value * -math.sin(angle)))
    return small_fft(turned, -1)


def parts_inverse(values):
    count = len(values)
    result = []
    for p, (real, imag) in enumerate(small_fft(values, 1)):
        angle = 2.0 * math.pi * p / (4 * count)
        result.append(real * math.cos(angle) - imag * math.sin(angle))
    return result


def split_bf16(value):
    high = value.astype(jnp.bfloat16)
    return high, (value - high.astype(jnp.float32)).astype(jnp.bfloat16)


def split_table(table_ref, split):
    size = table_ref.shape[1]
    for direction in range(2):
        high, low = split_bf16(table_ref[direction])
        split[direction, :size] = high
        split[direction, size : 2 * size] = high
        split[direction, 2 * size :] = low


def transform(value, split, direction):
    high, low = split_bf16(value)
    return jnp.dot(
        jnp.concatenate([high, low, high], axis=1),
        split[direction],
        preferred_element_type=jnp.float32,
    )


def spectrum_product(left, right, conjugate):
    height = left.shape[1] // 2
    left_real, left_imag = left[:, :height], left[:, height:]
    right_real, right_imag = right[:, :height], right[:, height:]
    if conjugate:
        real = left_real * right_real + left_imag * right_imag
        imag = left_real * right_imag - left_imag * right_real
    else:
        real = left_real * right_real - left_imag * right_imag
        imag = left_real * right_imag + left_imag * right_real
    return jnp.concatenate([real, imag], axis=1)


def first_chunk(load, work, twiddle_ref, index):
    parts, height = work.shape[0], work.shape[2] // 2
    row = pl.multiple_of(index * 16, 16)
    values = [load(p, row) for p in range(parts)]
    for half in (0, 8):
        rows = pl.ds(row + half, 8)
        turned = parts_forward([value[half : half + 8] for value in values])
        for r, value in enumerate(turned):
            cosine = twiddle_ref[r : r + 1, :height]
            sine = twiddle_ref[r : r + 1, height:]
            work[r, rows, :height], work[r, rows, height:] = turn(value, cosine, sine)


def last_chunk(store, work, twiddle_ref, index):
    parts, height = work.shape[0], work.shape[2] // 2
    row = pl.multiple_of(index * 16, 16)
    halves = []
    for half in (0, 8):
        rows = pl.ds(row + half, 8)
        values = []
        for r in range(parts):
            cosine = twiddle_ref[r : r + 1, :height]
            sine = twiddle_ref[r : r + 1, height:]
            value = (work[r, rows, :height], work[r, rows, height:])
            values.append(turn(value, cosine, -sine))
        halves.append(parts_inverse(values))
    for p in range(parts):
        store(p, row, jnp.concatenate([halves[0][p], halves[1][p]], axis=0))


GROUP = 4


def run_chunks(width, chunk, parts=0, block=None):
    chunks = width // 16
    per = math.gcd(chunks, GROUP)
    paired = parts * per == GROUP * chunks

    def one(index, carry):
        if paired:
            block(index * GROUP)
        for b in range(per):
            chunk(index * per + b)
        return carry

    lax.fori_loop(0, chunks // per, one, 0)
    if not paired and parts > 0:
        run_blocks(parts, block)


def run_blocks(parts, block):
    def one(index, carry):
        block(index * GROUP)
        return carry

    lax.fori_loop(0, parts // GROUP, one, 0)


def group_of(r):
    return pl.ds(pl.multiple_of(r, GROUP), GROUP)


def read_group(ref, r):
    _, width, columns = ref.shape
    return ref[group_of(r)].reshape(GROUP * width, columns)


def write_group(ref, r, value):
    ref[group_of(r)] = value.reshape((GROUP,) + ref.shape[1:])


def envelope_at(decay, start, length, height):
    position = (start + lax.broadcasted_iota(jnp.int32, (1, height), 1)).astype(jnp.float32)
    fraction = position * (1.0 / length)
    return jnp.exp(-decay * fraction), fraction


def columns_of(p, height):
    return slice(p * height, (p + 1) * height)


def filter_kernel(
    w_t_ref, hidden_ref, decay_ref, table_ref, twiddle_ref, filter_ref, spectrum_ref, work, split
):
    parts, width, height = work.shape[0], work.shape[1], work.shape[2] // 2
    length = filter_ref.shape[1]
    scale = length**-0.5
    split_table(table_ref, split)
    filter_ref[...] = jnp.dot(
        w_t_ref[...], hidden_ref[...], precision=HIGH, preferred_element_type=jnp.float32
    )

    def load(p, row):
        rows, columns = pl.ds(row, 16), columns_of(p, height)
        envelope, _ = envelope_at(decay_ref[rows, :], p * height, length, height)
        value = filter_ref[rows, columns] * envelope * scale
        filter_ref[rows, columns] = value
        return value

    def block(r):
        write_group(spectrum_ref, r, transform(read_group(work, r), split, 0))

    run_chunks(width, lambda i: first_chunk(load, work, twiddle_ref, i))
    run_blocks(parts, block)


def load_from(ref):
    def load(p, row):
        return ref[p, pl.ds(row, 16), :].astype(jnp.float32)

    return load


def store_to(ref, skip_ref, load):
    def store(p, row, value):
        value = value + skip_ref[pl.ds(row, 16), :] * load(p, row)
        ref[p, pl.ds(row, 16), :] = value.astype(jnp.bfloat16)

    return store


def conv_kernel(
    x_ref, h_any, table_ref, twiddle_ref, skip_ref, y_ref, x_any, work, spectra, h, split, sems
):
    parts, width = work.shape[0], work.shape[1]
    copy_in = pltpu.make_async_copy(h_any, h, sems.at[0])
    copy_in.start()
    split_table(table_ref, split)
    load = load_from(x_ref)

    def block(r):
        spectrum = transform(read_group(work, r), split, 0)
        write_group(spectra, r, spectrum)
        product = spectrum_product(read_group(h, r), spectrum, False)
        write_group(work, r, transform(product, split, 1))

    run_chunks(width, lambda i: first_chunk(load, work, twiddle_ref, i))
    copy_in.wait()
    run_blocks(parts, block)
    copy_out = pltpu.make_async_copy(spectra, x_any, sems.at[1])
    copy_out.start()
    store = store_to(y_ref, skip_ref, load)
    run_chunks(width, lambda i: last_chunk(store, work, twiddle_ref, i))
    copy_out.wait()


def grad_kernel(
    x_ref,
    g_ref,
    x_any,
    h_any,
    filter_any,
    table_ref,
    twiddle_ref,
    skip_ref,
    decay_ref,
    hidden_ref,
    w_ref,
    cosine_ref,
    positional_ref,
    z_ref,
    small_ref,
    first_ref,
    work,
    cross,
    h,
    raw,
    sums,
    split,
    sems,
):
    parts, height = work.shape[0], work.shape[2] // 2
    width, length = raw.shape
    hidden_count = hidden_ref.shape[0]
    scale = length**-0.5
    copies = [
        pltpu.make_async_copy(source, target, sems.at[at])
        for at, (source, target) in enumerate(((x_any, cross), (h_any, h), (filter_any, raw)))
    ]
    for copy in copies:
        copy.start()
    split_table(table_ref, split)
    load = load_from(g_ref)

    def block(r):
        spectrum = transform(read_group(work, r), split, 0)
        product = spectrum_product(read_group(h, r), spectrum, True)
        write_group(work, r, transform(product, split, 1))
        product = spectrum_product(read_group(cross, r), spectrum, True)
        write_group(cross, r, transform(product, split, 1))

    def store(p, row, value):
        rows, columns = pl.ds(row, 16), columns_of(p, height)
        envelope, fraction = envelope_at(decay_ref[rows, :], p * height, length, height)
        decay_part = value * raw[rows, columns] * fraction
        skip_part = load_from(x_ref)(p, row) * load(p, row)
        raw[rows, columns] = value * envelope * scale
        if p > 0:
            decay_part = decay_part + sums[0, rows, :]
            skip_part = skip_part + sums[1, rows, :]
        sums[0, rows, :] = decay_part
        sums[1, rows, :] = skip_part

    run_chunks(width, lambda i: first_chunk(load, work, twiddle_ref, i))
    for copy in copies:
        copy.wait()
    run_blocks(parts, block)
    store_z = store_to(z_ref, skip_ref, load)
    run_chunks(width, lambda i: last_chunk(store_z, work, twiddle_ref, i))
    run_chunks(width, lambda i: last_chunk(store, cross, twiddle_ref, i))

    def dot_pairs(left, right, along):
        def dot(one, two):
            return lax.dot_general(
                one, two, (((1,), (along,)), ((), ())), preferred_element_type=jnp.float32
            )

        return dot(left[0], right[0]) + (dot(left[0], right[1]) + dot(left[1], right[0]))

    second = jnp.zeros((hidden_count, width), jnp.float32)
    band_total = positional_ref.shape[0]
    first = jnp.zeros((band_total, hidden_count), jnp.float32)
    w_pair = split_bf16(w_ref[...])
    chunk = min(length, 512)
    for at in range(0, length, chunk):
        columns = slice(at, at + chunk)
        raw_pair = split_bf16(raw[:, columns])
        second += dot_pairs(split_bf16(hidden_ref[:, columns]), raw_pair, 1)
        hidden_part = dot_pairs(w_pair, raw_pair, 0) * cosine_ref[:, columns]
        first += dot_pairs(split_bf16(positional_ref[:, columns]), split_bf16(hidden_part), 1)

    first_ref[:band_total, :], first_ref[band_total:, :] = split_bf16(first * scale)
    small_ref[:hidden_count, :] = (second * scale).astype(jnp.bfloat16)
    place = lax.broadcasted_iota(jnp.int32, (16, width), 0)
    tail = jnp.zeros((16, width), jnp.float32)
    decay_pair = split_bf16(jnp.sum(sums[0].T, axis=0, keepdims=True) * -scale)
    skip_pair = split_bf16(jnp.sum(sums[1].T, axis=0, keepdims=True) * scale)
    for at, row in enumerate(decay_pair + skip_pair):
        tail = jnp.where(place == at, row.astype(jnp.float32), tail)
    small_ref[hidden_count:, :] = tail.astype(jnp.bfloat16)


def params(limit=63):
    return pltpu.CompilerParams(vmem_limit_bytes=limit * MIB)


def estimate(flops, nbytes):
    return pl.CostEstimate(flops=flops, bytes_accessed=nbytes, transcendentals=0)


def chunk_copies(pairs, sems, first):
    return [
        [
            pltpu.make_async_copy(source, target, sems.at[first + at * len(chunk) + which])
            for which, (source, target) in enumerate(chunk)
        ]
        for at, chunk in enumerate(pairs)
    ]


def run_streams(blocks, group, width, shared, wide_in, wide_out, shared_out, sems, work):
    def part(refs, at):
        return [ref.at[pl.ds(at * group, group)] for ref in refs]

    def lanes(refs, at):
        return [ref.at[:, pl.ds(at * group * width, group * width)] for ref in refs]

    chunks = range(blocks // group)
    incoming, outgoing = [], []
    for at in chunks:
        pairs = [tuple(part(pair, at)) for pair in shared]
        incoming.append(pairs + [tuple(lanes(pair, at)) for pair in wide_in])
        pairs = [tuple(part(pair, at)) for pair in shared_out]
        outgoing.append(pairs + [tuple(lanes(pair, at)) for pair in wide_out])
    arrivals = chunk_copies(incoming, sems, 0)
    departures = chunk_copies(outgoing, sems, len(arrivals) * len(arrivals[0]))
    for chunk in arrivals:
        for copy in chunk:
            copy.start()
    for at in chunks:
        for copy in arrivals[at]:
            copy.wait()
        for block in range(at * group, (at + 1) * group):
            work(block, slice(block * width, (block + 1) * width))
        for copy in departures[at]:
            copy.start()
    for chunk in departures:
        for copy in chunk:
            copy.wait()


def gate_kernel(group, left_any, right_any, out_any, left_ref, right_ref, out_ref, sems):
    count, width, _ = out_ref.shape

    def work(block, lanes):
        left = left_ref[:, lanes].astype(jnp.float32)
        right = right_ref[:, lanes].astype(jnp.float32)
        out_ref[block] = (left * right).T.astype(jnp.bfloat16)

    wide = [(left_any, left_ref), (right_any, right_ref)]
    run_streams(count, group, width, [], wide, [], [(out_ref, out_any)], sems, work)


def gate(left, right, count):
    rows, columns = left.shape
    width = columns // count
    if width % 128 != 0:
        product = (left.astype(jnp.float32) * right.astype(jnp.float32)).astype(jnp.bfloat16)
        return product.reshape(rows, count, width).transpose(1, 2, 0)
    group = math.gcd(count, 2)
    out = jax.ShapeDtypeStruct((count, width, rows), jnp.bfloat16)
    wide = pltpu.VMEM((rows, columns), jnp.bfloat16)
    return pl.pallas_call(
        functools.partial(gate_kernel, group),
        in_specs=[pl.BlockSpec(memory_space=pl.ANY)] * 2,
        out_specs=pl.BlockSpec(memory_space=pl.ANY),
        out_shape=out,
        scratch_shapes=[
            wide,
            wide,
            pltpu.VMEM(out.shape, jnp.bfloat16),
            pltpu.SemaphoreType.DMA((3 * count // group,)),
        ],
        compiler_params=params(),
        cost_estimate=estimate(rows * columns, rows * columns * 6),
    )(left, right)


def ungate_kernel(group, factors, *refs):
    back_any, factor_anys = refs[0], refs[1 : factors + 1]
    out_anys = refs[factors + 1 : 2 * factors + 1]
    back_ref, *rest = refs[2 * factors + 1 :]
    factor_refs, out_refs, sems = rest[:factors], rest[factors:-1], rest[-1]
    count, width, _ = back_ref.shape

    def work(block, lanes):
        back = back_ref[block].astype(jnp.float32).T
        for factor_ref, out_ref in zip(factor_refs, out_refs):
            factor = factor_ref[:, lanes].astype(jnp.float32)
            out_ref[:, lanes] = (back * factor).astype(jnp.bfloat16)

    shared = [(back_any, back_ref)]
    wide_in = list(zip(factor_anys, factor_refs))
    wide_out = list(zip(out_refs, out_anys))
    run_streams(count, group, width, shared, wide_in, wide_out, [], sems, work)


def ungate(back, factors):
    count, width, rows = back.shape
    columns = count * width
    if width % 128 != 0:
        part = back.transpose(2, 0, 1).reshape(rows, columns).astype(jnp.float32)
        return [(part * factor.astype(jnp.float32)).astype(jnp.bfloat16) for factor in factors]
    group = math.gcd(count, 2)
    anywhere = pl.BlockSpec(memory_space=pl.ANY)
    wide = pltpu.VMEM((rows, columns), jnp.bfloat16)
    copies = (1 + 2 * len(factors)) * count // group
    return pl.pallas_call(
        functools.partial(ungate_kernel, group, len(factors)),
        in_specs=[anywhere] * (1 + len(factors)),
        out_specs=[anywhere] * len(factors),
        out_shape=[jax.ShapeDtypeStruct((rows, columns), jnp.bfloat16)] * len(factors),
        scratch_shapes=[pltpu.VMEM(back.shape, jnp.bfloat16)]
        + [wide] * (2 * len(factors))
        + [pltpu.SemaphoreType.DMA((copies,))],
        compiler_params=params(),
        cost_estimate=estimate(rows * columns, rows * columns * (2 + 4 * len(factors))),
    )(back, *factors)


def gather_all(block, count, index, inner):
    def swaps(held, masks):
        received = [held]
        for mask in masks:
            pairs = [(i, i ^ mask) for i in range(count)]
            received.append(lax.ppermute(held, "seq", pairs))
        return jnp.stack(received)

    across = swaps(block, range(inner, count, inner))
    held = swaps(across, range(1, inner))
    bits = count.bit_length() - 1
    inner_bits = inner.bit_length() - 1
    held = held.reshape((2,) * bits + block.shape)
    for axis in range(bits):
        bit = inner_bits - 1 - axis if axis < inner_bits else bits - 1 - (axis - inner_bits)
        held = jnp.where((index >> bit) % 2 == 1, jnp.flip(held, axis), held)
    held = held.reshape((inner, count // inner) + block.shape)
    return jnp.swapaxes(held, 0, 1).reshape((count,) + block.shape), across


def per_device(q_proj, k_proj, v_proj, grad_out, w_first, w_second, decay_rate, skip_gain):
    height, chan_tp = q_proj.shape
    parts = lax.axis_size("seq")
    length = height * parts
    width = chan_tp // parts
    band_total, hidden_count = w_first.shape
    seq_index = lax.axis_index("seq")

    def exchange(values):
        return lax.all_to_all(values, "seq", split_axis=0, concat_axis=0, tiled=True)

    gated_in = exchange(gate(k_proj, v_proj, parts))
    gated_grad = gate(grad_out, q_proj, parts)

    tables = jnp.asarray(transform_tables(length, height))
    twiddle = jnp.asarray(twiddle_table(length, height))
    positional = positional_table(length, band_total // 2)
    sine_input = jnp.dot(
        w_first.T, positional, precision=HIGH, preferred_element_type=jnp.float32
    )
    hidden = jnp.sin(sine_input)
    cosine = jnp.cos(sine_input)
    offset = seq_index * width
    w_mine = lax.dynamic_slice_in_dim(w_second, offset, width, 1)
    decay_mine = lax.dynamic_slice_in_dim(decay_rate, offset, width, 0)[:, None]
    skip_mine = lax.dynamic_slice_in_dim(skip_gain, offset, width, 0)[:, None]

    spectrum_shape = jax.ShapeDtypeStruct((parts, width, 2 * height), jnp.float32)
    work = pltpu.VMEM(spectrum_shape.shape, jnp.float32)
    split = pltpu.VMEM((2, 6 * height, 2 * height), jnp.bfloat16)
    anywhere = pl.BlockSpec(memory_space=pl.ANY)
    in_vmem = pl.BlockSpec(memory_space=pltpu.VMEM)
    product_flops = 2 * 3 * parts * 4 * height * height * width

    long_filter, filter_spectrum = pl.pallas_call(
        filter_kernel,
        in_specs=[in_vmem] * 5,
        out_specs=[in_vmem, in_vmem],
        out_shape=[jax.ShapeDtypeStruct((width, length), jnp.float32), spectrum_shape],
        scratch_shapes=[work, split],
        compiler_params=params(),
        cost_estimate=estimate(1000, 1000),
    )(w_mine.T, hidden, decay_mine, tables, twiddle)

    gated_grad, long_filter, filter_spectrum, w_mine, skip_mine, positional = (
        lax.optimization_barrier(
            (gated_grad, long_filter, filter_spectrum, w_mine, skip_mine, positional)
        )
    )
    gated_grad = exchange(gated_grad)
    sems = pltpu.SemaphoreType.DMA((2,))
    block_shape = jax.ShapeDtypeStruct(gated_in.shape, jnp.bfloat16)

    convolved, in_spectrum = pl.pallas_call(
        conv_kernel,
        in_specs=[in_vmem, anywhere, in_vmem, in_vmem, in_vmem],
        out_specs=[in_vmem, anywhere],
        out_shape=[block_shape, spectrum_shape],
        scratch_shapes=[work, work, work, split, sems],
        compiler_params=params(),
        cost_estimate=estimate(2 * product_flops, length * width * 20),
    )(gated_in, filter_spectrum, tables, twiddle, skip_mine)
    conv_back = exchange(convolved)

    grad_gated, small, first_pair = pl.pallas_call(
        grad_kernel,
        in_specs=[in_vmem, in_vmem, anywhere, anywhere, anywhere] + [in_vmem] * 8,
        out_specs=[in_vmem, in_vmem, in_vmem],
        out_shape=[
            block_shape,
            jax.ShapeDtypeStruct((hidden_count + 16, width), jnp.bfloat16),
            jax.ShapeDtypeStruct((2 * band_total, hidden_count), jnp.bfloat16),
        ],
        scratch_shapes=[
            work,
            work,
            work,
            pltpu.VMEM((width, length), jnp.float32),
            pltpu.VMEM((2, width, height), jnp.float32),
            split,
            pltpu.SemaphoreType.DMA((3,)),
        ],
        compiler_params=params(),
        cost_estimate=estimate(3 * product_flops, length * width * 20),
    )(
        gated_in,
        gated_grad,
        in_spectrum,
        filter_spectrum,
        long_filter,
        tables,
        twiddle,
        skip_mine,
        decay_mine,
        hidden,
        w_mine,
        cosine,
        positional,
    )
    packed = jnp.concatenate([small, first_pair.reshape(-1, width)], axis=0)
    gathered, across = gather_all(packed, parts, seq_index, math.gcd(parts, 4))
    grad_gated, _ = lax.optimization_barrier((grad_gated, across))
    grad_back = exchange(grad_gated)
    second = gathered[:, :hidden_count].astype(jnp.float32)
    grad_second = second.transpose(1, 0, 2).reshape(hidden_count, chan_tp)
    tail = gathered[:, hidden_count : hidden_count + 4].astype(jnp.float32)
    grad_decay = (tail[:, 0] + tail[:, 1]).reshape(chan_tp)
    grad_skip = (tail[:, 2] + tail[:, 3]).reshape(chan_tp)
    first_rows = gathered[:, hidden_count + 16 :].astype(jnp.float32).sum(axis=0)
    grad_first = first_rows.reshape(2, band_total, hidden_count).sum(axis=0)
    if lax.axis_size("tp") == 2:
        grad_first = grad_first + lax.ppermute(grad_first, "tp", [(0, 1), (1, 0)])
    else:
        grad_first = lax.psum(grad_first, "tp")
    (grad_q,) = ungate(conv_back, (grad_out,))
    grad_k, grad_v = ungate(grad_back, (v_proj, k_proj))
    return (grad_q, grad_k, grad_v, grad_first, grad_second, grad_decay, grad_skip)


def solution(mesh):
    return jax.shard_map(
        per_device,
        mesh=mesh,
        in_specs=(
            P("seq", "tp"),
            P("seq", "tp"),
            P("seq", "tp"),
            P("seq", "tp"),
            P(),
            P(None, "tp"),
            P("tp"),
            P("tp"),
        ),
        out_specs=(
            P("seq", "tp"),
            P("seq", "tp"),
            P("seq", "tp"),
            P(),
            P(None, "tp"),
            P("tp"),
            P("tp"),
        ),
        check_vma=False,
    )
```
